256 devices in a mesh: ctx: 32 (over y, z_hi, core), tp: 8 (over x, z_lo).
Axes of the slice: x: 4, y: 4, z: 8 (z_hi: 4, z_lo: 2; z = z_hi * 2 + z_lo), core: 2. Of those that a mesh axis runs over, the one named last changes fastest.
Arguments:
- tokens: bfloat16 [16384, 2560], P('ctx'), may hold values from -6 to 6
- inner_weight: bfloat16 [2560, 5120], P(None, 'tp'), may hold values from -0.125 to 0.125
- shared_weight: bfloat16 [2560, 256], replicated, may hold values from -0.125 to 0.125
- step_weight: bfloat16 [2560, 80], P(None, 'tp'), may hold values from -0.125 to 0.125
- conv_inner: float32 [4, 5120], P(None, 'tp'), may hold values from -3 to 3
- conv_shared: float32 [4, 256], replicated, may hold values from -0.375 to 0.375
- step_bias: float32 [80], P('tp'), may hold values from -2 to 1
- decay_rate: float32 [80], P('tp'), may hold values from 0 to 0.06, as said below
- skip_gain: float32 [80], P('tp'), may hold values from 0.5 to 1.5
- cotangent: bfloat16 [16384, 5120], P('ctx', 'tp'), may hold values from -6 to 6
Outputs:
- mixed: bfloat16 [16384, 5120], P('ctx', 'tp')
- grad_tokens: bfloat16 [16384, 2560], P('ctx', 'tp')
- grad_inner_weight: float32 [2560, 5120], P('ctx', 'tp')
- grad_shared_weight: float32 [2560, 256], P('ctx', 'tp')
- grad_step_weight: float32 [2560, 80], P('ctx', 'tp')
The draws below stay inside these ranges and needn't reach their ends.
Inputs may be any that keep to these rules, and one draw needn't show every extreme that they name: `decay_rate`: decay rates are positive.
All inputs are finite; a program needn't handle non-finite values.
Results may differ from the reference program's by a relative error of at most 0.0031.
Values sent between devices are 32-bit elements; how exact they have to be, the bound alone decides.
No kernel may reach another device: no remote copies, remote signals or barrier semaphores. Data moves between devices by JAX's collectives and lax.ppermute only.
A program may use at most 192 MiB of HBM per device.

```python
import jax
import jax.numpy as jnp
from jax import lax

D = 2560
HEADS = 80
P_SIZE = 64
N = 128
K = 4
GROUP = 256
TOKENS = 16384


def draw_decay_rate(key, part):
    key = jax.random.fold_in(key, 11)
    uniform_draw = jax.random.uniform(key, (HEADS,), jnp.float32)
    lowest = jnp.log(0.5 / TOKENS)
    highest = jnp.log(0.06)
    rate = jnp.exp(lowest + uniform_draw * (highest - lowest))
    return rate.astype(jnp.float32)


def raised(result, stream_key, source, target, blocks, factor):
    owner, partner = [(jnp.arange(result.shape[axis_at]) // (result.shape[axis_at] // blocks)).reshape([-1 if axis == axis_at else 1 for axis in range(result.ndim)]) for axis_at in (source, target)]
    chosen = jax.random.permutation(stream_key, blocks)[partner]
    strong = (owner == chosen) | (owner == (partner + blocks // 2) % blocks)
    return jnp.where(strong, factor * result, result)


def block_scale(own_key, shape, split, least, high):
    level = 1.0
    for dim, blocks in split:
        heights = jax.random.uniform(jax.random.fold_in(jax.random.fold_in(own_key, 6), dim), (blocks,), jnp.float32, least / len(split), high / len(split))
        level = level * jnp.repeat(jnp.exp(heights), shape[dim] // blocks).reshape((-1,) + (1,) * (len(shape) - 1 - dim))
    return level


def centred(stream_key, dims, deviation, limit, cuts=(), dtype=jnp.bfloat16):
    entries = jax.random.normal(stream_key, dims, jnp.float32) * deviation
    if len(cuts) > 0:
        entries = block_scale(stream_key, dims, cuts, -0.22, 0.18) * entries
    return jnp.clip(entries, min=-limit, max=limit).astype(dtype)


def heavy_noise(key, dims, spread, most, split, heavy, dtype=jnp.bfloat16):
    array = spread * jax.random.normal(key, dims, jnp.float32)
    if split:
        array = array * block_scale(key, dims, split, -0.22, 0.18)
    return jnp.clip(raised(array, jax.random.fold_in(key, 3), *heavy), -most, most).astype(dtype)


def setup_inputs(seed: int = 0) -> dict:
    key_of = jax.random.split(jax.random.key(seed), 11)
    tokens = heavy_noise(key_of[0], (TOKENS, D), 1.0, 6.0, ((0, 32),), (0, 1, 32, 2.75))
    inner_weight = centred(key_of[1], (D, HEADS * P_SIZE), D ** -0.5, 0.125, ((1, 8),))
    shared_weight = centred(key_of[2], (D, 2 * N), D ** -0.5, 0.125)
    step_weight = centred(key_of[3], (D, HEADS), D ** -0.5, 0.125, ((1, 8),))
    conv_inner = centred(key_of[4], (K, HEADS * P_SIZE), K ** -0.5, 3.0, ((1, 8),), jnp.float32)
    conv_shared = centred(key_of[5], (K, 2 * N), (2 * N) ** -0.5, 0.375, (), jnp.float32)
    step_bias = jnp.clip(-2.0 + 3.0 * jax.random.uniform(key_of[6], (HEADS,), jnp.float32) ** block_scale(key_of[6], (HEADS,), ((0, 8),), -0.2, 0.2), -2.0, 1.0)
    decay_rate = draw_decay_rate(jax.random.fold_in(key_of[10], 71), 0)
    skip_gain = jnp.clip(0.5 + 1.0 * jax.random.uniform(key_of[8], (HEADS,), jnp.float32) ** block_scale(key_of[8], (HEADS,), ((0, 8),), -0.2, 0.2), 0.5, 1.5)
    cotangent = centred(key_of[9], (TOKENS, HEADS * P_SIZE), 1.0, 6.0, ((0, 32), (1, 8)))
    return {"tokens": tokens, "inner_weight": inner_weight, "shared_weight": shared_weight, "step_weight": step_weight, "conv_inner": conv_inner, "conv_shared": conv_shared, "step_bias": step_bias, "decay_rate": decay_rate, "skip_gain": skip_gain, "cotangent": cotangent}


def group_terms(values, b_vectors, c_vectors, step_size, decay_rate, skip_gain):
    log_decay = -decay_rate[None, :] * step_size
    cum_logs = jnp.cumsum(log_decay, 0)
    length = step_size.shape[0]
    causal = (jnp.arange(length)[:, None] >= jnp.arange(length)[None, :])[:, :, None]
    log_gaps = cum_logs[:, None, :] - cum_logs[None, :, :]
    decays = jnp.where(causal, jnp.exp(jnp.where(causal, log_gaps, 0.0)), 0.0)
    scores = jnp.dot(c_vectors, b_vectors.T, precision=lax.Precision.HIGHEST)
    weights = scores[:, :, None] * decays * step_size[None, :, :]
    inside = jnp.einsum('ijh,jhp->ihp', weights, values, precision=lax.Precision.HIGHEST)
    inside = inside + skip_gain[None, :, None] * values
    tail_weight = jnp.exp(cum_logs[-1][None, :] - cum_logs) * step_size
    written = jnp.einsum('jh,jhp,jn->hpn', tail_weight, values, b_vectors, precision=lax.Precision.HIGHEST)
    return (inside, cum_logs, written)

def reference(tokens, inner_weight, shared_weight, step_weight, conv_inner, conv_shared, step_bias, decay_rate, skip_gain, cotangent):
    inner = HEADS * P_SIZE
    blocks_count = TOKENS // GROUP
    inner_pre = jnp.dot(tokens, inner_weight, preferred_element_type=jnp.float32)
    shared_pre = jnp.dot(tokens, shared_weight, preferred_element_type=jnp.float32)
    step_pre = jnp.dot(tokens, step_weight, preferred_element_type=jnp.float32)
    pre = jnp.concatenate([inner_pre, shared_pre], 1)
    conv_taps = jnp.concatenate([conv_inner, conv_shared], 1).astype(jnp.float32)

    def layer_mix(pre, step_pre):
        padded = jnp.pad(pre, ((K - 1, 0), (0, 0)))
        conv_out = jnp.zeros(pre.shape, jnp.float32)
        for offset in range(K):
            conv_out = conv_out + conv_taps[offset][None, :] * padded[offset:offset + TOKENS]
        active = jax.nn.silu(conv_out)
        values = active[:, :inner].reshape(blocks_count, GROUP, HEADS, P_SIZE)
        b_vectors = active[:, inner:inner + N].reshape(blocks_count, GROUP, N)
        c_vectors = active[:, inner + N:].reshape(blocks_count, GROUP, N)
        step_size = jax.nn.softplus(step_pre + step_bias[None, :]).reshape(blocks_count, GROUP, HEADS)

        def advance(memory, blocks):
            values_b, b_block, c_block, step_block = blocks
            inside, cum_logs, written = group_terms(values_b, b_block, c_block, step_block, decay_rate, skip_gain)
            carried = jnp.einsum('in,hpn->ihp', c_block, memory, precision=lax.Precision.HIGHEST)
            carried = carried * jnp.exp(cum_logs)[:, :, None]
            fresh = jnp.exp(cum_logs[-1])[:, None, None] * memory + written
            return (fresh, inside + carried)
        start_memory = jnp.zeros((HEADS, P_SIZE, N), jnp.float32)
        _, outputs = lax.scan(advance, start_memory, (values, b_vectors, c_vectors, step_size))
        return outputs.reshape(TOKENS, inner)
    mixed_full, pullback = jax.vjp(layer_mix, pre, step_pre)
    grad_pre, grad_step = pullback(cotangent.astype(jnp.float32))
    grad_inner = grad_pre[:, :inner].astype(jnp.bfloat16)
    grad_shared = grad_pre[:, inner:]
    grad_tokens = jnp.dot(grad_inner, inner_weight.T, preferred_element_type=jnp.float32)
    grad_tokens = grad_tokens + jnp.dot(grad_shared, shared_weight.astype(jnp.float32).T, precision=lax.Precision.HIGHEST)
    grad_tokens = grad_tokens + jnp.dot(grad_step, step_weight.astype(jnp.float32).T, precision=lax.Precision.HIGHEST)
    tokens_wide = tokens.astype(jnp.float32)
    grad_inner_weight = jnp.dot(tokens.T, grad_inner, preferred_element_type=jnp.float32)
    grad_shared_weight = jnp.dot(tokens_wide.T, grad_shared, precision=lax.Precision.HIGHEST)
    grad_step_weight = jnp.dot(tokens_wide.T, grad_step, precision=lax.Precision.HIGHEST)
    return (mixed_full.astype(jnp.bfloat16), grad_tokens.astype(jnp.bfloat16), grad_inner_weight, grad_shared_weight, grad_step_weight)
```

```python
import functools

import jax
import jax.numpy as jnp
from jax import lax
from jax.experimental import pallas as pl
from jax.experimental.pallas import tpu as pltpu
from jax.sharding import PartitionSpec as P

P_SIZE = 64
N = 128
K = 4
LANES = 128
SLOT = 16
F32 = jnp.float32
BF16 = jnp.bfloat16
NN = (((1,), (0,)), ((), ()))
NT = (((1,), (1,)), ((), ()))
TN = (((0,), (0,)), ((), ()))
PARAMS = pltpu.CompilerParams(vmem_limit_bytes=48 * 1024 * 1024)


def shifted(block, axis, distance):
    size = lax.axis_size(axis)
    return lax.ppermute(block, axis, [(i, (i + distance) % size) for i in range(size)])


def dot1(a, b, dims):
    return lax.dot_general(a, b, dims, preferred_element_type=F32)


def split(a):
    high = a.astype(BF16)
    return high, (a - high.astype(F32)).astype(BF16)


def dot3(a, b, dims):
    ah, al = a
    bh, bl = b
    return dot1(ah, bh, dims) + (dot1(ah, bl, dims) + dot1(al, bh, dims))


def dot2(a, b, dims):
    return dot1(a[0], b, dims) + dot1(a[1], b, dims)


def sigmoid(z):
    return 1.0 / (1.0 + jnp.exp(-z))


def of_tile(cols, k):
    lane = lax.broadcasted_iota(jnp.int32, (cols.shape[0], LANES), 1)
    left = jnp.broadcast_to(cols[:, 2 * k : 2 * k + 1], lane.shape)
    right = jnp.broadcast_to(cols[:, 2 * k + 1 : 2 * k + 2], lane.shape)
    return jnp.where(lane < P_SIZE, left, right)


def triangle_sum(a, dims):
    length = a.shape[0]
    row = lax.broadcasted_iota(jnp.int32, (length, length), 0)
    col = lax.broadcasted_iota(jnp.int32, (length, length), 1)
    reach = row >= col if dims == NN else row <= col
    ones = jnp.where(reach, 1.0, 0.0).astype(BF16)
    first = a.astype(BF16).astype(F32)
    second = (a - first).astype(BF16).astype(F32)
    third = (a - first - second).astype(BF16).astype(F32)
    packed = first + pltpu.roll(second, SLOT, 1) + pltpu.roll(third, 2 * SLOT, 1)
    sums = dot1(ones, packed.astype(BF16), NN)
    total = sums + pltpu.roll(sums, LANES - SLOT, 1) + pltpu.roll(sums, LANES - 2 * SLOT, 1)
    lane = lax.broadcasted_iota(jnp.int32, total.shape, 1)
    return jnp.where(lane < SLOT, total, 0.0)


def project_kernel(
    tiles, heads,
    edge_ref, tok_ref, rim_ref, wi_ref, ws_ref, wt_ref, ci_ref, cs_ref, par_ref, cot_ref,
    z_ref, sp_ref, dt_ref, cum_ref, cumt_ref, pay_ref,
    lhs, acc_i, acc_s, acc_t,
):
    step = pl.program_id(0)
    length = tok_ref.shape[0]
    head_rows = lhs.shape[0] - length
    inner = wi_ref.shape[1]

    @pl.when(step == 0)
    def _():
        acc_i[...] = jnp.zeros_like(acc_i)
        acc_s[...] = jnp.zeros_like(acc_s)
        acc_t[...] = jnp.zeros_like(acc_t)

    keep = jnp.where(edge_ref[0] == 0, 0.0, 1.0)
    rim = rim_ref[...] * keep
    lhs[0:head_rows, :] = jnp.concatenate([jnp.zeros_like(rim), rim], 0).astype(BF16)
    lhs[head_rows:, :] = tok_ref[...]
    left = lhs[...]
    acc_i[...] += dot1(left, wi_ref[...], NN)
    acc_s[...] += dot1(left, ws_ref[...], NN)
    acc_t[:, 0:heads] += dot1(left, wt_ref[...], NN)

    @pl.when(step == pl.num_programs(0) - 1)
    def _():
        start = head_rows - (K - 1)
        sp = acc_t[head_rows:, :] + par_ref[0:1, :]
        sp_ref[...] = sp
        dt = jnp.maximum(sp, 0.0) + jnp.log1p(jnp.exp(-jnp.abs(sp)))
        dt_ref[...] = dt
        cum = triangle_sum(-par_ref[1:2, :] * dt, NN)
        cum_ref[...] = cum
        cumt_ref[...] = jnp.transpose(cum)[0:SLOT, :]
        last = cum[length - 1 :, :]
        write_weight = dt * jnp.exp(last - cum)
        read_weight = jnp.exp(cum)

        def conv(acc, taps, k):
            lo = k * LANES
            out = taps[0:1, lo : lo + LANES] * acc[start : start + length, lo : lo + LANES]
            for j in range(1, K):
                out += taps[j : j + 1, lo : lo + LANES] * acc[
                    start + j : start + j + length, lo : lo + LANES
                ]
            return out

        zb = conv(acc_s, cs_ref, 0)
        z_ref[:, inner : inner + LANES] = zb
        zc = conv(acc_s, cs_ref, 1)
        z_ref[:, inner + LANES :] = zc
        b2 = split(zb * sigmoid(zb))
        c2 = split(zc * sigmoid(zc))
        groups = N // 8
        pay_ref[:, 8 * tiles :, :] = jnp.zeros((2 * groups, 8, LANES), F32)
        for k in range(tiles):
            lo = k * LANES
            z = conv(acc_i, ci_ref, k)
            z_ref[:, lo : lo + LANES] = z
            x2 = split(z * sigmoid(z) * of_tile(write_weight, k))
            state = dot3(b2, x2, TN)
            g2 = split(cot_ref[:, lo : lo + LANES].astype(F32) * of_tile(read_weight, k))
            grad = dot3(c2, g2, TN)
            pay_ref[0:groups, 8 * k : 8 * k + 8, :] = state.reshape(groups, 8, LANES)
            pay_ref[groups:, 8 * k : 8 * k + 8, :] = grad.reshape(groups, 8, LANES)
            row = of_tile(last, k)
            pay_ref[:, 8 * tiles + k : 8 * tiles + k + 1, :] = jnp.broadcast_to(
                row[None], (2 * groups, 1, LANES)
            )


def ctx_scan_kernel(tiles, edge_ref, in_ref, out_ref):
    count = in_ref.shape[0]
    rows = 8 * tiles
    backward = edge_ref[0] >= count // 2

    def turn(i, held):
        at = jnp.where(backward, count - 1 - i, i)
        out_ref[at] = held
        got = in_ref[at]
        decay = jnp.exp(got[rows:, :])
        wide = jnp.concatenate(
            [jnp.broadcast_to(decay[k : k + 1, :], (8, LANES)) for k in range(tiles)], 0
        )
        return got[0:rows, :] + wide * held

    lax.fori_loop(0, count, turn, jnp.zeros((rows, LANES), F32), unroll=4)


def local_kernel(
    zv_ref, zb_ref, zc_ref, dt_ref, cum_ref, cumt_ref, cot_ref,
    y_ref, u_ref, db_ref, dc_ref,
    scores, grad_scores, dt_wide, cum_wide,
):
    tile = pl.program_id(0)
    length = zv_ref.shape[0]
    half = length // 2
    zb = zb_ref[...]
    zc = zc_ref[...]
    b = zb * sigmoid(zb)
    c = zc * sigmoid(zc)
    bh, bl = split(b)
    ch, cl = split(c)

    @pl.when(tile == 0)
    def _():
        row = lax.broadcasted_iota(jnp.int32, (half, half), 0)
        col = lax.broadcasted_iota(jnp.int32, (half, half), 1)
        for chunk in range(2):
            at = slice(chunk * half, (chunk + 1) * half)
            full = dot3((ch[at], cl[at]), (bh[at], bl[at]), NT)
            scores[chunk] = jnp.where(row >= col, full, 0.0)
        grad_scores[...] = jnp.zeros_like(grad_scores)
        db_ref[...] = jnp.zeros_like(db_ref)
        dc_ref[...] = jnp.zeros_like(dc_ref)

    lane = lax.broadcasted_iota(jnp.int32, (length, LANES), 1)

    def pick(ref):
        cols = ref[...]
        left = jnp.sum(jnp.where(lane == 2 * tile, cols, 0.0), 1, keepdims=True)
        right = jnp.sum(jnp.where(lane == 2 * tile + 1, cols, 0.0), 1, keepdims=True)
        return left, right

    dt_cols = pick(dt_ref)
    cum_cols = pick(cum_ref)
    dt_wide[...] = jnp.where(lane < P_SIZE, dt_cols[0], dt_cols[1])
    cum_wide[...] = jnp.where(lane < P_SIZE, cum_cols[0], cum_cols[1])
    zv = zv_ref[...]
    x = zv * sigmoid(zv) * dt_wide[...]
    g = cot_ref[...]
    xh, xl = split(x)
    gt = jnp.transpose(g.astype(F32)).astype(BF16)

    for chunk in range(2):
        at = slice(chunk * half, (chunk + 1) * half)
        ys = []
        us = []
        for head in range(2):
            of = slice(head * P_SIZE, (head + 1) * P_SIZE)
            row_logs = cumt_ref[pl.ds(2 * tile + head, 1), at]
            gaps = jnp.minimum(cum_cols[head][at] - row_logs, 0.0)
            decays = jnp.exp(gaps)
            weights = scores[chunk] * decays
            wh, wl = split(weights)
            x_pair = jnp.concatenate([xh[at, of], xl[at, of]], 1)
            y_pair = dot1(wh, x_pair, NN) + dot1(wl, x_pair, NN)
            ys.append(y_pair[:, 0:P_SIZE] + y_pair[:, P_SIZE:])
            us.append(dot1(gt[of, at], wh, NN) + dot1(gt[of, at], wl, NN))
            g_pair = jnp.concatenate([g[at, of], g[at, of]], 1)
            grad_scores[chunk] += dot1(g_pair, x_pair, NT) * decays
        y_ref[at, :] = jnp.concatenate(ys, 1)
        u_ref[at, :] = jnp.transpose(jnp.concatenate(us, 0))

    early = slice(0, half)
    late = slice(half, length)
    cum = cum_wide[...]
    middle = cum[half - 1 : half, :]
    down = jnp.exp(middle - cum[early])
    up = jnp.exp(cum[late] - middle)
    xd = split(x[early] * down)
    gd = split(g[late].astype(F32) * up)
    b0 = (bh[early], bl[early])
    c1 = (ch[late], cl[late])
    state = split(dot3(b0, xd, TN))
    grad = split(dot3(c1, gd, TN))
    y_ref[late, :] += up * dot3(c1, state, NN)
    u_ref[early, :] += down * dot3(b0, grad, NN)
    dc_ref[late, :] += dot3(gd, state, NT)
    db_ref[early, :] += dot3(xd, grad, NT)

    @pl.when(tile == pl.num_programs(0) - 1)
    def _():
        row = lax.broadcasted_iota(jnp.int32, (half, half), 0)
        col = lax.broadcasted_iota(jnp.int32, (half, half), 1)
        for chunk in range(2):
            at = slice(chunk * half, (chunk + 1) * half)
            gs = split(jnp.where(row >= col, grad_scores[chunk], 0.0))
            dc_ref[at, :] += dot3(gs, (bh[at], bl[at]), NN)
            db_ref[at, :] += dot3(gs, (ch[at], cl[at]), TN)


def join_kernel(
    tiles,
    z_ref, sp_ref, dt_ref, cum_ref, par_ref, cot_ref, y_ref, u_ref, db_ref, dc_ref,
    pay_ref, arrived_ref,
    mixed_ref, dconv_ref, gstep_ref,
):
    length = z_ref.shape[0]
    inner = tiles * LANES
    groups = N // 8
    dt = dt_ref[...]
    cum = cum_ref[...]
    last = cum[length - 1 :, :]
    read_weight = jnp.exp(cum)
    tail_weight = jnp.exp(last - cum)
    total_decay = jnp.exp(last)
    zb = z_ref[:, inner : inner + LANES]
    zc = z_ref[:, inner + LANES :]
    sb = sigmoid(zb)
    sc = sigmoid(zc)
    b2 = split(zb * sb)
    c2 = split(zc * sc)
    db = db_ref[...]
    dc = dc_ref[...]
    reads = jnp.zeros((length, LANES), F32)
    writes = jnp.zeros((length, LANES), F32)
    ends = jnp.zeros((1, LANES), F32)
    lane = lax.broadcasted_iota(jnp.int32, (LANES, LANES), 1)
    row = lax.broadcasted_iota(jnp.int32, (LANES, LANES), 0)
    for k in range(tiles):
        at = slice(k * LANES, (k + 1) * LANES)
        rows = slice(8 * k, 8 * k + 8)
        gather = jnp.where(lane == 2 * k + row // P_SIZE, 1.0, 0.0).astype(BF16)
        state = arrived_ref[0:groups, rows, :].reshape(N, LANES)
        grad = arrived_ref[groups:, rows, :].reshape(N, LANES)
        state2 = split(state)
        grad2 = split(grad)
        z = z_ref[:, at]
        s = sigmoid(z)
        v = z * s
        g = cot_ref[:, at].astype(F32)
        read_k = of_tile(read_weight, k)
        tail_k = of_tile(tail_weight, k)
        dt_k = of_tile(dt, k)
        skip = of_tile(par_ref[2:3, :], k)
        y = y_ref[:, at] + read_k * dot3(c2, state2, NN)
        u = u_ref[:, at] + tail_k * dot3(b2, grad2, NN)
        mixed_ref[:, at] = (y + skip * v).astype(BF16)
        dv = dt_k * u + skip * g
        dconv_ref[:, at] = dv * (s * (1.0 + z * (1.0 - s)))
        reads += dot2(split(g * y), gather, NN)
        writes += dot2(split(v * u), gather, NN)
        dc += dot3(split(g * read_k), state2, NT)
        db += dot3(split(v * dt_k * tail_k), grad2, NT)
        own = pay_ref[0:groups, rows, :].reshape(N, LANES)
        end = jnp.sum(grad * (own + of_tile(total_decay, k) * state), 0, keepdims=True)
        end = jnp.broadcast_to(end, (8, LANES))
        ends += dot2(split(end), gather, NN)[0:1]
    dconv_ref[:, inner : inner + LANES] = db * (sb * (1.0 + zb * (1.0 - sb)))
    dconv_ref[:, inner + LANES :] = dc * (sc * (1.0 + zc * (1.0 - sc)))
    grad_logs = triangle_sum(reads - dt * writes, TN) + ends
    grad_dt = writes - par_ref[1:2, :] * grad_logs
    gstep_ref[...] = grad_dt * sigmoid(sp_ref[...])


def conv_back_kernel(edge_ref, dconv_ref, rim_ref, ci_ref, cs_ref, gi_ref, gs_ref, gst_ref, wide):
    length = dconv_ref.shape[0]
    inner = ci_ref.shape[1]
    wide[0:length, :] = dconv_ref[...]
    wide[length:, :] = rim_ref[...] * jnp.where(edge_ref[1] == 0, 1.0, 0.0)

    def back(taps, offset, k):
        lo = k * LANES
        at = slice(offset + lo, offset + lo + LANES)
        out = taps[K - 1 : K, lo : lo + LANES] * wide[0:length, at]
        for j in range(1, K):
            out += taps[K - 1 - j : K - j, lo : lo + LANES] * wide[j : j + length, at]
        return out

    for k in range(inner // LANES):
        gi_ref[:, k * LANES : (k + 1) * LANES] = back(ci_ref, 0, k).astype(BF16)
    for k in range(2):
        at = slice(k * LANES, (k + 1) * LANES)
        grad = back(cs_ref, inner, k)
        gs_ref[:, at] = grad
        gst_ref[at, :] = jnp.transpose(grad)


def token_grad_kernel(heads, wi_ref, ws_ref, wt_ref, gi_ref, gs_ref, gstep_ref, out_ref, halves):
    shared = ws_ref.shape[1]

    @pl.when(pl.program_id(0) == 0)
    def _():
        high, low = split(gs_ref[...])
        halves[:, 0:shared] = high
        halves[:, shared : 2 * shared] = low
        high, low = split(gstep_ref[...])
        halves[:, 2 * shared : 2 * shared + LANES] = high
        halves[:, 2 * shared + LANES :] = low

    total = dot1(wi_ref[...], gi_ref[...], NT)
    total += dot1(ws_ref[...], halves[:, 0:shared], NT)
    total += dot1(ws_ref[...], halves[:, shared : 2 * shared], NT)
    wt = wt_ref[...]
    total += dot1(wt, halves[:, 2 * shared : 2 * shared + heads], NT)
    total += dot1(wt, halves[:, 2 * shared + LANES : 2 * shared + LANES + heads], NT)
    out_ref[0] = total


def weight_grad_kernel(tok_ref, gi_ref, out_ref):
    out_ref[...] = dot1(tok_ref[...], gi_ref[...], TN).reshape(out_ref.shape)


def side_grad_kernel(parts_ref, gstep_ref, tok_ref, out_ref, left):
    rows = parts_ref.shape[1]

    @pl.when(pl.program_id(0) == 0)
    def _():
        total = parts_ref[0]
        for i in range(1, parts_ref.shape[0]):
            total += parts_ref[i]
        steps = jnp.transpose(gstep_ref[...])[0:SLOT, :]
        high, low = split(jnp.concatenate([total, steps], 0))
        left[0] = high
        left[1] = low

    out_ref[...] = dot2((left[0], left[1]), tok_ref[...], NN)


def sum_kernel(parts_ref, out_ref):
    total = parts_ref[0]
    for i in range(1, parts_ref.shape[0]):
        total += parts_ref[i]
    out_ref[...] = jnp.transpose(total).astype(out_ref.dtype)


def whole(shape):
    return pl.BlockSpec(shape, lambda *_: (0,) * len(shape))


def smem():
    return pl.BlockSpec(memory_space=pltpu.SMEM)


def body(
    tokens,
    inner_weight,
    shared_weight,
    step_weight,
    conv_inner,
    conv_shared,
    step_bias,
    decay_rate,
    skip_gain,
    cotangent,
):
    length, width = tokens.shape
    inner = inner_weight.shape[1]
    shared = shared_weight.shape[1]
    heads = step_weight.shape[1]
    tiles = inner // LANES
    ctx = lax.axis_size("ctx")
    tp = lax.axis_size("tp")
    place = lax.axis_index("ctx")
    edge = jnp.stack([place, (place == ctx - 1).astype(jnp.int32)]).astype(jnp.int32)
    sds = jax.ShapeDtypeStruct

    rim = shifted(tokens[length - 8 :].astype(F32), "ctx", 1)
    params = jnp.pad(
        jnp.stack([step_bias, decay_rate, skip_gain]), ((0, 5), (0, LANES - heads))
    )

    block = 512
    total = inner + shared
    pay_rows = 8 * tiles + 8
    z, sp, dt, cum, cum_t, pay = pl.pallas_call(
        functools.partial(project_kernel, tiles, heads),
        grid=(width // block,),
        in_specs=[
            smem(),
            pl.BlockSpec((length, block), lambda i: (0, i)),
            pl.BlockSpec((8, block), lambda i: (0, i)),
            pl.BlockSpec((block, inner), lambda i: (i, 0)),
            pl.BlockSpec((block, shared), lambda i: (i, 0)),
            pl.BlockSpec((block, heads), lambda i: (i, 0)),
            whole((K, inner)),
            whole((K, shared)),
            whole((8, LANES)),
            whole((length, inner)),
        ],
        out_specs=[
            whole((length, total)),
            whole((length, LANES)),
            whole((length, LANES)),
            whole((length, LANES)),
            whole((SLOT, length)),
            whole((ctx, pay_rows, LANES)),
        ],
        out_shape=[
            sds((length, total), F32),
            sds((length, LANES), F32),
            sds((length, LANES), F32),
            sds((length, LANES), F32),
            sds((SLOT, length), F32),
            sds((ctx, pay_rows, LANES), F32),
        ],
        scratch_shapes=[
            pltpu.VMEM((length + 16, block), BF16),
            pltpu.VMEM((length + 16, inner), F32),
            pltpu.VMEM((length + 16, shared), F32),
            pltpu.VMEM((length + 16, LANES), F32),
        ],
        compiler_params=PARAMS,
        name="project",
    )(
        edge, tokens, rim, inner_weight, shared_weight, step_weight,
        conv_inner, conv_shared, params, cotangent,
    )

    by_rows = lax.all_to_all(pay, "ctx", 0, 0, tiled=True)

    y, u, db, dc = pl.pallas_call(
        local_kernel,
        grid=(tiles,),
        in_specs=[
            pl.BlockSpec((length, LANES), lambda i: (0, i)),
            pl.BlockSpec((length, LANES), lambda i: (0, tiles)),
            pl.BlockSpec((length, LANES), lambda i: (0, tiles + 1)),
            whole((length, LANES)),
            whole((length, LANES)),
            whole((SLOT, length)),
            pl.BlockSpec((length, LANES), lambda i: (0, i)),
        ],
        out_specs=[
            pl.BlockSpec((length, LANES), lambda i: (0, i)),
            pl.BlockSpec((length, LANES), lambda i: (0, i)),
            whole((length, LANES)),
            whole((length, LANES)),
        ],
        out_shape=[
            sds((length, inner), F32),
            sds((length, inner), F32),
            sds((length, LANES), F32),
            sds((length, LANES), F32),
        ],
        scratch_shapes=[
            pltpu.VMEM((2, length // 2, length // 2), F32),
            pltpu.VMEM((2, length // 2, length // 2), F32),
            pltpu.VMEM((length, LANES), F32),
            pltpu.VMEM((length, LANES), F32),
        ],
        compiler_params=PARAMS,
        cost_estimate=pl.CostEstimate(
            flops=10 * length * length * inner, bytes_accessed=8_000_000, transcendentals=0
        ),
        name="local",
    )(z, z, z, dt, cum, cum_t, cotangent)

    scanned = pl.pallas_call(
        functools.partial(ctx_scan_kernel, tiles),
        in_specs=[smem(), whole((ctx, pay_rows, LANES))],
        out_specs=whole((ctx, 8 * tiles, LANES)),
        out_shape=sds((ctx, 8 * tiles, LANES), F32),
        compiler_params=PARAMS,
        name="ctx_scan",
    )(edge, by_rows)
    arrived = lax.all_to_all(scanned, "ctx", 0, 0, tiled=True)

    mixed, dconv, gstep = pl.pallas_call(
        functools.partial(join_kernel, tiles),
        out_shape=[
            sds((length, inner), BF16),
            sds((length, total), F32),
            sds((length, LANES), F32),
        ],
        compiler_params=PARAMS,
        name="join",
    )(z, sp, dt, cum, params, cotangent, y, u, db, dc, pay, arrived)

    rim_back = shifted(dconv[0:8], "ctx", -1)
    grad_inner, grad_shared, grad_shared_t = pl.pallas_call(
        conv_back_kernel,
        in_specs=[
            smem(),
            whole((length, total)),
            whole((8, total)),
            whole((K, inner)),
            whole((K, shared)),
        ],
        out_specs=[whole((length, inner)), whole((length, shared)), whole((shared, length))],
        out_shape=[
            sds((length, inner), BF16),
            sds((length, shared), F32),
            sds((shared, length), F32),
        ],
        scratch_shapes=[pltpu.VMEM((length + 8, total), F32)],
        compiler_params=PARAMS,
        name="conv_back",
    )(edge, dconv, rim_back, conv_inner, conv_shared)

    shared_cols = shared // tp
    shared_parts = lax.all_to_all(
        grad_shared_t.reshape(tp, shared_cols, length), "tp", 0, 0, tiled=True
    )

    rows = width // ctx
    per = 8
    weight_parts = pl.pallas_call(
        weight_grad_kernel,
        grid=(ctx // per,),
        in_specs=[
            pl.BlockSpec((length, per * rows), lambda i: (0, i)),
            whole((length, inner)),
        ],
        out_specs=pl.BlockSpec((per, rows, inner), lambda i: (i, 0, 0)),
        out_shape=sds((ctx, rows, inner), F32),
        compiler_params=PARAMS,
        name="weight_grad",
    )(tokens, grad_inner)
    grad_inner_weight = lax.psum_scatter(weight_parts, "ctx", scatter_dimension=0, tiled=False)

    cols = width // tp
    token_parts = pl.pallas_call(
        functools.partial(token_grad_kernel, heads),
        grid=(tp,),
        in_specs=[
            pl.BlockSpec((cols, inner), lambda i: (i, 0)),
            pl.BlockSpec((cols, shared), lambda i: (i, 0)),
            pl.BlockSpec((cols, heads), lambda i: (i, 0)),
            whole((length, inner)),
            whole((length, shared)),
            whole((length, LANES)),
        ],
        out_specs=pl.BlockSpec((1, cols, length), lambda i: (i, 0, 0)),
        out_shape=sds((tp, cols, length), F32),
        scratch_shapes=[pltpu.VMEM((length, 2 * shared + 2 * LANES), BF16)],
        compiler_params=PARAMS,
        name="token_grad",
    )(inner_weight, shared_weight, step_weight, grad_inner, grad_shared, gstep)
    token_parts = lax.all_to_all(token_parts, "tp", 0, 0, tiled=True)

    side_rows = shared_cols + SLOT
    side = pl.pallas_call(
        side_grad_kernel,
        grid=(width // block,),
        in_specs=[
            whole((tp, shared_cols, length)),
            whole((length, LANES)),
            pl.BlockSpec((length, block), lambda i: (0, i)),
        ],
        out_specs=pl.BlockSpec((side_rows, block), lambda i: (0, i)),
        out_shape=sds((side_rows, width), F32),
        scratch_shapes=[pltpu.VMEM((2, side_rows, length), BF16)],
        compiler_params=PARAMS,
        name="side_grad",
    )(shared_parts, gstep, tokens)
    side = jnp.transpose(side.reshape(side_rows, ctx, rows), (1, 0, 2))
    side = jnp.sum(lax.all_to_all(side, "ctx", 0, 0, tiled=True), 0).T

    grad_tokens = pl.pallas_call(
        sum_kernel,
        out_shape=sds((length, cols), BF16),
        compiler_params=PARAMS,
        name="token_sum",
    )(token_parts)
    return (
        mixed,
        grad_tokens,
        grad_inner_weight,
        side[:, :shared_cols],
        side[:, shared_cols : shared_cols + heads],
    )


def solution(mesh):
    in_specs = (
        P("ctx", None),
        P(None, "tp"),
        P(),
        P(None, "tp"),
        P(None, "tp"),
        P(),
        P("tp"),
        P("tp"),
        P("tp"),
        P("ctx", "tp"),
    )
    out_specs = (P("ctx", "tp"), P("ctx", "tp"), P("ctx", "tp"), P("ctx", "tp"), P("ctx", "tp"))
    return jax.shard_map(body, mesh=mesh, in_specs=in_specs, out_specs=out_specs, check_vma=False)
```

```python
import functools

import jax
import jax.numpy as jnp
from jax import lax
from jax.experimental import pallas as pl
from jax.experimental.pallas import tpu as pltpu
from jax.sharding import PartitionSpec as P

P_SIZE = 64
N = 128
K = 4
LANES = 128
SLOT = 16
CORES = 2
RING = 4
F32 = jnp.float32
BF16 = jnp.bfloat16
NN = (((1,), (0,)), ((), ()))
NT = (((1,), (1,)), ((), ()))
TN = (((0,), (0,)), ((), ()))
PARAMS = pltpu.CompilerParams(vmem_limit_bytes=60 * 1024 * 1024)


def shifted(block, axis, distance):
    size = lax.axis_size(axis)
    return lax.ppermute(block, axis, [(i, (i + distance) % size) for i in range(size)])


def ctx_shift(block, dy, dz, dcore):
    def at(y, z, core):
        return (y % RING) * RING * CORES + (z % RING) * CORES + core % CORES

    route = [
        (at(y, z, core), at(y + dy, z + dz, core + dcore))
        for y in range(RING)
        for z in range(RING)
        for core in range(CORES)
    ]
    return lax.ppermute(block, "ctx", route)


def dot1(a, b, dims):
    return lax.dot_general(a, b, dims, preferred_element_type=F32)


def split(a):
    high = a.astype(BF16)
    return high, (a - high.astype(F32)).astype(BF16)


def dot3(a, b, dims):
    ah, al = a
    bh, bl = b
    return dot1(ah, bh, dims) + (dot1(ah, bl, dims) + dot1(al, bh, dims))


def dot2(a, b, dims):
    return dot1(a[0], b, dims) + dot1(a[1], b, dims)


def sigmoid(z):
    return 1.0 / (1.0 + jnp.exp(-z))


def of_tile(cols, k):
    lane = lax.broadcasted_iota(jnp.int32, (cols.shape[0], LANES), 1)
    left = jnp.broadcast_to(cols[:, 2 * k : 2 * k + 1], lane.shape)
    right = jnp.broadcast_to(cols[:, 2 * k + 1 : 2 * k + 2], lane.shape)
    return jnp.where(lane < P_SIZE, left, right)


def moving_tile(cols, k):
    return of_tile(pltpu.roll(cols, (LANES - 2 * k) % LANES, 1), 0)


def triangle_sum(a, dims):
    length = a.shape[0]
    row = lax.broadcasted_iota(jnp.int32, (length, length), 0)
    col = lax.broadcasted_iota(jnp.int32, (length, length), 1)
    reach = row >= col if dims == NN else row <= col
    ones = jnp.where(reach, 1.0, 0.0).astype(BF16)
    first = a.astype(BF16).astype(F32)
    second = (a - first).astype(BF16).astype(F32)
    third = (a - first - second).astype(BF16).astype(F32)
    packed = first + pltpu.roll(second, SLOT, 1) + pltpu.roll(third, 2 * SLOT, 1)
    sums = dot1(ones, packed.astype(BF16), NN)
    total = sums + pltpu.roll(sums, LANES - SLOT, 1) + pltpu.roll(sums, LANES - 2 * SLOT, 1)
    lane = lax.broadcasted_iota(jnp.int32, total.shape, 1)
    return jnp.where(lane < SLOT, total, 0.0)


def project_kernel(
    tiles, heads,
    edge_ref, tok_ref, rim_ref, wi_ref, ws_ref, wt_ref, ci_ref, cs_ref, par_ref, cot_ref,
    z_ref, sp_ref, dt_ref, cum_ref, cumt_ref, keep_ref, send_ref,
    lhs, acc_i, acc_s, acc_t,
):
    step = pl.program_id(0)
    length = tok_ref.shape[0]
    head_rows = lhs.shape[0] - length
    inner = wi_ref.shape[1]

    @pl.when(step == 0)
    def _():
        acc_i[...] = jnp.zeros_like(acc_i)
        acc_s[...] = jnp.zeros_like(acc_s)
        acc_t[...] = jnp.zeros_like(acc_t)

    keep = jnp.where(edge_ref[0] == 0, 0.0, 1.0)
    rim = rim_ref[...] * keep
    lhs[0:head_rows, :] = jnp.concatenate([jnp.zeros_like(rim), rim], 0).astype(BF16)
    lhs[head_rows:, :] = tok_ref[...]
    left = lhs[...]
    acc_i[...] += dot1(left, wi_ref[...], NN)
    acc_s[...] += dot1(left, ws_ref[...], NN)
    acc_t[:, 0:heads] += dot1(left, wt_ref[...], NT)

    @pl.when(step == pl.num_programs(0) - 1)
    def _():
        start = head_rows - (K - 1)
        sp = acc_t[head_rows:, :] + par_ref[0:1, :]
        sp_ref[...] = sp
        dt = jnp.maximum(sp, 0.0) + jnp.log1p(jnp.exp(-jnp.abs(sp)))
        dt_ref[...] = dt
        cum = triangle_sum(-par_ref[1:2, :] * dt, NN)
        cum_ref[...] = cum
        cumt_ref[...] = jnp.transpose(cum)[0:SLOT, :]
        last = cum[length - 1 :, :]
        write_weight = dt * jnp.exp(last - cum)
        read_weight = jnp.exp(cum)

        def conv(acc, taps, k):
            lo = k * LANES
            out = taps[0:1, lo : lo + LANES] * acc[start : start + length, lo : lo + LANES]
            for j in range(1, K):
                out += taps[j : j + 1, lo : lo + LANES] * acc[
                    start + j : start + j + length, lo : lo + LANES
                ]
            return out

        zb = conv(acc_s, cs_ref, 0)
        z_ref[:, inner : inner + LANES] = zb
        zc = conv(acc_s, cs_ref, 1)
        z_ref[:, inner + LANES :] = zc
        b2 = split(zb * sigmoid(zb))
        c2 = split(zc * sigmoid(zc))
        groups = N // 8
        forward = edge_ref[2] == 0
        blank = jnp.zeros((groups, 8, LANES), F32)
        keep_ref[:, 8 * tiles :, :] = blank
        send_ref[:, 8 * tiles :, :] = blank
        for k in range(tiles):
            lo = k * LANES
            rows = slice(8 * k, 8 * k + 8)
            z = conv(acc_i, ci_ref, k)
            z_ref[:, lo : lo + LANES] = z
            x2 = split(z * sigmoid(z) * of_tile(write_weight, k))
            state = dot3(b2, x2, TN)
            g2 = split(cot_ref[:, lo : lo + LANES].astype(F32) * of_tile(read_weight, k))
            grad = dot3(c2, g2, TN)
            keep_ref[:, rows, :] = jnp.where(forward, state, grad).reshape(groups, 8, LANES)
            send_ref[:, rows, :] = jnp.where(forward, grad, state).reshape(groups, 8, LANES)
            row = jnp.broadcast_to(of_tile(last, k)[None], (groups, 1, LANES))
            keep_ref[:, 8 * tiles + k : 8 * tiles + k + 1, :] = row
            send_ref[:, 8 * tiles + k : 8 * tiles + k + 1, :] = row


def decay_rows(tiles, block):
    decay = jnp.exp(block[..., 8 * tiles :, :])
    shape = block.shape[:-2] + (8, LANES)
    return jnp.concatenate(
        [jnp.broadcast_to(decay[..., k : k + 1, :], shape) for k in range(tiles)], -2
    )


def chip_kernel(tiles, keep_ref, got_ref, out_ref):
    rows = 8 * tiles
    for i in range(keep_ref.shape[0]):
        keep = keep_ref[i]
        got = got_ref[i]
        out_ref[i, 0:rows, :] = got[0:rows, :] + decay_rows(tiles, got) * keep[0:rows, :]
        out_ref[i, rows:, :] = got[rows:, :] + keep[rows:, :]


def onward_kernel(tiles, keep_ref, arrived_ref, out_ref):
    rows = 8 * tiles
    for i in range(keep_ref.shape[0]):
        keep = keep_ref[i]
        out_ref[i] = keep[0:rows, :] + decay_rows(tiles, keep) * arrived_ref[i]


def ctx_scan_kernel(tiles, edge_ref, in_ref, after_ref, out_ref):
    count = in_ref.shape[0]
    rows = 8 * tiles
    backward = edge_ref[2] == 1

    def turn(i, held):
        at = jnp.where(backward, count - 1 - i, i)
        out_ref[at] = held
        got = in_ref[at]
        return got[0:rows, :] + decay_rows(tiles, got) * held

    lax.fori_loop(0, count, turn, jnp.zeros((rows, LANES), F32), unroll=4)


def local_kernel(
    zv_ref, zb_ref, zc_ref, dt_ref, cum_ref, cumt_ref, cot_ref,
    y_ref, u_ref, db_ref, dc_ref,
    scores, grad_scores, dt_wide, cum_wide,
):
    tile = pl.program_id(0)
    length = zv_ref.shape[0]
    half = length // 2
    zb = zb_ref[...]
    zc = zc_ref[...]
    b = zb * sigmoid(zb)
    c = zc * sigmoid(zc)
    bh, bl = split(b)
    ch, cl = split(c)

    @pl.when(tile == 0)
    def _():
        row = lax.broadcasted_iota(jnp.int32, (half, half), 0)
        col = lax.broadcasted_iota(jnp.int32, (half, half), 1)
        for chunk in range(2):
            at = slice(chunk * half, (chunk + 1) * half)
            full = dot3((ch[at], cl[at]), (bh[at], bl[at]), NT)
            scores[chunk] = jnp.where(row >= col, full, 0.0)
        grad_scores[...] = jnp.zeros_like(grad_scores)
        db_ref[...] = jnp.zeros_like(db_ref)
        dc_ref[...] = jnp.zeros_like(dc_ref)

    lane = lax.broadcasted_iota(jnp.int32, (length, LANES), 1)

    def pick(ref):
        cols = pltpu.roll(ref[...], (LANES - 2 * tile) % LANES, 1)
        return cols[:, 0:1], cols[:, 1:2]

    dt_cols = pick(dt_ref)
    cum_cols = pick(cum_ref)
    dt_wide[...] = jnp.where(lane < P_SIZE, dt_cols[0], dt_cols[1])
    cum_wide[...] = jnp.where(lane < P_SIZE, cum_cols[0], cum_cols[1])
    zv = zv_ref[...]
    x = zv * sigmoid(zv) * dt_wide[...]
    g = cot_ref[...]
    xh, xl = split(x)
    gt = jnp.transpose(g.astype(F32)).astype(BF16)

    for chunk in range(2):
        at = slice(chunk * half, (chunk + 1) * half)
        ys = []
        us = []
        for head in range(2):
            of = slice(head * P_SIZE, (head + 1) * P_SIZE)
            row_logs = cumt_ref[pl.ds(2 * tile + head, 1), at]
            gaps = jnp.minimum(cum_cols[head][at] - row_logs, 0.0)
            decays = jnp.exp(gaps)
            weights = scores[chunk] * decays
            wh, wl = split(weights)
            x_pair = jnp.concatenate([xh[at, of], xl[at, of]], 1)
            y_pair = dot1(wh, x_pair, NN) + dot1(wl, x_pair, NN)
            ys.append(y_pair[:, 0:P_SIZE] + y_pair[:, P_SIZE:])
            us.append(dot1(gt[of, at], wh, NN) + dot1(gt[of, at], wl, NN))
            g_pair = jnp.concatenate([g[at, of], g[at, of]], 1)
            grad_scores[chunk] += dot1(g_pair, x_pair, NT) * decays
        y_ref[at, :] = jnp.concatenate(ys, 1)
        u_ref[at, :] = jnp.transpose(jnp.concatenate(us, 0))

    early = slice(0, half)
    late = slice(half, length)
    cum = cum_wide[...]
    middle = cum[half - 1 : half, :]
    down = jnp.exp(middle - cum[early])
    up = jnp.exp(cum[late] - middle)
    xd = split(x[early] * down)
    gd = split(g[late].astype(F32) * up)
    b0 = (bh[early], bl[early])
    c1 = (ch[late], cl[late])
    state = split(dot3(b0, xd, TN))
    grad = split(dot3(c1, gd, TN))
    y_ref[late, :] += up * dot3(c1, state, NN)
    u_ref[early, :] += down * dot3(b0, grad, NN)
    dc_ref[late, :] += dot3(gd, state, NT)
    db_ref[early, :] += dot3(xd, grad, NT)

    @pl.when(tile == pl.num_programs(0) - 1)
    def _():
        row = lax.broadcasted_iota(jnp.int32, (half, half), 0)
        col = lax.broadcasted_iota(jnp.int32, (half, half), 1)
        for chunk in range(2):
            at = slice(chunk * half, (chunk + 1) * half)
            gs = split(jnp.where(row >= col, grad_scores[chunk], 0.0))
            dc_ref[at, :] += dot3(gs, (bh[at], bl[at]), NN)
            db_ref[at, :] += dot3(gs, (ch[at], cl[at]), TN)


def join_kernel(
    tiles,
    edge_ref, zv_ref, zb_ref, zc_ref, sp_ref, dt_ref, cum_ref, par_ref, cot_ref, y_ref, u_ref,
    db_ref, dc_ref, keep_ref, send_ref, arrived_ref, other_ref,
    mixed_ref, dinner_ref, dshared_ref, gstep_ref, rim_ref,
    reads, writes, ends, db_sum, dc_sum,
):
    k = pl.program_id(0)
    length = zv_ref.shape[0]
    groups = N // 8
    forward = edge_ref[2] == 0

    @pl.when(k == 0)
    def _():
        reads[...] = jnp.zeros_like(reads)
        writes[...] = jnp.zeros_like(writes)
        ends[...] = jnp.zeros_like(ends)
        db_sum[...] = db_ref[...]
        dc_sum[...] = dc_ref[...]

    zb = zb_ref[...]
    zc = zc_ref[...]
    sb = sigmoid(zb)
    sc = sigmoid(zc)
    b2 = split(zb * sb)
    c2 = split(zc * sc)
    lane = lax.broadcasted_iota(jnp.int32, (LANES, LANES), 1)
    row = lax.broadcasted_iota(jnp.int32, (LANES, LANES), 0)
    gather = jnp.where(lane == 2 * k + row // P_SIZE, 1.0, 0.0).astype(BF16)
    rows = pl.ds(pl.multiple_of(8 * k, 8), 8)
    arrived = arrived_ref[:, rows, :].reshape(N, LANES)
    other = other_ref[:, rows, :].reshape(N, LANES)
    keep = keep_ref[:, rows, :].reshape(N, LANES)
    send = send_ref[:, rows, :].reshape(N, LANES)
    state = jnp.where(forward, arrived, other)
    grad = jnp.where(forward, other, arrived)
    own = jnp.where(forward, keep, send)
    state2 = split(state)
    grad2 = split(grad)
    z = zv_ref[...]
    s = sigmoid(z)
    v = z * s
    g = cot_ref[...].astype(F32)
    cum = moving_tile(cum_ref[...], k)
    dt_k = moving_tile(dt_ref[...], k)
    skip = moving_tile(par_ref[...], k)[2:3, :]
    last = cum[length - 1 :, :]
    read_k = jnp.exp(cum)
    tail_k = jnp.exp(last - cum)
    y = y_ref[...] + read_k * dot3(c2, state2, NN)
    u = u_ref[...] + tail_k * dot3(b2, grad2, NN)
    mixed_ref[...] = (y + skip * v).astype(BF16)
    dv = dt_k * u + skip * g
    dinner = dv * (s * (1.0 + z * (1.0 - s)))
    dinner_ref[...] = dinner
    rim_ref[:, pl.ds(pl.multiple_of(k * LANES, LANES), LANES)] = dinner[0:8]
    reads[...] += dot2(split(g * y), gather, NN)
    writes[...] += dot2(split(v * u), gather, NN)
    dc_sum[...] += dot3(split(g * read_k), state2, NT)
    db_sum[...] += dot3(split(v * dt_k * tail_k), grad2, NT)
    end = jnp.sum(grad * (own + jnp.exp(last) * state), 0, keepdims=True)
    ends[...] += dot2(split(jnp.broadcast_to(end, (8, LANES))), gather, NN)

    @pl.when(k == tiles - 1)
    def _():
        dshared_ref[:, 0:LANES] = db_sum[...] * (sb * (1.0 + zb * (1.0 - sb)))
        dshared_ref[:, LANES:] = dc_sum[...] * (sc * (1.0 + zc * (1.0 - sc)))
        rim_ref[:, tiles * LANES :] = dshared_ref[0:8, :]
        grad_logs = triangle_sum(reads[...] - dt_ref[...] * writes[...], TN) + ends[0:1]
        grad_dt = writes[...] - par_ref[1:2, :] * grad_logs
        gstep_ref[...] = grad_dt * sigmoid(sp_ref[...])


def conv_back_kernel(
    edge_ref, dinner_ref, dshared_ref, rim_ref, ci_ref, cs_ref, gstep_ref,
    gi_ref, gst_ref, right_ref, wide_i, wide_s,
):
    length, inner = dinner_ref.shape
    shared = dshared_ref.shape[1]
    rim = rim_ref[...] * jnp.where(edge_ref[1] == 0, 1.0, 0.0)
    wide_i[0:length, :] = dinner_ref[...]
    wide_i[length:, :] = rim[:, 0:inner]
    wide_s[0:length, :] = dshared_ref[...]
    wide_s[length:, :] = rim[:, inner:]

    def back(wide, taps, k):
        at = slice(k * LANES, (k + 1) * LANES)
        out = taps[K - 1 : K, at] * wide[0:length, at]
        for j in range(1, K):
            out += taps[K - 1 - j : K - j, at] * wide[j : j + length, at]
        return out

    for k in range(shared // LANES):
        at = slice(k * LANES, (k + 1) * LANES)
        grad = jnp.transpose(back(wide_s, cs_ref, k))
        gst_ref[at, :] = grad
        high, low = split(grad)
        right_ref[inner + k * LANES : inner + (k + 1) * LANES, :] = high
        right_ref[inner + shared + k * LANES : inner + shared + (k + 1) * LANES, :] = low
    high, low = split(jnp.transpose(gstep_ref[...])[0:SLOT, :])
    right_ref[inner + 2 * shared : inner + 2 * shared + SLOT, :] = high
    right_ref[inner + 2 * shared + SLOT :, :] = low
    for k in range(inner // LANES):
        at = slice(k * LANES, (k + 1) * LANES)
        grad = back(wide_i, ci_ref, k)
        gi_ref[:, at] = grad.astype(BF16)
        right_ref[at, :] = jnp.transpose(grad).astype(BF16)


def token_grad_kernel(heads, wi_ref, ws_ref, wt_ref, right_ref, after_ref, out_ref, left):
    inner = wi_ref.shape[1]
    shared = ws_ref.shape[1]
    end = inner + 2 * shared
    left[:, 0:inner] = wi_ref[...]
    left[:, inner : inner + shared] = ws_ref[...]
    left[:, inner + shared : end] = ws_ref[...]
    blank = jnp.zeros((SLOT - heads, left.shape[0]), F32)
    step = jnp.concatenate([wt_ref[...].astype(F32), blank], 0)
    left[:, end:] = jnp.transpose(jnp.concatenate([step, step], 0)).astype(BF16)
    out_ref[...] = dot1(left[...], right_ref[...], NN).reshape(out_ref.shape)


def put_rows(edge_ref, product, mine_ref, other_ref):
    rows = mine_ref.shape[1] * mine_ref.shape[2] // RING
    parts = product.reshape(RING, CORES, rows, product.shape[1])

    def put(first, second):
        for z in range(RING):
            at = z * rows % mine_ref.shape[2]
            first[0, z * rows // mine_ref.shape[2], at : at + rows, :] = parts[z, 0]
            second[0, z * rows // mine_ref.shape[2], at : at + rows, :] = parts[z, 1]

    @pl.when(edge_ref[2] == 0)
    def _():
        put(mine_ref, other_ref)

    @pl.when(edge_ref[2] == 1)
    def _():
        put(other_ref, mine_ref)


def weight_grad_kernel(
    edge_ref, tok_ref, gi_ref, mine_a_ref, other_a_ref, mine_b_ref, other_b_ref
):
    product = dot1(tok_ref[...], gi_ref[...], TN)
    lanes = mine_a_ref.shape[3]
    put_rows(edge_ref, product[:, 0:lanes], mine_a_ref, other_a_ref)
    put_rows(edge_ref, product[:, lanes:], mine_b_ref, other_b_ref)


def side_grad_kernel(
    edge_ref, parts_ref, gstep_ref, tok_ref, after_ref, mine_ref, other_ref, right
):
    shared_cols = parts_ref.shape[1]

    @pl.when(pl.program_id(0) == 0)
    def _():
        total = parts_ref[0]
        for i in range(1, parts_ref.shape[0]):
            total += parts_ref[i]
        blank = jnp.zeros((LANES - shared_cols, total.shape[1]), F32)
        cols = jnp.transpose(jnp.concatenate([total, blank], 0))
        high, low = split(cols + pltpu.roll(gstep_ref[...], shared_cols, 1))
        right[:, 0:LANES] = high
        right[:, LANES:] = low

    both = dot1(tok_ref[...], right[...], TN)
    put_rows(edge_ref, both[:, 0:LANES] + both[:, LANES:], mine_ref, other_ref)


def ring_parts(place, part, up_ref, down_ref, hold_ref, own_ref):
    above, facing, below = [(place + i) % RING for i in (1, 2, 3)]
    up_ref[0] = part(facing, 0)
    up_ref[1] = part(above, 1)
    down_ref[0] = part(facing, 1)
    down_ref[1] = part(below, 0)
    hold_ref[0] = part(above, 0)
    hold_ref[1] = part(below, 1)
    own_ref[0] = part(place, 0)
    own_ref[1] = part(place, 1)


def core_sum_kernel(edge_ref, *refs):
    blocks = refs[:-5]
    up_ref, down_ref, hold_ref, own_ref = refs[-4:]

    def part(target, half):
        sums = [
            blocks[i][target, half] + blocks[i + 1][target, half]
            for i in range(0, len(blocks), 2)
        ]
        return jnp.concatenate(sums, 1) if len(sums) > 1 else sums[0]

    ring_parts(edge_ref[3], part, up_ref, down_ref, hold_ref, own_ref)


def pass_on_kernel(hold_ref, from_below_ref, from_above_ref, after_ref, up_ref, down_ref):
    up_ref[...] = hold_ref[0] + from_below_ref[0]
    down_ref[...] = hold_ref[1] + from_above_ref[0]


def ring_sum(own_ref, from_below_ref, from_above_ref, last_below_ref, last_above_ref):
    first = own_ref[0] + from_above_ref[1] + last_below_ref[...]
    second = own_ref[1] + from_below_ref[1] + last_above_ref[...]
    return first, second


def next_ring_kernel(
    edge_ref, own_in, from_below_ref, from_above_ref, last_below_ref, last_above_ref, after_ref,
    up_ref, down_ref, hold_ref, own_ref, sums,
):
    first, second = ring_sum(
        own_in, from_below_ref, from_above_ref, last_below_ref, last_above_ref
    )
    half = RING // 2
    shape = (half,) + sums.shape[1:]
    sums[0:half] = first.reshape(shape)
    sums[half:] = second.reshape(shape)

    def part(target, which):
        return sums[target, which]

    ring_parts(edge_ref[4], part, up_ref, down_ref, hold_ref, own_ref)


def last_ring_kernel(*refs):
    inner_ref, shared_ref, step_ref, side = refs[10:]
    half = inner_ref.shape[0] // 2
    at = (slice(0, half), slice(half, 2 * half))
    lanes = refs[0].shape[2]
    shared_cols = shared_ref.shape[0]
    rest = inner_ref.shape[1] - lanes
    side[2 * half :, :] = jnp.zeros((side.shape[0] - 2 * half, LANES), F32)
    for rows, part in zip(at, ring_sum(*refs[0:5])):
        inner_ref[rows, 0:lanes] = part
    for rows, part in zip(at, ring_sum(*refs[5:10])):
        inner_ref[rows, lanes:] = part[:, 0:rest]
        side[rows, :] = part[:, rest:]
    flat = jnp.transpose(side[...])
    shared_ref[...] = flat[0:shared_cols, 0 : 2 * half]
    step_ref[...] = flat[shared_cols : shared_cols + step_ref.shape[0], 0 : 2 * half]


def sum_kernel(parts_ref, out_ref):
    total = parts_ref[0]
    for i in range(1, parts_ref.shape[0]):
        total += parts_ref[i]
    out_ref[...] = total.astype(out_ref.dtype)


def whole(shape):
    return pl.BlockSpec(shape, lambda *_: (0,) * len(shape))


def after():
    return pl.BlockSpec(memory_space=pl.ANY)


def smem():
    return pl.BlockSpec(memory_space=pltpu.SMEM)


def body(
    tokens,
    inner_weight,
    shared_weight,
    step_weight,
    conv_inner,
    conv_shared,
    step_bias,
    decay_rate,
    skip_gain,
    cotangent,
):
    length, width = tokens.shape
    inner = inner_weight.shape[1]
    shared = shared_weight.shape[1]
    heads = step_weight.shape[1]
    tiles = inner // LANES
    ctx = lax.axis_size("ctx")
    tp = lax.axis_size("tp")
    place = lax.axis_index("ctx")
    core = place % CORES
    z_place = place // CORES % RING
    y_place = place // (CORES * RING)
    edge = jnp.stack([place, (place == ctx - 1).astype(jnp.int32), core, y_place, z_place])
    edge = edge.astype(jnp.int32)
    chips = ctx // CORES
    same_core = [[CORES * chip + i for chip in range(chips)] for i in range(CORES)]
    sds = jax.ShapeDtypeStruct
    step_weight_t = step_weight.T

    rim = shifted(tokens[length - 8 :].astype(F32), "ctx", 1)
    params = jnp.pad(
        jnp.stack([step_bias, decay_rate, skip_gain]), ((0, 5), (0, LANES - heads))
    )

    block = 512
    total = inner + shared
    pay_rows = 8 * tiles + 8
    z, sp, dt, cum, cum_t, keep, send = pl.pallas_call(
        functools.partial(project_kernel, tiles, heads),
        grid=(width // block,),
        in_specs=[
            smem(),
            pl.BlockSpec((length, block), lambda i: (0, i)),
            pl.BlockSpec((8, block), lambda i: (0, i)),
            pl.BlockSpec((block, inner), lambda i: (i, 0)),
            pl.BlockSpec((block, shared), lambda i: (i, 0)),
            pl.BlockSpec((heads, block), lambda i: (0, i)),
            whole((K, inner)),
            whole((K, shared)),
            whole((8, LANES)),
            whole((length, inner)),
        ],
        out_specs=[
            whole((length, total)),
            whole((length, LANES)),
            whole((length, LANES)),
            whole((length, LANES)),
            whole((SLOT, length)),
            whole((chips, pay_rows, LANES)),
            whole((chips, pay_rows, LANES)),
        ],
        out_shape=[
            sds((length, total), F32),
            sds((length, LANES), F32),
            sds((length, LANES), F32),
            sds((length, LANES), F32),
            sds((SLOT, length), F32),
            sds((chips, pay_rows, LANES), F32),
            sds((chips, pay_rows, LANES), F32),
        ],
        scratch_shapes=[
            pltpu.VMEM((length + 16, block), BF16),
            pltpu.VMEM((length + 16, inner), F32),
            pltpu.VMEM((length + 16, shared), F32),
            pltpu.VMEM((length + 16, LANES), F32),
        ],
        compiler_params=PARAMS,
        name="project",
    )(
        edge, tokens, rim, inner_weight, shared_weight, step_weight_t,
        conv_inner, conv_shared, params, cotangent,
    )

    got = ctx_shift(send, 0, 0, 1)
    chip_state = pl.pallas_call(
        functools.partial(chip_kernel, tiles),
        out_shape=sds((chips, pay_rows, LANES), F32),
        compiler_params=PARAMS,
        name="chip_state",
    )(keep, got)
    by_rows = lax.all_to_all(
        chip_state, "ctx", 0, 0, axis_index_groups=same_core, tiled=True
    )

    y, u, db, dc = pl.pallas_call(
        local_kernel,
        grid=(tiles,),
        in_specs=[
            pl.BlockSpec((length, LANES), lambda i: (0, i)),
            pl.BlockSpec((length, LANES), lambda i: (0, tiles)),
            pl.BlockSpec((length, LANES), lambda i: (0, tiles + 1)),
            whole((length, LANES)),
            whole((length, LANES)),
            whole((SLOT, length)),
            pl.BlockSpec((length, LANES), lambda i: (0, i)),
        ],
        out_specs=[
            pl.BlockSpec((length, LANES), lambda i: (0, i)),
            pl.BlockSpec((length, LANES), lambda i: (0, i)),
            whole((length, LANES)),
            whole((length, LANES)),
        ],
        out_shape=[
            sds((length, inner), F32),
            sds((length, inner), F32),
            sds((length, LANES), F32),
            sds((length, LANES), F32),
        ],
        scratch_shapes=[
            pltpu.VMEM((2, length // 2, length // 2), F32),
            pltpu.VMEM((2, length // 2, length // 2), F32),
            pltpu.VMEM((length, LANES), F32),
            pltpu.VMEM((length, LANES), F32),
        ],
        compiler_params=PARAMS,
        cost_estimate=pl.CostEstimate(
            flops=10 * length * length * inner, bytes_accessed=8_000_000, transcendentals=0
        ),
        name="local",
    )(z, z, z, dt, cum, cum_t, cotangent)

    scanned = pl.pallas_call(
        functools.partial(ctx_scan_kernel, tiles),
        in_specs=[smem(), whole((chips, pay_rows, LANES)), after()],
        out_specs=whole((chips, 8 * tiles, LANES)),
        out_shape=sds((chips, 8 * tiles, LANES), F32),
        compiler_params=PARAMS,
        name="ctx_scan",
    )(edge, by_rows, dc)
    arrived = lax.all_to_all(scanned, "ctx", 0, 0, axis_index_groups=same_core, tiled=True)
    onward = pl.pallas_call(
        functools.partial(onward_kernel, tiles),
        out_shape=sds((chips, 8 * tiles, LANES), F32),
        compiler_params=PARAMS,
        name="onward",
    )(keep, arrived)
    other = ctx_shift(onward, 0, 0, 1)

    tile = pl.BlockSpec((length, LANES), lambda i: (0, i))
    column = whole((length, LANES))
    mixed, dinner, dshared, gstep, rim_out = pl.pallas_call(
        functools.partial(join_kernel, tiles),
        grid=(tiles,),
        in_specs=[
            smem(),
            tile,
            pl.BlockSpec((length, LANES), lambda i: (0, tiles)),
            pl.BlockSpec((length, LANES), lambda i: (0, tiles + 1)),
            column,
            column,
            column,
            whole((8, LANES)),
            tile,
            tile,
            tile,
            column,
            column,
            whole((chips, pay_rows, LANES)),
            whole((chips, pay_rows, LANES)),
            whole((chips, 8 * tiles, LANES)),
            whole((chips, 8 * tiles, LANES)),
        ],
        out_specs=[tile, tile, whole((length, shared)), column, whole((8, total))],
        out_shape=[
            sds((length, inner), BF16),
            sds((length, inner), F32),
            sds((length, shared), F32),
            sds((length, LANES), F32),
            sds((8, total), F32),
        ],
        scratch_shapes=[
            pltpu.VMEM((length, LANES), F32),
            pltpu.VMEM((length, LANES), F32),
            pltpu.VMEM((8, LANES), F32),
            pltpu.VMEM((length, LANES), F32),
            pltpu.VMEM((length, LANES), F32),
        ],
        compiler_params=PARAMS,
        name="join",
    )(
        edge, z, z, z, sp, dt, cum, params, cotangent, y, u, db, dc,
        keep, send, arrived, other,
    )

    rim_back = shifted(rim_out, "ctx", -1)
    right_rows = inner + 2 * shared + 2 * SLOT
    grad_inner, grad_shared_t, right = pl.pallas_call(
        conv_back_kernel,
        in_specs=[
            smem(),
            whole((length, inner)),
            whole((length, shared)),
            whole((8, total)),
            whole((K, inner)),
            whole((K, shared)),
            column,
        ],
        out_specs=[
            whole((length, inner)), whole((shared, length)), whole((right_rows, length)),
        ],
        out_shape=[
            sds((length, inner), BF16),
            sds((shared, length), F32),
            sds((right_rows, length), BF16),
        ],
        scratch_shapes=[
            pltpu.VMEM((length + 8, inner), F32),
            pltpu.VMEM((length + 8, shared), F32),
        ],
        compiler_params=PARAMS,
        name="conv_back",
    )(edge, dinner, dshared, rim_back, conv_inner, conv_shared, gstep)

    shared_cols = shared // tp
    shared_parts = lax.all_to_all(
        grad_shared_t.reshape(tp, shared_cols, length), "tp", 0, 0, tiled=True
    )

    rows = width // ctx
    y_half = RING * rows // 2
    z_half = rows // 2
    lanes = (inner + LANES) // 2
    rest = inner - lanes

    def row_block(wide):
        return pl.BlockSpec((1, 2, y_half, wide), lambda i: (i, 0, 0, 0))

    def row_shape(wide):
        return sds((RING, 2, y_half, wide), F32)

    mine, other_a, mine_b, other_b = pl.pallas_call(
        weight_grad_kernel,
        grid=(RING,),
        in_specs=[
            smem(),
            pl.BlockSpec((length, width // RING), lambda i: (0, i)),
            whole((length, inner)),
        ],
        out_specs=[row_block(lanes)] * 2 + [row_block(rest)] * 2,
        out_shape=[row_shape(lanes)] * 2 + [row_shape(rest)] * 2,
        compiler_params=PARAMS,
        name="weight_grad",
    )(edge, tokens, grad_inner)
    got_a = ctx_shift(other_a, 0, 0, 1)
    got_b = ctx_shift(other_b, 0, 0, 1)

    cols = width // tp
    per = 2
    token_parts = pl.pallas_call(
        functools.partial(token_grad_kernel, heads),
        grid=(tp // per,),
        in_specs=[
            pl.BlockSpec((per * cols, inner), lambda i: (i, 0)),
            pl.BlockSpec((per * cols, shared), lambda i: (i, 0)),
            pl.BlockSpec((heads, per * cols), lambda i: (0, i)),
            whole((right_rows, length)),
            after(),
        ],
        out_specs=pl.BlockSpec((per, cols, length), lambda i: (i, 0, 0)),
        out_shape=sds((tp, cols, length), F32),
        scratch_shapes=[pltpu.VMEM((per * cols, right_rows), BF16)],
        compiler_params=PARAMS,
        name="token_grad",
    )(inner_weight, shared_weight, step_weight_t, right, mine)
    token_got = lax.all_to_all(token_parts, "tp", 0, 0, tiled=True)

    def core_sum(blocks, ready):
        return pl.pallas_call(
            core_sum_kernel,
            in_specs=[smem()] + [whole(block.shape) for block in blocks] + [after()],
            out_specs=[whole((2, y_half, lanes))] * 4,
            out_shape=[sds((2, y_half, lanes), F32)] * 4,
            compiler_params=PARAMS,
            name="core_sum",
        )(edge, *blocks, ready)

    def exchange(up, down, dy, dz):
        return ctx_shift(up, dy, dz, 0), ctx_shift(down, -dy, -dz, 0)

    def pass_on(hold, below, above, ready):
        half = hold.shape[1]
        return pl.pallas_call(
            pass_on_kernel,
            in_specs=[whole(hold.shape)] * 3 + [after()],
            out_specs=[whole((half, lanes))] * 2,
            out_shape=[sds((half, lanes), F32)] * 2,
            compiler_params=PARAMS,
            name="pass_on",
        )(hold, below, above, ready)

    def next_ring(own, below, above, last_below, last_above, ready):
        return pl.pallas_call(
            next_ring_kernel,
            in_specs=[smem()]
            + [whole((2, y_half, lanes))] * 3
            + [whole((y_half, lanes))] * 2
            + [after()],
            out_specs=[whole((2, z_half, lanes))] * 4,
            out_shape=[sds((2, z_half, lanes), F32)] * 4,
            scratch_shapes=[pltpu.VMEM((RING, 2, z_half, lanes), F32)],
            compiler_params=PARAMS,
            name="next_ring",
        )(edge, own, below, above, last_below, last_above, ready)

    up_a, down_a, hold_a, own_a = core_sum((mine, got_a), token_parts)
    first_a = exchange(up_a, down_a, 1, 0)
    side_mine, side_other = pl.pallas_call(
        side_grad_kernel,
        grid=(RING,),
        in_specs=[
            smem(),
            whole((tp, shared_cols, length)),
            column,
            pl.BlockSpec((length, width // RING), lambda i: (0, i)),
            after(),
        ],
        out_specs=[row_block(LANES)] * 2,
        out_shape=[row_shape(LANES)] * 2,
        scratch_shapes=[pltpu.VMEM((length, 2 * LANES), BF16)],
        compiler_params=PARAMS,
        name="side_grad",
    )(edge, shared_parts, gstep, tokens, hold_a)
    side_got = ctx_shift(side_other, 0, 0, 1)
    up_b, down_b, hold_b, own_b = core_sum((mine_b, got_b, side_mine, side_got), hold_a)
    first_b = exchange(up_b, down_b, 1, 0)
    up_a, down_a = pass_on(hold_a, *first_a, hold_b)
    second_a = exchange(up_a, down_a, 1, 0)
    up_b, down_b = pass_on(hold_b, *first_b, up_a)
    second_b = exchange(up_b, down_b, 1, 0)
    up_a, down_a, hold_a, own_a = next_ring(own_a, *first_a, *second_a, up_b)
    first_a = exchange(up_a, down_a, 0, 1)
    up_b, down_b, hold_b, own_b = next_ring(own_b, *first_b, *second_b, hold_a)
    first_b = exchange(up_b, down_b, 0, 1)
    up_a, down_a = pass_on(hold_a, *first_a, hold_b)
    second_a = exchange(up_a, down_a, 0, 1)
    up_b, down_b = pass_on(hold_b, *first_b, up_a)
    second_b = exchange(up_b, down_b, 0, 1)
    grad_inner_weight, grad_shared_weight, grad_step_weight = pl.pallas_call(
        last_ring_kernel,
        out_shape=[
            sds((rows, inner), F32),
            sds((shared_cols, rows), F32),
            sds((heads, rows), F32),
        ],
        scratch_shapes=[pltpu.VMEM((LANES, LANES), F32)],
        compiler_params=PARAMS,
        name="last_ring",
    )(own_a, *first_a, *second_a, own_b, *first_b, *second_b)

    grad_tokens = pl.pallas_call(
        sum_kernel,
        out_shape=sds((cols, length), BF16),
        compiler_params=PARAMS,
        name="token_sum",
    )(token_got)
    return (
        mixed,
        grad_tokens.T,
        grad_inner_weight,
        grad_shared_weight.T,
        grad_step_weight.T,
    )


def solution(mesh):
    in_specs = (
        P("ctx", None),
        P(None, "tp"),
        P(),
        P(None, "tp"),
        P(None, "tp"),
        P(),
        P("tp"),
        P("tp"),
        P("tp"),
        P("ctx", "tp"),
    )
    out_specs = (P("ctx", "tp"), P("ctx", "tp"), P("ctx", "tp"), P("ctx", "tp"), P("ctx", "tp"))
    return jax.shard_map(body, mesh=mesh, in_specs=in_specs, out_specs=out_specs, check_vma=False)
```

```python
import functools

import jax
import jax.numpy as jnp
from jax import lax
from jax.experimental import pallas as pl
from jax.experimental.pallas import tpu as pltpu
from jax.sharding import PartitionSpec as P

P_SIZE = 64
N = 128
K = 4
LANES = 128
SLOT = 16
CORES = 2
RING = 4
F32 = jnp.float32
BF16 = jnp.bfloat16
NN = (((1,), (0,)), ((), ()))
NT = (((1,), (1,)), ((), ()))
TN = (((0,), (0,)), ((), ()))
BLOCK = 512
MIB = 1024 * 1024
PARAMS = pltpu.CompilerParams(vmem_limit_bytes=20 * MIB)
LARGE = pltpu.CompilerParams(vmem_limit_bytes=63 * MIB)
DMA = pltpu.SemaphoreType.DMA


def shifted(block, axis, distance):
    size = lax.axis_size(axis)
    return lax.ppermute(block, axis, [(i, (i + distance) % size) for i in range(size)])


def ctx_shift(block, dy, dz, dcore):
    def at(y, z, core):
        return (y % RING) * RING * CORES + (z % RING) * CORES + core % CORES

    route = [
        (at(y, z, core), at(y + dy, z + dz, core + dcore))
        for y in range(RING)
        for z in range(RING)
        for core in range(CORES)
    ]
    return lax.ppermute(block, "ctx", route)


def places():
    place = lax.axis_index("ctx")
    return place // (RING * CORES), place // CORES % RING, place % CORES


def dot1(a, b, dims):
    return lax.dot_general(a, b, dims, preferred_element_type=F32)


def split(a):
    high = a.astype(BF16)
    return high, (a - high.astype(F32)).astype(BF16)


def dot3(a, b, dims):
    ah, al = a
    bh, bl = b
    return dot1(ah, bh, dims) + (dot1(ah, bl, dims) + dot1(al, bh, dims))


def dot2(a, b, dims):
    return dot1(a[0], b, dims) + dot1(a[1], b, dims)


def halves(a, axis):
    return jnp.concatenate(split(a), axis)


def square(a):
    both = halves(a, 1)
    return jnp.concatenate([both, both], 0)


def full_dot(left, right):
    both = dot1(left, right, NN)
    return both[:, 0:LANES] + both[:, LANES:]


def tall_dot(left, right):
    both = dot1(left, right, NN)
    return (both[0:LANES, 0:LANES] + both[LANES:, LANES:]) + (
        both[0:LANES, LANES:] + both[LANES:, 0:LANES]
    )


def sigmoid(z):
    return 1.0 / (1.0 + jnp.exp(-z))


def of_tile(cols, k):
    lane = lax.broadcasted_iota(jnp.int32, (cols.shape[0], LANES), 1)
    left = jnp.broadcast_to(cols[:, 2 * k : 2 * k + 1], lane.shape)
    right = jnp.broadcast_to(cols[:, 2 * k + 1 : 2 * k + 2], lane.shape)
    return jnp.where(lane < P_SIZE, left, right)


def triangle_sum(a, dims):
    length = a.shape[0]
    row = lax.broadcasted_iota(jnp.int32, (length, length), 0)
    col = lax.broadcasted_iota(jnp.int32, (length, length), 1)
    reach = row >= col if dims == NN else row <= col
    ones = jnp.where(reach, 1.0, 0.0).astype(BF16)
    first = a.astype(BF16).astype(F32)
    second = (a - first).astype(BF16).astype(F32)
    third = (a - first - second).astype(BF16).astype(F32)
    packed = first + pltpu.roll(second, SLOT, 1) + pltpu.roll(third, 2 * SLOT, 1)
    sums = dot1(ones, packed.astype(BF16), NN)
    total = sums + pltpu.roll(sums, LANES - SLOT, 1) + pltpu.roll(sums, LANES - 2 * SLOT, 1)
    lane = lax.broadcasted_iota(jnp.int32, total.shape, 1)
    return jnp.where(lane < SLOT, total, 0.0)


def project_kernel(
    tiles, heads,
    tok_ref, rim_ref, wi_ref, ws_ref, wt_ref, ci_ref, cs_ref, bias_ref, rate_ref, skip_ref, cot_ref,
    z_ref, sp_ref, dt_ref, cum_ref, cumt_ref, keep_ref, send_ref, par_ref,
    lhs, rhs, acc, cot, tok_sem, wi_sem, ws_sem, cot_sem,
):
    length = tok_ref.shape[0]
    head_rows = lhs.shape[1] - length
    inner = wi_ref.shape[1]
    total = inner + ws_ref.shape[1]
    par_ref[...] = jnp.zeros_like(par_ref)
    for i, ref in enumerate((bias_ref, rate_ref, skip_ref)):
        par_ref[i : i + 1, 0:heads] = ref[...]
    steps = tok_ref.shape[1] // BLOCK
    copies = []
    for step in range(steps):
        at = slice(step * BLOCK, (step + 1) * BLOCK)
        copies.append([
            pltpu.make_async_copy(
                tok_ref.at[:, at], lhs.at[step, head_rows:], tok_sem.at[step]
            ),
            pltpu.make_async_copy(wi_ref.at[at], rhs.at[step, :, 0:inner], wi_sem.at[step]),
            pltpu.make_async_copy(ws_ref.at[at], rhs.at[step, :, inner:total], ws_sem.at[step]),
        ])
    last_copy = pltpu.make_async_copy(cot_ref, cot, cot_sem)
    for copy in copies[0] + copies[1]:
        copy.start()
    keep = jnp.where(lax.axis_index("ctx") == 0, 0.0, 1.0)
    blank = jnp.zeros((LANES - heads, BLOCK), F32)
    for step in range(steps):
        at = slice(step * BLOCK, (step + 1) * BLOCK)
        rim = rim_ref[:, at] * keep
        lhs[step, 0:head_rows, :] = jnp.concatenate([jnp.zeros_like(rim), rim], 0).astype(BF16)
        weights = jnp.concatenate([wt_ref[:, at].astype(F32), blank], 0)
        rhs[step, :, total:] = jnp.transpose(weights).astype(BF16)
        for copy in copies[step]:
            copy.wait()
        for copy in copies[step + 2] if step + 2 < steps else [last_copy] * (step + 2 == steps):
            copy.start()
        product = dot1(lhs[step], rhs[step], NN)
        if step == 0:
            acc[...] = product
        else:
            acc[...] += product
    last_copy.wait()
    start = head_rows - (K - 1)
    sp = acc[head_rows:, total:] + par_ref[0:1, :]
    sp_ref[...] = sp
    dt = jnp.maximum(sp, 0.0) + jnp.log1p(jnp.exp(-jnp.abs(sp)))
    dt_ref[...] = dt
    cum = triangle_sum(-par_ref[1:2, :] * dt, NN)
    cum_ref[...] = cum
    cumt_ref[...] = jnp.transpose(cum)[0:SLOT, :]
    last = cum[length - 1 :, :]
    write_weight = dt * jnp.exp(last - cum)
    read_weight = jnp.exp(cum)

    def conv(at, taps, k):
        lo = k * LANES
        out = taps[0:1, lo : lo + LANES] * acc[start : start + length, at : at + LANES]
        for j in range(1, K):
            out += taps[j : j + 1, lo : lo + LANES] * acc[
                start + j : start + j + length, at : at + LANES
            ]
        return out

    zb = conv(inner, cs_ref, 0)
    z_ref[:, inner : inner + LANES] = zb
    zc = conv(inner + LANES, cs_ref, 1)
    z_ref[:, inner + LANES :] = zc
    b_rows = halves(jnp.transpose(zb * sigmoid(zb)), 0)
    c_rows = halves(jnp.transpose(zc * sigmoid(zc)), 0)
    groups = N // 8
    forward = places()[2] == 0
    blank = jnp.zeros((groups, 8, LANES), F32)
    keep_ref[:, 8 * tiles :, :] = blank
    send_ref[:, 8 * tiles :, :] = blank
    for k in range(tiles):
        lo = k * LANES
        rows = slice(8 * k, 8 * k + 8)
        z = conv(lo, ci_ref, k)
        z_ref[:, lo : lo + LANES] = z
        x = z * sigmoid(z) * of_tile(write_weight, k)
        state = tall_dot(b_rows, halves(x, 1))
        g = cot[:, lo : lo + LANES].astype(F32) * of_tile(read_weight, k)
        grad = tall_dot(c_rows, halves(g, 1))
        keep_ref[:, rows, :] = jnp.where(forward, state, grad).reshape(groups, 8, LANES)
        send_ref[:, rows, :] = jnp.where(forward, grad, state).reshape(groups, 8, LANES)
        row = jnp.broadcast_to(of_tile(last, k)[None], (groups, 1, LANES))
        keep_ref[:, 8 * tiles + k : 8 * tiles + k + 1, :] = row
        send_ref[:, 8 * tiles + k : 8 * tiles + k + 1, :] = row


def decay_rows(tiles, block):
    decay = jnp.exp(block[..., 8 * tiles :, :])
    shape = block.shape[:-2] + (8, LANES)
    return jnp.concatenate(
        [jnp.broadcast_to(decay[..., k : k + 1, :], shape) for k in range(tiles)], -2
    )


def chip_kernel(tiles, keep_ref, got_ref, out_ref):
    rows = 8 * tiles
    for i in range(keep_ref.shape[0]):
        keep = keep_ref[i]
        got = got_ref[i]
        out_ref[i, 0:rows, :] = got[0:rows, :] + decay_rows(tiles, got) * keep[0:rows, :]
        out_ref[i, rows:, :] = got[rows:, :] + keep[rows:, :]


def onward_kernel(tiles, keep_ref, arrived_ref, after_ref, out_ref):
    rows = 8 * tiles
    for i in range(keep_ref.shape[0]):
        keep = keep_ref[i]
        out_ref[i] = keep[0:rows, :] + decay_rows(tiles, keep) * arrived_ref[i]


def ctx_scan_kernel(tiles, in_ref, after_ref, out_ref):
    count = in_ref.shape[0]
    rows = 8 * tiles
    backward = places()[2] == 1

    def turn(i, held):
        at = jnp.where(backward, count - 1 - i, i)
        out_ref[at] = held
        got = in_ref[at]
        return got[0:rows, :] + decay_rows(tiles, got) * held

    lax.fori_loop(0, count, turn, jnp.zeros((rows, LANES), F32), unroll=4)


def local_kernel(
    tiles,
    z_ref, dt_ref, cum_ref, cumt_ref, cot_ref,
    y_ref, u_ref, db_ref, dc_ref,
    scores, grad_scores,
):
    length = z_ref.shape[0]
    half = length // 2
    inner = tiles * LANES
    chunks = (slice(0, half), slice(half, length))
    early, late = chunks
    zb = z_ref[:, inner : inner + LANES]
    zc = z_ref[:, inner + LANES :]
    b = zb * sigmoid(zb)
    c = zc * sigmoid(zc)
    b_wide = halves(b, 1)
    c_wide = halves(c, 1)
    b_rows = halves(jnp.transpose(b[early]), 0)
    c_rows = halves(jnp.transpose(c[late]), 0)
    row = lax.broadcasted_iota(jnp.int32, (half, half), 0)
    col = lax.broadcasted_iota(jnp.int32, (half, half), 1)
    lane = lax.broadcasted_iota(jnp.int32, (length, LANES), 1)

    def pieces(wide, at):
        return wide[at, 0:LANES], wide[at, LANES:]

    for chunk, at in enumerate(chunks):
        full = dot3(pieces(c_wide, at), pieces(b_wide, at), NT)
        scores[chunk] = jnp.where(row >= col, full, 0.0)
    grad_scores[...] = jnp.zeros_like(grad_scores)
    db_ref[...] = jnp.zeros_like(db_ref)
    dc_ref[...] = jnp.zeros_like(dc_ref)

    def one_tile(tile, carry):
        here = pl.ds(pl.multiple_of(tile * LANES, LANES), LANES)
        turn = (LANES - 2 * tile) % LANES
        dt_cols = pltpu.roll(dt_ref[...], turn, 1)
        cum_cols = pltpu.roll(cum_ref[...], turn, 1)
        dt = jnp.where(lane < P_SIZE, dt_cols[:, 0:1], dt_cols[:, 1:2])
        cum = jnp.where(lane < P_SIZE, cum_cols[:, 0:1], cum_cols[:, 1:2])
        z = z_ref[:, here]
        x = z * sigmoid(z) * dt
        g = cot_ref[:, here]
        xh, xl = split(x)
        gt = jnp.transpose(g.astype(F32)).astype(BF16)
        for chunk, at in enumerate(chunks):
            ys = []
            us = []
            for head in range(2):
                of = slice(head * P_SIZE, (head + 1) * P_SIZE)
                row_logs = cumt_ref[pl.ds(2 * tile + head, 1), at]
                decays = jnp.exp(jnp.minimum(cum_cols[at, head : head + 1] - row_logs, 0.0))
                wh, wl = split(scores[chunk] * decays)
                x_pair = jnp.concatenate([xh[at, of], xl[at, of]], 1)
                y_pair = dot1(wh, x_pair, NN) + dot1(wl, x_pair, NN)
                ys.append(y_pair[:, 0:P_SIZE] + y_pair[:, P_SIZE:])
                us.append(dot1(gt[of, at], wh, NN) + dot1(gt[of, at], wl, NN))
                g_pair = jnp.concatenate([g[at, of], g[at, of]], 1)
                grad_scores[chunk] += dot1(g_pair, x_pair, NT) * decays
            y_ref[at, here] = jnp.concatenate(ys, 1)
            u_ref[at, here] = jnp.transpose(jnp.concatenate(us, 0))
        middle = cum[half - 1 : half, :]
        down = jnp.exp(middle - cum[early])
        up = jnp.exp(cum[late] - middle)
        xd = halves(x[early] * down, 1)
        gd = halves(g[late].astype(F32) * up, 1)
        state = tall_dot(b_rows, xd)
        grad = tall_dot(c_rows, gd)
        y_ref[late, here] += up * full_dot(c_wide[late], square(state))
        u_ref[early, here] += down * full_dot(b_wide[early], square(grad))
        dc_ref[late, :] += full_dot(gd, square(jnp.transpose(state)))
        db_ref[early, :] += full_dot(xd, square(jnp.transpose(grad)))
        return carry

    lax.fori_loop(0, tiles, one_tile, 0)
    for chunk, at in enumerate(chunks):
        gs = split(jnp.where(row >= col, grad_scores[chunk], 0.0))
        dc_ref[at, :] += dot3(gs, pieces(b_wide, at), NN)
        db_ref[at, :] += dot3(gs, pieces(c_wide, at), TN)


def join_kernel(
    tiles,
    z_ref, sp_ref, dt_ref, cum_ref, par_ref, cot_ref, y_ref, u_ref,
    db_ref, dc_ref, keep_ref, send_ref, arrived_ref, other_ref,
    mixed_ref, dinner_ref, dshared_ref, gstep_ref, rim_ref,
    z_in, cot_in, y_in, u_in, state_in, z_sem, cot_sem, y_sem, u_sem, state_sem,
):
    length = z_ref.shape[0]
    inner = tiles * LANES
    states = [
        pltpu.make_async_copy(ref.at[:, 0 : 8 * tiles], state_in.at[i], state_sem.at[i])
        for i, ref in enumerate((arrived_ref, keep_ref, send_ref, other_ref))
    ]
    sides = pltpu.make_async_copy(
        z_ref.at[:, inner:], z_in.at[:, inner:], z_sem.at[tiles]
    )
    loads = []
    for k in range(tiles):
        at = slice(k * LANES, (k + 1) * LANES)
        loads.append([
            pltpu.make_async_copy(ref.at[:, at], held.at[:, at], sem.at[k])
            for ref, held, sem in (
                (z_ref, z_in, z_sem), (cot_ref, cot_in, cot_sem),
                (y_ref, y_in, y_sem), (u_ref, u_in, u_sem),
            )
        ])
    for copy in [sides, *states, *loads[0], *loads[1]]:
        copy.start()
    forward = places()[2] == 0
    dt = dt_ref[...]
    cum = cum_ref[...]
    last = cum[length - 1 :, :]
    read_weight = jnp.exp(cum)
    tail_weight = jnp.exp(last - cum)
    total_decay = jnp.exp(last)
    sides.wait()
    zb = z_in[:, inner : inner + LANES]
    zc = z_in[:, inner + LANES :]
    b_wide = halves(zb * sigmoid(zb), 1)
    c_wide = halves(zc * sigmoid(zc), 1)
    reads = jnp.zeros((length, LANES), F32)
    writes = jnp.zeros((length, LANES), F32)
    ends = jnp.zeros((8, LANES), F32)
    db = db_ref[...]
    dc = dc_ref[...]
    lane = lax.broadcasted_iota(jnp.int32, (LANES, LANES), 1)
    row = lax.broadcasted_iota(jnp.int32, (LANES, LANES), 0)
    for copy in states:
        copy.wait()
    for k in range(tiles):
        for copy in loads[k]:
            copy.wait()
        for copy in loads[k + 2] if k + 2 < tiles else []:
            copy.start()
        at = slice(k * LANES, (k + 1) * LANES)
        rows = slice(8 * k, 8 * k + 8)
        gather = jnp.where(lane == 2 * k + row // P_SIZE, 1.0, 0.0).astype(BF16)
        gather = jnp.concatenate([gather, gather], 0)
        arrived = state_in[0, :, rows, :].reshape(N, LANES)
        other = state_in[3, :, rows, :].reshape(N, LANES)
        keep = state_in[1, :, rows, :].reshape(N, LANES)
        send = state_in[2, :, rows, :].reshape(N, LANES)
        state = jnp.where(forward, arrived, other)
        grad = jnp.where(forward, other, arrived)
        own = jnp.where(forward, keep, send)
        z = z_in[:, at]
        s = sigmoid(z)
        v = z * s
        g = cot_in[:, at].astype(F32)
        read_k = of_tile(read_weight, k)
        tail_k = of_tile(tail_weight, k)
        dt_k = of_tile(dt, k)
        skip = of_tile(par_ref[...], k)[2:3, :]
        y = y_in[:, at] + read_k * full_dot(c_wide, square(state))
        u = u_in[:, at] + tail_k * full_dot(b_wide, square(grad))
        mixed_ref[:, at] = (y + skip * v).astype(BF16)
        dv = dt_k * u + skip * g
        dinner_ref[:, at] = dv * (s * (1.0 + z * (1.0 - s)))
        reads += dot1(halves(g * y, 1), gather, NN)
        writes += dot1(halves(v * u, 1), gather, NN)
        dc += full_dot(halves(g * read_k, 1), square(jnp.transpose(state)))
        db += full_dot(halves(v * dt_k * tail_k, 1), square(jnp.transpose(grad)))
        end = jnp.sum(grad * (own + of_tile(total_decay, k) * state), 0, keepdims=True)
        ends += dot1(halves(jnp.broadcast_to(end, (8, LANES)), 1), gather, NN)
    sb = sigmoid(zb)
    sc = sigmoid(zc)
    dshared_ref[:, 0:LANES] = db * (sb * (1.0 + zb * (1.0 - sb)))
    dshared_ref[:, LANES:] = dc * (sc * (1.0 + zc * (1.0 - sc)))
    rim_ref[:, 0:inner] = dinner_ref[0:8, :]
    rim_ref[:, inner:] = dshared_ref[0:8, :]
    grad_logs = triangle_sum(reads - dt * writes, TN) + ends[0:1]
    grad_dt = writes - par_ref[1:2, :] * grad_logs
    gstep_ref[...] = grad_dt * sigmoid(sp_ref[...])


def conv_back_kernel(
    dinner_ref, dshared_ref, rim_ref, ci_ref, cs_ref, gstep_ref,
    gi_ref, gst_ref, right_ref, wide_i, wide_s, gi, gst, right, gi_sem, gst_sem, right_sem,
):
    length, inner = dinner_ref.shape
    shared = dshared_ref.shape[1]
    rim = rim_ref[...] * jnp.where(lax.axis_index("ctx") < lax.axis_size("ctx") - 1, 1.0, 0.0)
    wide_s[0:length, :] = dshared_ref[...]
    wide_s[length:, :] = rim[:, inner:]

    def back(wide, taps, k):
        at = slice(k * LANES, (k + 1) * LANES)
        out = taps[K - 1 : K, at] * wide[0:length, at]
        for j in range(1, K):
            out += taps[K - 1 - j : K - j, at] * wide[j : j + length, at]
        return out

    for k in range(shared // LANES):
        at = slice(k * LANES, (k + 1) * LANES)
        grad = jnp.transpose(back(wide_s, cs_ref, k))
        gst[at, :] = grad
        high, low = split(grad)
        right[inner + k * LANES : inner + (k + 1) * LANES, :] = high
        right[inner + shared + k * LANES : inner + shared + (k + 1) * LANES, :] = low
    gst_copy = pltpu.make_async_copy(gst, gst_ref, gst_sem)
    gst_copy.start()
    high, low = split(jnp.transpose(gstep_ref[...])[0:SLOT, :])
    right[inner + 2 * shared : inner + 2 * shared + SLOT, :] = high
    right[inner + 2 * shared + SLOT :, :] = low
    wide_i[0:length, :] = dinner_ref[...]
    wide_i[length:, :] = rim[:, 0:inner]
    for k in range(inner // LANES):
        at = slice(k * LANES, (k + 1) * LANES)
        grad = back(wide_i, ci_ref, k)
        gi[:, at] = grad.astype(BF16)
        right[at, :] = jnp.transpose(grad).astype(BF16)
    gi_copy = pltpu.make_async_copy(gi, gi_ref, gi_sem)
    gi_copy.start()
    right_copy = pltpu.make_async_copy(right, right_ref, right_sem)
    right_copy.start()
    gst_copy.wait()
    gi_copy.wait()
    right_copy.wait()


def prepare_kernel(
    heads, tok_ref, wi_ref, ws_ref, wt_ref, after_ref, tok_t_ref, left_ref, mark_ref
):
    inner = wi_ref.shape[1]
    shared = ws_ref.shape[1]
    end = inner + 2 * shared
    mark_ref[...] = jnp.zeros_like(mark_ref)

    def turn(step, carry):
        at = pl.ds(pl.multiple_of(step * BLOCK, BLOCK), BLOCK)
        tok_t_ref[at, :] = jnp.transpose(tok_ref[:, at].astype(F32)).astype(BF16)
        return carry

    lax.fori_loop(0, tok_ref.shape[1] // BLOCK, turn, 0)
    left_ref[:, 0:inner] = wi_ref[...]
    left_ref[:, inner : inner + shared] = ws_ref[...]
    left_ref[:, inner + shared : end] = ws_ref[...]
    blank = jnp.zeros((SLOT - heads, left_ref.shape[0]), F32)
    step = jnp.concatenate([wt_ref[...].astype(F32), blank], 0)
    left_ref[:, end:] = jnp.transpose(jnp.concatenate([step, step], 0)).astype(BF16)


def token_grad_kernel(
    left_ref, right_ref, out_ref, mark_ref, left, right, out, left_sem, right_sem, out_sem
):
    mark_ref[...] = jnp.zeros_like(mark_ref)
    count, cols, length = out_ref.shape
    per = count // RING
    slab = per * cols
    right_copy = pltpu.make_async_copy(right_ref, right, right_sem)
    right_copy.start()
    loads = [
        pltpu.make_async_copy(left_ref.at[pl.ds(i * slab, slab)], left.at[i], left_sem.at[i])
        for i in range(RING)
    ]
    for copy in loads[0:2]:
        copy.start()
    right_copy.wait()
    stores = []
    for i in range(RING):
        loads[i].wait()
        if i + 2 < RING:
            loads[i + 2].start()
        out[i] = dot1(left[i], right[...], NN).reshape(per, cols, length)
        copy = pltpu.make_async_copy(out.at[i], out_ref.at[pl.ds(i * per, per)], out_sem.at[i])
        copy.start()
        stores.append(copy)
    for copy in stores:
        copy.wait()


def put_rows(y, product, mine_ref, other_ref):
    rows = mine_ref.shape[1] * mine_ref.shape[2] // RING
    parts = product.reshape(RING, CORES, rows, product.shape[1])

    def put(first, second):
        for z in range(RING):
            at = z * rows % mine_ref.shape[2]
            first[y, z * rows // mine_ref.shape[2], at : at + rows, :] = parts[z, 0]
            second[y, z * rows // mine_ref.shape[2], at : at + rows, :] = parts[z, 1]

    @pl.when(places()[2] == 0)
    def _():
        put(mine_ref, other_ref)

    @pl.when(places()[2] == 1)
    def _():
        put(other_ref, mine_ref)


def weight_grad_kernel(tok_ref, gi_ref, after_ref, mine_ref, other_ref):
    slab = tok_ref.shape[0] // RING
    right = gi_ref[...]

    def turn(y, carry):
        at = pl.ds(pl.multiple_of(y * slab, slab), slab)
        put_rows(y, dot1(tok_ref[at, :], right, NN), mine_ref, other_ref)
        return carry

    lax.fori_loop(0, RING, turn, 0)


def side_grad_kernel(parts_ref, gstep_ref, tok_ref, mine_ref, other_ref):
    slab = tok_ref.shape[0] // RING
    shared_cols = parts_ref.shape[1]
    total = parts_ref[0]
    for i in range(1, parts_ref.shape[0]):
        total += parts_ref[i]
    blank = jnp.zeros((LANES - shared_cols, total.shape[1]), F32)
    cols = jnp.transpose(jnp.concatenate([total, blank], 0))
    right = halves(cols + pltpu.roll(gstep_ref[...], shared_cols, 1), 1)

    def turn(y, carry):
        at = pl.ds(pl.multiple_of(y * slab, slab), slab)
        both = dot1(tok_ref[at, :], right, NN)
        put_rows(y, both[:, 0:LANES] + both[:, LANES:], mine_ref, other_ref)
        return carry

    lax.fori_loop(0, RING, turn, 0)


def ring_parts(place, part, up_ref, down_ref, hold_ref, own_ref):
    above, facing, below = [(place + i) % RING for i in (1, 2, 3)]
    up_ref[0] = part(facing, 0)
    up_ref[1] = part(above, 1)
    down_ref[0] = part(facing, 1)
    down_ref[1] = part(below, 0)
    hold_ref[0] = part(above, 0)
    hold_ref[1] = part(below, 1)
    own_ref[0] = part(place, 0)
    own_ref[1] = part(place, 1)


def core_sum_kernel(lanes, *refs):
    blocks = refs[:-4]

    def part(target, half):
        sums = [
            blocks[i][target, half, :, at] + blocks[i + 1][target, half, :, at]
            for i, at in zip(range(0, len(blocks), 2), lanes)
        ]
        return jnp.concatenate(sums, 1) if len(sums) > 1 else sums[0]

    ring_parts(places()[0], part, *refs[-4:])


def pass_on_kernel(hold_ref, from_below_ref, from_above_ref, up_ref, down_ref):
    up_ref[...] = hold_ref[0] + from_below_ref[0]
    down_ref[...] = hold_ref[1] + from_above_ref[0]


def ring_sum(own_ref, from_below_ref, from_above_ref, last_below_ref, last_above_ref):
    first = own_ref[0] + from_above_ref[1] + last_below_ref[...]
    second = own_ref[1] + from_below_ref[1] + last_above_ref[...]
    return first, second


def next_ring_kernel(
    own_in, from_below_ref, from_above_ref, last_below_ref, last_above_ref,
    up_ref, down_ref, hold_ref, own_ref, sums,
):
    first, second = ring_sum(
        own_in, from_below_ref, from_above_ref, last_below_ref, last_above_ref
    )
    half = RING // 2
    shape = (half,) + sums.shape[1:]
    sums[0:half] = first.reshape(shape)
    sums[half:] = second.reshape(shape)

    def part(target, which):
        return sums[target, which]

    ring_parts(places()[1], part, up_ref, down_ref, hold_ref, own_ref)


def last_ring_kernel(*refs):
    inner_ref, shared_ref, step_ref, side = refs[11:]
    half = inner_ref.shape[0] // 2
    at = (slice(0, half), slice(half, 2 * half))
    lanes = refs[0].shape[2]
    shared_cols = shared_ref.shape[0]
    rest = inner_ref.shape[1] - lanes
    side[2 * half :, :] = jnp.zeros((side.shape[0] - 2 * half, LANES), F32)
    for rows, part in zip(at, ring_sum(*refs[0:5])):
        inner_ref[rows, 0:lanes] = part
    for rows, part in zip(at, ring_sum(*refs[5:10])):
        inner_ref[rows, lanes:] = part[:, 0:rest]
        side[rows, :] = part[:, rest:]
    flat = jnp.transpose(side[...])
    shared_ref[...] = flat[0:shared_cols, 0 : 2 * half]
    step_ref[...] = flat[shared_cols : shared_cols + step_ref.shape[0], 0 : 2 * half]


def sum_kernel(parts_ref, out_ref, mark_ref, parts, sem):
    mark_ref[...] = jnp.zeros_like(mark_ref)
    rows = out_ref.shape[0] // RING
    copies = []
    for i in range(RING):
        copy = pltpu.make_async_copy(
            parts_ref.at[:, pl.ds(i * rows, rows)], parts.at[i], sem.at[i]
        )
        copy.start()
        copies.append(copy)
    for i in range(RING):
        copies[i].wait()
        total = parts[i, 0]
        for j in range(1, parts_ref.shape[0]):
            total += parts[i, j]
        out_ref[i * rows : (i + 1) * rows, :] = total.astype(out_ref.dtype)


def whole(shape):
    return pl.BlockSpec(shape, lambda *_: (0,) * len(shape))


def after():
    return pl.BlockSpec(memory_space=pltpu.HBM)


def far():
    return pl.BlockSpec(memory_space=pltpu.HBM)


def body(
    tokens,
    inner_weight,
    shared_weight,
    step_weight,
    conv_inner,
    conv_shared,
    step_bias,
    decay_rate,
    skip_gain,
    cotangent,
):
    length, width = tokens.shape
    inner = inner_weight.shape[1]
    shared = shared_weight.shape[1]
    heads = step_weight.shape[1]
    tiles = inner // LANES
    ctx = lax.axis_size("ctx")
    tp = lax.axis_size("tp")
    chips = ctx // CORES
    same_core = [[CORES * chip + i for chip in range(chips)] for i in range(CORES)]
    sds = jax.ShapeDtypeStruct
    step_weight_t = step_weight.T

    rim = shifted(tokens[length - 8 :].astype(F32), "ctx", 1)

    total = inner + shared
    pay_rows = 8 * tiles + 8
    z, sp, dt, cum, cum_t, keep, send, params = pl.pallas_call(
        functools.partial(project_kernel, tiles, heads),
        in_specs=[
            far(),
            whole((8, width)),
            far(),
            far(),
            whole((heads, width)),
            whole((K, inner)),
            whole((K, shared)),
            whole((1, heads)),
            whole((1, heads)),
            whole((1, heads)),
            far(),
        ],
        out_specs=[
            whole((length, total)),
            whole((length, LANES)),
            whole((length, LANES)),
            whole((length, LANES)),
            whole((SLOT, length)),
            whole((chips, pay_rows, LANES)),
            whole((chips, pay_rows, LANES)),
            whole((8, LANES)),
        ],
        out_shape=[
            sds((length, total), F32),
            sds((length, LANES), F32),
            sds((length, LANES), F32),
            sds((length, LANES), F32),
            sds((SLOT, length), F32),
            sds((chips, pay_rows, LANES), F32),
            sds((chips, pay_rows, LANES), F32),
            sds((8, LANES), F32),
        ],
        scratch_shapes=[
            pltpu.VMEM((width // BLOCK, length + 16, BLOCK), BF16),
            pltpu.VMEM((width // BLOCK, BLOCK, total + LANES), BF16),
            pltpu.VMEM((length + 16, total + LANES), F32),
            pltpu.VMEM((length, inner), BF16),
            DMA((width // BLOCK,)),
            DMA((width // BLOCK,)),
            DMA((width // BLOCK,)),
            DMA,
        ],
        compiler_params=LARGE,
        name="project",
    )(
        tokens, rim, inner_weight, shared_weight, step_weight_t,
        conv_inner, conv_shared, step_bias[None], decay_rate[None], skip_gain[None], cotangent,
    )

    got = ctx_shift(send, 0, 0, 1)
    chip_state = pl.pallas_call(
        functools.partial(chip_kernel, tiles),
        out_shape=sds((chips, pay_rows, LANES), F32),
        compiler_params=LARGE,
        name="chip_state",
    )(keep, got)
    by_rows = lax.all_to_all(
        chip_state, "ctx", 0, 0, axis_index_groups=same_core, tiled=True
    )

    y, u, db, dc = pl.pallas_call(
        functools.partial(local_kernel, tiles),
        out_shape=[
            sds((length, inner), F32),
            sds((length, inner), F32),
            sds((length, LANES), F32),
            sds((length, LANES), F32),
        ],
        scratch_shapes=[
            pltpu.VMEM((2, length // 2, length // 2), F32),
            pltpu.VMEM((2, length // 2, length // 2), F32),
        ],
        compiler_params=LARGE,
        cost_estimate=pl.CostEstimate(
            flops=10 * length * length * inner, bytes_accessed=8_000_000, transcendentals=0
        ),
        name="local",
    )(z, dt, cum, cum_t, cotangent)

    scanned = pl.pallas_call(
        functools.partial(ctx_scan_kernel, tiles),
        in_specs=[whole((chips, pay_rows, LANES)), after()],
        out_specs=whole((chips, 8 * tiles, LANES)),
        out_shape=sds((chips, 8 * tiles, LANES), F32),
        compiler_params=LARGE,
        name="ctx_scan",
    )(by_rows, dc)
    arrived = lax.all_to_all(scanned, "ctx", 0, 0, axis_index_groups=same_core, tiled=True)
    right_rows = inner + 2 * shared + 2 * SLOT
    tok_t, left, mark = pl.pallas_call(
        functools.partial(prepare_kernel, heads),
        in_specs=[
            whole((length, width)),
            whole((width, inner)),
            whole((width, shared)),
            whole((heads, width)),
            after(),
        ],
        out_specs=[whole((width, length)), whole((width, right_rows)), whole((8, LANES))],
        out_shape=[
            sds((width, length), BF16),
            sds((width, right_rows), BF16),
            sds((8, LANES), F32),
        ],
        compiler_params=LARGE,
        name="prepare",
    )(tokens, inner_weight, shared_weight, step_weight_t, scanned)
    onward = pl.pallas_call(
        functools.partial(onward_kernel, tiles),
        in_specs=[
            whole((chips, pay_rows, LANES)), whole((chips, 8 * tiles, LANES)), after(),
        ],
        out_specs=whole((chips, 8 * tiles, LANES)),
        out_shape=sds((chips, 8 * tiles, LANES), F32),
        compiler_params=LARGE,
        name="onward",
    )(keep, arrived, mark)
    other = ctx_shift(onward, 0, 0, 1)

    column = whole((length, LANES))
    mixed, dinner, dshared, gstep, rim_out = pl.pallas_call(
        functools.partial(join_kernel, tiles),
        in_specs=[
            far(),
            column,
            column,
            column,
            whole((8, LANES)),
            far(),
            far(),
            far(),
            column,
            column,
            far(),
            far(),
            far(),
            far(),
        ],
        out_specs=[
            whole((length, inner)), whole((length, inner)), whole((length, shared)), column,
            whole((8, total)),
        ],
        out_shape=[
            sds((length, inner), BF16),
            sds((length, inner), F32),
            sds((length, shared), F32),
            sds((length, LANES), F32),
            sds((8, total), F32),
        ],
        scratch_shapes=[
            pltpu.VMEM((length, total), F32),
            pltpu.VMEM((length, inner), BF16),
            pltpu.VMEM((length, inner), F32),
            pltpu.VMEM((length, inner), F32),
            pltpu.VMEM((4, chips, 8 * tiles, LANES), F32),
            DMA((tiles + 1,)),
            DMA((tiles,)),
            DMA((tiles,)),
            DMA((tiles,)),
            DMA((4,)),
        ],
        compiler_params=LARGE,
        name="join",
    )(
        z, sp, dt, cum, params, cotangent, y, u, db, dc,
        keep, send, arrived, other,
    )

    rim_back = shifted(rim_out, "ctx", -1)
    grad_inner, grad_shared_t, right = pl.pallas_call(
        conv_back_kernel,
        in_specs=[
            whole((length, inner)),
            whole((length, shared)),
            whole((8, total)),
            whole((K, inner)),
            whole((K, shared)),
            column,
        ],
        out_specs=[far(), far(), far()],
        out_shape=[
            sds((length, inner), BF16),
            sds((shared, length), F32),
            sds((right_rows, length), BF16),
        ],
        scratch_shapes=[
            pltpu.VMEM((length + 8, inner), F32),
            pltpu.VMEM((length + 8, shared), F32),
            pltpu.VMEM((length, inner), BF16),
            pltpu.VMEM((shared, length), F32),
            pltpu.VMEM((right_rows, length), BF16),
            DMA,
            DMA,
            DMA,
        ],
        compiler_params=LARGE,
        name="conv_back",
    )(dinner, dshared, rim_back, conv_inner, conv_shared, gstep)

    shared_cols = shared // tp
    shared_parts = lax.all_to_all(
        grad_shared_t.reshape(tp, shared_cols, length), "tp", 0, 0, tiled=True
    )

    cols = width // tp
    per = tp // RING
    token_parts, token_mark = pl.pallas_call(
        token_grad_kernel,
        in_specs=[far(), far()],
        out_specs=[far(), whole((8, LANES))],
        out_shape=[sds((tp, cols, length), F32), sds((8, LANES), F32)],
        scratch_shapes=[
            pltpu.VMEM((RING, per * cols, right_rows), BF16),
            pltpu.VMEM((right_rows, length), BF16),
            pltpu.VMEM((RING, per, cols, length), F32),
            DMA((RING,)),
            DMA,
            DMA((RING,)),
        ],
        compiler_params=LARGE,
        name="token_grad",
    )(left, right)
    token_got = lax.all_to_all(token_parts, "tp", 0, 0, tiled=True)

    rows = width // ctx
    y_half = RING * rows // 2
    z_half = rows // 2
    lanes = (inner + LANES) // 2

    def row_block(wide):
        return whole((RING, 2, y_half, wide))

    def row_shape(wide):
        return sds((RING, 2, y_half, wide), F32)

    mine, core_other = pl.pallas_call(
        weight_grad_kernel,
        in_specs=[whole((width, length)), whole((length, inner)), after()],
        out_specs=[row_block(inner)] * 2,
        out_shape=[row_shape(inner)] * 2,
        compiler_params=PARAMS,
        name="weight_grad",
    )(tok_t, grad_inner, token_mark)
    core_got = ctx_shift(core_other, 0, 0, 1)

    def core_sum(blocks, spans):
        return pl.pallas_call(
            functools.partial(core_sum_kernel, spans),
            in_specs=[whole(block.shape) for block in blocks],
            out_specs=[whole((2, y_half, lanes))] * 4,
            out_shape=[sds((2, y_half, lanes), F32)] * 4,
            compiler_params=PARAMS,
            name="core_sum",
        )(*blocks)

    def exchange(up, down, dy, dz):
        return ctx_shift(up, dy, dz, 0), ctx_shift(down, -dy, -dz, 0)

    def pass_on(hold, below, above):
        half = hold.shape[1]
        return pl.pallas_call(
            pass_on_kernel,
            in_specs=[whole(hold.shape)] * 3,
            out_specs=[whole((half, lanes))] * 2,
            out_shape=[sds((half, lanes), F32)] * 2,
            compiler_params=PARAMS,
            name="pass_on",
        )(hold, below, above)

    def next_ring(own, below, above, last_below, last_above):
        return pl.pallas_call(
            next_ring_kernel,
            in_specs=[whole((2, y_half, lanes))] * 3
            + [whole((y_half, lanes))] * 2,
            out_specs=[whole((2, z_half, lanes))] * 4,
            out_shape=[sds((2, z_half, lanes), F32)] * 4,
            scratch_shapes=[pltpu.VMEM((RING, 2, z_half, lanes), F32)],
            compiler_params=PARAMS,
            name="next_ring",
        )(own, below, above, last_below, last_above)

    side_mine, side_other = pl.pallas_call(
        side_grad_kernel,
        in_specs=[
            whole((tp, shared_cols, length)),
            column,
            whole((width, length)),
        ],
        out_specs=[row_block(LANES)] * 2,
        out_shape=[row_shape(LANES)] * 2,
        compiler_params=PARAMS,
        name="side_grad",
    )(shared_parts, gstep, tok_t)
    side_got = ctx_shift(side_other, 0, 0, 1)
    up_a, down_a, hold_a, own_a = core_sum((mine, core_got), [slice(0, lanes)])
    first_a = exchange(up_a, down_a, 1, 0)
    up_b, down_b, hold_b, own_b = core_sum(
        (mine, core_got, side_mine, side_got), [slice(lanes, inner), slice(0, LANES)]
    )
    first_b = exchange(up_b, down_b, 1, 0)
    up_a, down_a = pass_on(hold_a, *first_a)
    second_a = exchange(up_a, down_a, 1, 0)
    up_b, down_b = pass_on(hold_b, *first_b)
    second_b = exchange(up_b, down_b, 1, 0)
    up_a, down_a, hold_a, own_a = next_ring(own_a, *first_a, *second_a)
    first_a = exchange(up_a, down_a, 0, 1)
    up_b, down_b, hold_b, own_b = next_ring(own_b, *first_b, *second_b)
    first_b = exchange(up_b, down_b, 0, 1)
    up_a, down_a = pass_on(hold_a, *first_a)
    second_a = exchange(up_a, down_a, 0, 1)
    up_b, down_b = pass_on(hold_b, *first_b)
    second_b = exchange(up_b, down_b, 0, 1)
    grad_tokens, last_mark = pl.pallas_call(
        sum_kernel,
        in_specs=[far()],
        out_specs=[whole((cols, length)), whole((8, LANES))],
        out_shape=[sds((cols, length), BF16), sds((8, LANES), F32)],
        scratch_shapes=[pltpu.VMEM((RING, tp, cols // RING, length), F32), DMA((RING,))],
        compiler_params=LARGE,
        name="token_sum",
    )(token_got)
    grad_inner_weight, grad_shared_weight, grad_step_weight = pl.pallas_call(
        last_ring_kernel,
        out_shape=[
            sds((rows, inner), F32),
            sds((shared_cols, rows), F32),
            sds((heads, rows), F32),
        ],
        scratch_shapes=[pltpu.VMEM((LANES, LANES), F32)],
        compiler_params=PARAMS,
        name="last_ring",
    )(own_a, *first_a, *second_a, own_b, *first_b, *second_b, last_mark)

    return (
        mixed,
        grad_tokens.T,
        grad_inner_weight,
        grad_shared_weight.T,
        grad_step_weight.T,
    )


def solution(mesh):
    in_specs = (
        P("ctx", None),
        P(None, "tp"),
        P(),
        P(None, "tp"),
        P(None, "tp"),
        P(),
        P("tp"),
        P("tp"),
        P("tp"),
        P("ctx", "tp"),
    )
    out_specs = (P("ctx", "tp"), P("ctx", "tp"), P("ctx", "tp"), P("ctx", "tp"), P("ctx", "tp"))
    return jax.shard_map(body, mesh=mesh, in_specs=in_specs, out_specs=out_specs, check_vma=False)
```

```python
import functools

import jax
import jax.numpy as jnp
from jax import lax
from jax.experimental import pallas as pl
from jax.experimental.pallas import tpu as pltpu
from jax.sharding import PartitionSpec as P

P_SIZE = 64
N = 128
K = 4
LANES = 128
SLOT = 16
CORES = 2
RING = 4
F32 = jnp.float32
BF16 = jnp.bfloat16
NN = (((1,), (0,)), ((), ()))
NT = (((1,), (1,)), ((), ()))
TN = (((0,), (0,)), ((), ()))
BLOCK = 512
MIB = 1024 * 1024
PARAMS = pltpu.CompilerParams(vmem_limit_bytes=20 * MIB)
LARGE = pltpu.CompilerParams(vmem_limit_bytes=63 * MIB)
CHEAP = pl.CostEstimate(flops=1, bytes_accessed=1, transcendentals=0)
DMA = pltpu.SemaphoreType.DMA


def shifted(block, axis, distance):
    size = lax.axis_size(axis)
    return lax.ppermute(block, axis, [(i, (i + distance) % size) for i in range(size)])


def ctx_shift(block, dy, dz, dcore):
    def at(y, z, core):
        return (y % RING) * RING * CORES + (z % RING) * CORES + core % CORES

    route = [
        (at(y, z, core), at(y + dy, z + dz, core + dcore))
        for y in range(RING)
        for z in range(RING)
        for core in range(CORES)
    ]
    return lax.ppermute(block, "ctx", route)


def tp_shift(block, dx, dz):
    def at(x, z):
        return x % RING * 2 + z % 2

    route = [(at(x, z), at(x + dx, z + dz)) for x in range(RING) for z in range(2)]
    return lax.ppermute(block, "tp", route)


def places():
    place = lax.axis_index("ctx")
    return place // (RING * CORES), place // CORES % RING, place % CORES


def dot1(a, b, dims):
    return lax.dot_general(a, b, dims, preferred_element_type=F32)


def split(a):
    high = a.astype(BF16)
    return high, (a - high.astype(F32)).astype(BF16)


def dot3(a, b, dims):
    ah, al = a
    bh, bl = b
    return dot1(ah, bh, dims) + (dot1(ah, bl, dims) + dot1(al, bh, dims))


def dot2(a, b, dims):
    return dot1(a[0], b, dims) + dot1(a[1], b, dims)


def halves(a, axis):
    return jnp.concatenate(split(a), axis)


def square(a):
    both = halves(a, 1)
    return jnp.concatenate([both, both], 0)


def full_dot(left, right):
    both = dot1(left, right, NN)
    return both[:, 0:LANES] + both[:, LANES:]


def tall_dot(left, right):
    both = dot1(left, right, NN)
    return (both[0:LANES, 0:LANES] + both[LANES:, LANES:]) + (
        both[0:LANES, LANES:] + both[LANES:, 0:LANES]
    )


def sigmoid(z):
    return 1.0 / (1.0 + jnp.exp(-z))


def of_tile(cols, k):
    lane = lax.broadcasted_iota(jnp.int32, (cols.shape[0], LANES), 1)
    left = jnp.broadcast_to(cols[:, 2 * k : 2 * k + 1], lane.shape)
    right = jnp.broadcast_to(cols[:, 2 * k + 1 : 2 * k + 2], lane.shape)
    return jnp.where(lane < P_SIZE, left, right)


def triangle_sum(a, dims):
    length = a.shape[0]
    row = lax.broadcasted_iota(jnp.int32, (length, length), 0)
    col = lax.broadcasted_iota(jnp.int32, (length, length), 1)
    reach = row >= col if dims == NN else row <= col
    ones = jnp.where(reach, 1.0, 0.0).astype(BF16)
    first = a.astype(BF16).astype(F32)
    second = (a - first).astype(BF16).astype(F32)
    third = (a - first - second).astype(BF16).astype(F32)
    packed = first + pltpu.roll(second, SLOT, 1) + pltpu.roll(third, 2 * SLOT, 1)
    sums = dot1(ones, packed.astype(BF16), NN)
    total = sums + pltpu.roll(sums, LANES - SLOT, 1) + pltpu.roll(sums, LANES - 2 * SLOT, 1)
    lane = lax.broadcasted_iota(jnp.int32, total.shape, 1)
    return jnp.where(lane < SLOT, total, 0.0)


def project_kernel(
    tiles, heads,
    tok_ref, rim_ref, wi_ref, ws_ref, wt_ref, ci_ref, cs_ref, bias_ref, rate_ref, skip_ref, cot_ref,
    z_ref, sp_ref, dt_ref, cum_ref, cumt_ref, keep_ref, send_ref, par_ref,
    lhs, rhs, acc, cot, tok_sem, wi_sem, ws_sem, cot_sem,
):
    length = tok_ref.shape[0]
    head_rows = lhs.shape[1] - length
    inner = wi_ref.shape[1]
    total = inner + ws_ref.shape[1]
    par_ref[...] = jnp.zeros_like(par_ref)
    for i, ref in enumerate((bias_ref, rate_ref, skip_ref)):
        par_ref[i : i + 1, 0:heads] = ref[...]
    steps = tok_ref.shape[1] // BLOCK
    copies = []
    for step in range(steps):
        at = slice(step * BLOCK, (step + 1) * BLOCK)
        copies.append([
            pltpu.make_async_copy(
                tok_ref.at[:, at], lhs.at[step, head_rows:], tok_sem.at[step]
            ),
            pltpu.make_async_copy(wi_ref.at[at], rhs.at[step, :, 0:inner], wi_sem.at[step]),
            pltpu.make_async_copy(ws_ref.at[at], rhs.at[step, :, inner:total], ws_sem.at[step]),
        ])
    last_copy = pltpu.make_async_copy(cot_ref, cot, cot_sem)
    for copy in copies[0] + copies[1]:
        copy.start()
    keep = jnp.where(lax.axis_index("ctx") == 0, 0.0, 1.0)
    blank = jnp.zeros((LANES - heads, BLOCK), F32)
    for step in range(steps):
        at = slice(step * BLOCK, (step + 1) * BLOCK)
        rim = rim_ref[:, at] * keep
        lhs[step, 0:head_rows, :] = jnp.concatenate([jnp.zeros_like(rim), rim], 0).astype(BF16)
        weights = jnp.concatenate([wt_ref[:, at].astype(F32), blank], 0)
        rhs[step, :, total:] = jnp.transpose(weights).astype(BF16)
        for copy in copies[step]:
            copy.wait()
        for copy in copies[step + 2] if step + 2 < steps else [last_copy] * (step + 2 == steps):
            copy.start()
        product = dot1(lhs[step], rhs[step], NN)
        if step == 0:
            acc[...] = product
        else:
            acc[...] += product
    last_copy.wait()
    start = head_rows - (K - 1)
    sp = acc[head_rows:, total:] + par_ref[0:1, :]
    sp_ref[...] = sp
    dt = jnp.maximum(sp, 0.0) + jnp.log1p(jnp.exp(-jnp.abs(sp)))
    dt_ref[...] = dt
    cum = triangle_sum(-par_ref[1:2, :] * dt, NN)
    cum_ref[...] = cum
    cumt_ref[...] = jnp.transpose(cum)[0:SLOT, :]
    last = cum[length - 1 :, :]
    write_weight = dt * jnp.exp(last - cum)
    read_weight = jnp.exp(cum)

    def conv(at, taps, k):
        lo = k * LANES
        out = taps[0:1, lo : lo + LANES] * acc[start : start + length, at : at + LANES]
        for j in range(1, K):
            out += taps[j : j + 1, lo : lo + LANES] * acc[
                start + j : start + j + length, at : at + LANES
            ]
        return out

    zb = conv(inner, cs_ref, 0)
    z_ref[:, inner : inner + LANES] = zb
    zc = conv(inner + LANES, cs_ref, 1)
    z_ref[:, inner + LANES :] = zc
    b_rows = halves(jnp.transpose(zb * sigmoid(zb)), 0)
    c_rows = halves(jnp.transpose(zc * sigmoid(zc)), 0)
    groups = N // 8
    forward = places()[2] == 0
    blank = jnp.zeros((groups, 8, LANES), F32)
    keep_ref[:, 8 * tiles :, :] = blank
    send_ref[:, 8 * tiles :, :] = blank
    for k in range(tiles):
        lo = k * LANES
        rows = slice(8 * k, 8 * k + 8)
        z = conv(lo, ci_ref, k)
        z_ref[:, lo : lo + LANES] = z
        x = z * sigmoid(z) * of_tile(write_weight, k)
        state = tall_dot(b_rows, halves(x, 1))
        g = cot[:, lo : lo + LANES].astype(F32) * of_tile(read_weight, k)
        grad = tall_dot(c_rows, halves(g, 1))
        keep_ref[:, rows, :] = jnp.where(forward, state, grad).reshape(groups, 8, LANES)
        send_ref[:, rows, :] = jnp.where(forward, grad, state).reshape(groups, 8, LANES)
        row = jnp.broadcast_to(of_tile(last, k)[None], (groups, 1, LANES))
        keep_ref[:, 8 * tiles + k : 8 * tiles + k + 1, :] = row
        send_ref[:, 8 * tiles + k : 8 * tiles + k + 1, :] = row


def decay_rows(tiles, block):
    decay = jnp.exp(block[..., 8 * tiles :, :])
    shape = block.shape[:-2] + (8, LANES)
    return jnp.concatenate(
        [jnp.broadcast_to(decay[..., k : k + 1, :], shape) for k in range(tiles)], -2
    )


def chip_kernel(tiles, keep_ref, got_ref, out_ref):
    rows = 8 * tiles
    for i in range(keep_ref.shape[0]):
        keep = keep_ref[i]
        got = got_ref[i]
        out_ref[i, 0:rows, :] = got[0:rows, :] + decay_rows(tiles, got) * keep[0:rows, :]
        out_ref[i, rows:, :] = got[rows:, :] + keep[rows:, :]


def onward_kernel(tiles, keep_ref, arrived_ref, after_ref, out_ref):
    rows = 8 * tiles
    for i in range(keep_ref.shape[0]):
        keep = keep_ref[i]
        out_ref[i] = keep[0:rows, :] + decay_rows(tiles, keep) * arrived_ref[i]


def ctx_scan_kernel(tiles, in_ref, after_ref, out_ref):
    count = in_ref.shape[0]
    rows = 8 * tiles
    backward = places()[2] == 1

    def turn(i, held):
        at = jnp.where(backward, count - 1 - i, i)
        out_ref[at] = held
        got = in_ref[at]
        return got[0:rows, :] + decay_rows(tiles, got) * held

    lax.fori_loop(0, count, turn, jnp.zeros((rows, LANES), F32), unroll=4)


def local_kernel(
    tiles,
    z_ref, dt_ref, cum_ref, cumt_ref, cot_ref,
    y_ref, u_ref, db_ref, dc_ref,
    scores, grad_scores,
):
    length = z_ref.shape[0]
    half = length // 2
    inner = tiles * LANES
    chunks = (slice(0, half), slice(half, length))
    early, late = chunks
    zb = z_ref[:, inner : inner + LANES]
    zc = z_ref[:, inner + LANES :]
    b = zb * sigmoid(zb)
    c = zc * sigmoid(zc)
    b_wide = halves(b, 1)
    c_wide = halves(c, 1)
    b_rows = halves(jnp.transpose(b[early]), 0)
    c_rows = halves(jnp.transpose(c[late]), 0)
    row = lax.broadcasted_iota(jnp.int32, (half, half), 0)
    col = lax.broadcasted_iota(jnp.int32, (half, half), 1)
    lane = lax.broadcasted_iota(jnp.int32, (length, LANES), 1)

    def pieces(wide, at):
        return wide[at, 0:LANES], wide[at, LANES:]

    for chunk, at in enumerate(chunks):
        full = dot3(pieces(c_wide, at), pieces(b_wide, at), NT)
        scores[chunk] = jnp.where(row >= col, full, 0.0)
    grad_scores[...] = jnp.zeros_like(grad_scores)
    db_ref[...] = jnp.zeros_like(db_ref)
    dc_ref[...] = jnp.zeros_like(dc_ref)

    def one_tile(tile, carry):
        here = pl.ds(pl.multiple_of(tile * LANES, LANES), LANES)
        turn = (LANES - 2 * tile) % LANES
        dt_cols = pltpu.roll(dt_ref[...], turn, 1)
        cum_cols = pltpu.roll(cum_ref[...], turn, 1)
        dt = jnp.where(lane < P_SIZE, dt_cols[:, 0:1], dt_cols[:, 1:2])
        cum = jnp.where(lane < P_SIZE, cum_cols[:, 0:1], cum_cols[:, 1:2])
        z = z_ref[:, here]
        x = z * sigmoid(z) * dt
        g = cot_ref[:, here]
        xh, xl = split(x)
        gt = jnp.transpose(g.astype(F32)).astype(BF16)
        for chunk, at in enumerate(chunks):
            ys = []
            us = []
            for head in range(2):
                of = slice(head * P_SIZE, (head + 1) * P_SIZE)
                row_logs = cumt_ref[pl.ds(2 * tile + head, 1), at]
                decays = jnp.exp(jnp.minimum(cum_cols[at, head : head + 1] - row_logs, 0.0))
                wh, wl = split(scores[chunk] * decays)
                x_pair = jnp.concatenate([xh[at, of], xl[at, of]], 1)
                y_pair = dot1(wh, x_pair, NN) + dot1(wl, x_pair, NN)
                ys.append(y_pair[:, 0:P_SIZE] + y_pair[:, P_SIZE:])
                us.append(dot1(gt[of, at], wh, NN) + dot1(gt[of, at], wl, NN))
                g_pair = jnp.concatenate([g[at, of], g[at, of]], 1)
                grad_scores[chunk] += dot1(g_pair, x_pair, NT) * decays
            y_ref[at, here] = jnp.concatenate(ys, 1)
            u_ref[at, here] = jnp.transpose(jnp.concatenate(us, 0))
        middle = cum[half - 1 : half, :]
        down = jnp.exp(middle - cum[early])
        up = jnp.exp(cum[late] - middle)
        xd = halves(x[early] * down, 1)
        gd = halves(g[late].astype(F32) * up, 1)
        state = tall_dot(b_rows, xd)
        grad = tall_dot(c_rows, gd)
        y_ref[late, here] += up * full_dot(c_wide[late], square(state))
        u_ref[early, here] += down * full_dot(b_wide[early], square(grad))
        dc_ref[late, :] += full_dot(gd, square(jnp.transpose(state)))
        db_ref[early, :] += full_dot(xd, square(jnp.transpose(grad)))
        return carry

    lax.fori_loop(0, tiles, one_tile, 0)
    for chunk, at in enumerate(chunks):
        gs = split(jnp.where(row >= col, grad_scores[chunk], 0.0))
        dc_ref[at, :] += dot3(gs, pieces(b_wide, at), NN)
        db_ref[at, :] += dot3(gs, pieces(c_wide, at), TN)


def join_kernel(
    tiles,
    z_ref, sp_ref, dt_ref, cum_ref, par_ref, cot_ref, y_ref, u_ref,
    db_ref, dc_ref, keep_ref, send_ref, arrived_ref, other_ref,
    mixed_ref, dinner_ref, dshared_ref, gstep_ref, rim_ref,
    z_in, cot_in, y_in, u_in, state_in, z_sem, cot_sem, y_sem, u_sem, state_sem,
):
    length = z_ref.shape[0]
    inner = tiles * LANES
    states = [
        pltpu.make_async_copy(ref.at[:, 0 : 8 * tiles], state_in.at[i], state_sem.at[i])
        for i, ref in enumerate((arrived_ref, keep_ref, send_ref, other_ref))
    ]
    sides = pltpu.make_async_copy(
        z_ref.at[:, inner:], z_in.at[:, inner:], z_sem.at[tiles]
    )
    loads = []
    for k in range(tiles):
        at = slice(k * LANES, (k + 1) * LANES)
        loads.append([
            pltpu.make_async_copy(ref.at[:, at], held.at[:, at], sem.at[k])
            for ref, held, sem in (
                (z_ref, z_in, z_sem), (cot_ref, cot_in, cot_sem),
                (y_ref, y_in, y_sem), (u_ref, u_in, u_sem),
            )
        ])
    for copy in [sides, *states, *loads[0], *loads[1]]:
        copy.start()
    forward = places()[2] == 0
    dt = dt_ref[...]
    cum = cum_ref[...]
    last = cum[length - 1 :, :]
    read_weight = jnp.exp(cum)
    tail_weight = jnp.exp(last - cum)
    total_decay = jnp.exp(last)
    sides.wait()
    zb = z_in[:, inner : inner + LANES]
    zc = z_in[:, inner + LANES :]
    b_wide = halves(zb * sigmoid(zb), 1)
    c_wide = halves(zc * sigmoid(zc), 1)
    reads = jnp.zeros((length, LANES), F32)
    writes = jnp.zeros((length, LANES), F32)
    ends = jnp.zeros((8, LANES), F32)
    db = db_ref[...]
    dc = dc_ref[...]
    lane = lax.broadcasted_iota(jnp.int32, (LANES, LANES), 1)
    row = lax.broadcasted_iota(jnp.int32, (LANES, LANES), 0)
    for copy in states:
        copy.wait()
    for k in range(tiles):
        for copy in loads[k]:
            copy.wait()
        for copy in loads[k + 2] if k + 2 < tiles else []:
            copy.start()
        at = slice(k * LANES, (k + 1) * LANES)
        rows = slice(8 * k, 8 * k + 8)
        gather = jnp.where(lane == 2 * k + row // P_SIZE, 1.0, 0.0).astype(BF16)
        gather = jnp.concatenate([gather, gather], 0)
        arrived = state_in[0, :, rows, :].reshape(N, LANES)
        other = state_in[3, :, rows, :].reshape(N, LANES)
        keep = state_in[1, :, rows, :].reshape(N, LANES)
        send = state_in[2, :, rows, :].reshape(N, LANES)
        state = jnp.where(forward, arrived, other)
        grad = jnp.where(forward, other, arrived)
        own = jnp.where(forward, keep, send)
        z = z_in[:, at]
        s = sigmoid(z)
        v = z * s
        g = cot_in[:, at].astype(F32)
        read_k = of_tile(read_weight, k)
        tail_k = of_tile(tail_weight, k)
        dt_k = of_tile(dt, k)
        skip = of_tile(par_ref[...], k)[2:3, :]
        y = y_in[:, at] + read_k * full_dot(c_wide, square(state))
        u = u_in[:, at] + tail_k * full_dot(b_wide, square(grad))
        mixed_ref[:, at] = (y + skip * v).astype(BF16)
        dv = dt_k * u + skip * g
        dinner_ref[:, at] = dv * (s * (1.0 + z * (1.0 - s)))
        reads += dot1(halves(g * y, 1), gather, NN)
        writes += dot1(halves(v * u, 1), gather, NN)
        dc += full_dot(halves(g * read_k, 1), square(jnp.transpose(state)))
        db += full_dot(halves(v * dt_k * tail_k, 1), square(jnp.transpose(grad)))
        end = jnp.sum(grad * (own + of_tile(total_decay, k) * state), 0, keepdims=True)
        ends += dot1(halves(jnp.broadcast_to(end, (8, LANES)), 1), gather, NN)
    sb = sigmoid(zb)
    sc = sigmoid(zc)
    dshared_ref[:, 0:LANES] = db * (sb * (1.0 + zb * (1.0 - sb)))
    dshared_ref[:, LANES:] = dc * (sc * (1.0 + zc * (1.0 - sc)))
    rim_ref[:, 0:inner] = dinner_ref[0:8, :]
    rim_ref[:, inner:] = dshared_ref[0:8, :]
    grad_logs = triangle_sum(reads - dt * writes, TN) + ends[0:1]
    grad_dt = writes - par_ref[1:2, :] * grad_logs
    gstep_ref[...] = grad_dt * sigmoid(sp_ref[...])


def conv_back_kernel(
    dinner_ref, dshared_ref, rim_ref, ci_ref, cs_ref, gstep_ref,
    gi_ref, gst_ref, right_ref, wide_i, wide_s, gi, gst, right, gi_sem, gst_sem, right_sem,
):
    length, inner = dinner_ref.shape
    shared = dshared_ref.shape[1]
    rim = rim_ref[...] * jnp.where(lax.axis_index("ctx") < lax.axis_size("ctx") - 1, 1.0, 0.0)
    wide_s[0:length, :] = dshared_ref[...]
    wide_s[length:, :] = rim[:, inner:]

    def back(wide, taps, k):
        at = slice(k * LANES, (k + 1) * LANES)
        out = taps[K - 1 : K, at] * wide[0:length, at]
        for j in range(1, K):
            out += taps[K - 1 - j : K - j, at] * wide[j : j + length, at]
        return out

    for k in range(shared // LANES):
        at = slice(k * LANES, (k + 1) * LANES)
        grad = jnp.transpose(back(wide_s, cs_ref, k))
        gst[at, :] = grad
        high, low = split(grad)
        right[inner + k * LANES : inner + (k + 1) * LANES, :] = high
        right[inner + shared + k * LANES : inner + shared + (k + 1) * LANES, :] = low
    gst_copy = pltpu.make_async_copy(gst, gst_ref, gst_sem)
    gst_copy.start()
    high, low = split(jnp.transpose(gstep_ref[...])[0:SLOT, :])
    right[inner + 2 * shared : inner + 2 * shared + SLOT, :] = high
    right[inner + 2 * shared + SLOT :, :] = low
    wide_i[0:length, :] = dinner_ref[...]
    wide_i[length:, :] = rim[:, 0:inner]
    for k in range(inner // LANES):
        at = slice(k * LANES, (k + 1) * LANES)
        grad = back(wide_i, ci_ref, k)
        gi[:, at] = grad.astype(BF16)
        right[at, :] = jnp.transpose(grad).astype(BF16)
    gi_copy = pltpu.make_async_copy(gi, gi_ref, gi_sem)
    gi_copy.start()
    right_copy = pltpu.make_async_copy(right, right_ref, right_sem)
    right_copy.start()
    gst_copy.wait()
    gi_copy.wait()
    right_copy.wait()


def prepare_kernel(
    heads, tok_ref, wi_ref, ws_ref, wt_ref, after_ref, tok_t_ref, left_ref, mark_ref
):
    inner = wi_ref.shape[1]
    shared = ws_ref.shape[1]
    end = inner + 2 * shared
    mark_ref[...] = jnp.zeros_like(mark_ref)

    def turn(step, carry):
        at = pl.ds(pl.multiple_of(step * BLOCK, BLOCK), BLOCK)
        tok_t_ref[at, :] = jnp.transpose(tok_ref[:, at].astype(F32)).astype(BF16)
        return carry

    lax.fori_loop(0, tok_ref.shape[1] // BLOCK, turn, 0)
    left_ref[:, 0:inner] = wi_ref[...]
    left_ref[:, inner : inner + shared] = ws_ref[...]
    left_ref[:, inner + shared : end] = ws_ref[...]
    blank = jnp.zeros((SLOT - heads, left_ref.shape[0]), F32)
    step = jnp.concatenate([wt_ref[...].astype(F32), blank], 0)
    left_ref[:, end:] = jnp.transpose(jnp.concatenate([step, step], 0)).astype(BF16)


def token_grad_kernel(
    left_ref, right_ref,
    up_ref, down_ref, hold_ref, own_ref, mine_ref, other_ref, mark_ref,
    left, right, up, down, hold, own, mine, other,
    left_sem, right_sem, ring_sem, mine_sem, other_sem,
):
    mark_ref[...] = jnp.zeros_like(mark_ref)
    place = lax.axis_index("tp")
    x, z = place // 2, place % 2
    rows = up_ref.shape[1]
    slab = left.shape[1]
    right_copy = pltpu.make_async_copy(right_ref, right, right_sem)
    right_copy.start()
    order = (2, 1, 3, 0)
    loads = [
        pltpu.make_async_copy(
            left_ref.at[pl.ds(pl.multiple_of((x + step) % RING * slab, slab), slab)],
            left.at[step],
            left_sem.at[step],
        )
        for step in range(RING)
    ]
    for step in order[0:2]:
        loads[step].start()
    right_copy.wait()
    rings = [
        pltpu.make_async_copy(held, ref, ring_sem.at[i])
        for i, (held, ref) in enumerate(
            ((up, up_ref), (down, down_ref), (hold, hold_ref), (own, own_ref))
        )
    ]
    stores = []
    for turn, step in enumerate(order):
        loads[step].wait()
        if turn + 2 < RING:
            loads[order[turn + 2]].start()
        product = dot1(left[step], right[...], NN).reshape(2, 2 * rows, right.shape[1])
        first, second = product[0, 0:rows], product[1, 0:rows]
        if step == 2:
            up[0] = first
            down[0] = second
        elif step == 1:
            hold[0] = first
            up[1] = second
            stores.append(rings[0])
        elif step == 3:
            down[1] = first
            hold[1] = second
            stores += rings[1:3]
        else:
            own[0] = first
            own[1] = second
            stores.append(rings[3])
        mine[step] = jnp.where(z == 0, product[0, rows:], product[1, rows:])
        other[step] = jnp.where(z == 0, product[1, rows:], product[0, rows:])
        sides = [
            pltpu.make_async_copy(mine.at[step], mine_ref.at[step], mine_sem.at[step]),
            pltpu.make_async_copy(other.at[step], other_ref.at[step], other_sem.at[step]),
        ]
        stores += sides
        for copy in sides:
            copy.start()
        if step == 1:
            rings[0].start()
        elif step == 3:
            rings[1].start()
            rings[2].start()
        elif step == 0:
            rings[3].start()
    for copy in stores:
        copy.wait()


def token_split_kernel(
    own_ref, from_below_ref, from_above_ref, last_below_ref, last_above_ref, after_ref,
    keep_ref, send_ref,
):
    near = lax.axis_index("tp") % 2 == 0
    first, second = ring_sum(
        own_ref, from_below_ref, from_above_ref, last_below_ref, last_above_ref
    )
    keep_ref[...] = jnp.where(near, first, second)
    send_ref[...] = jnp.where(near, second, first)


def token_ring_kernel(mine_ref, got_ref, after_ref, up_ref, down_ref, hold_ref, own_ref):
    half = up_ref.shape[1]

    def part(target, which):
        at = slice(which * half, (which + 1) * half)
        return mine_ref[target, at, :] + got_ref[target, at, :]

    ring_parts(0, part, up_ref, down_ref, hold_ref, own_ref)


def token_sum_kernel(
    keep_ref, got_ref,
    own_ref, from_below_ref, from_above_ref, last_below_ref, last_above_ref, after_ref,
    out_ref, mark_ref,
):
    mark_ref[...] = jnp.zeros_like(mark_ref)
    rows = keep_ref.shape[0]
    half = rows // 2
    first, second = ring_sum(
        own_ref, from_below_ref, from_above_ref, last_below_ref, last_above_ref
    )
    out_ref[0:rows, :] = (keep_ref[...] + got_ref[...]).astype(out_ref.dtype)
    out_ref[rows : rows + half, :] = first.astype(out_ref.dtype)
    out_ref[rows + half :, :] = second.astype(out_ref.dtype)


def put_rows(y, product, mine_ref, other_ref):
    rows = mine_ref.shape[1] * mine_ref.shape[2] // RING
    parts = product.reshape(RING, CORES, rows, product.shape[1])

    def put(first, second):
        for z in range(RING):
            at = z * rows % mine_ref.shape[2]
            first[y, z * rows // mine_ref.shape[2], at : at + rows, :] = parts[z, 0]
            second[y, z * rows // mine_ref.shape[2], at : at + rows, :] = parts[z, 1]

    @pl.when(places()[2] == 0)
    def _():
        put(mine_ref, other_ref)

    @pl.when(places()[2] == 1)
    def _():
        put(other_ref, mine_ref)


def weight_grad_kernel(tok_ref, gi_ref, after_ref, later_ref, mine_ref, other_ref):
    slab = tok_ref.shape[0] // RING
    right = gi_ref[...]

    def turn(y, carry):
        at = pl.ds(pl.multiple_of(y * slab, slab), slab)
        put_rows(y, dot1(tok_ref[at, :], right, NN), mine_ref, other_ref)
        return carry

    lax.fori_loop(0, RING, turn, 0)


def side_grad_kernel(parts_ref, gstep_ref, tok_ref, mine_ref, other_ref):
    slab = tok_ref.shape[0] // RING
    shared_cols = parts_ref.shape[1]
    total = parts_ref[0]
    for i in range(1, parts_ref.shape[0]):
        total += parts_ref[i]
    blank = jnp.zeros((LANES - shared_cols, total.shape[1]), F32)
    cols = jnp.transpose(jnp.concatenate([total, blank], 0))
    right = halves(cols + pltpu.roll(gstep_ref[...], shared_cols, 1), 1)

    def turn(y, carry):
        at = pl.ds(pl.multiple_of(y * slab, slab), slab)
        both = dot1(tok_ref[at, :], right, NN)
        put_rows(y, both[:, 0:LANES] + both[:, LANES:], mine_ref, other_ref)
        return carry

    lax.fori_loop(0, RING, turn, 0)


def ring_parts(place, part, up_ref, down_ref, hold_ref, own_ref):
    above, facing, below = [(place + i) % RING for i in (1, 2, 3)]
    up_ref[0] = part(facing, 0)
    up_ref[1] = part(above, 1)
    down_ref[0] = part(facing, 1)
    down_ref[1] = part(below, 0)
    hold_ref[0] = part(above, 0)
    hold_ref[1] = part(below, 1)
    own_ref[0] = part(place, 0)
    own_ref[1] = part(place, 1)


def core_sum_kernel(lanes, *refs):
    blocks = refs[:-5]

    def part(target, half):
        sums = [
            blocks[i][target, half, :, at] + blocks[i + 1][target, half, :, at]
            for i, at in zip(range(0, len(blocks), 2), lanes)
        ]
        return jnp.concatenate(sums, 1) if len(sums) > 1 else sums[0]

    ring_parts(places()[0], part, *refs[-4:])


def pass_on_kernel(hold_ref, from_below_ref, from_above_ref, after_ref, up_ref, down_ref):
    up_ref[...] = hold_ref[0] + from_below_ref[0]
    down_ref[...] = hold_ref[1] + from_above_ref[0]


def ring_sum(own_ref, from_below_ref, from_above_ref, last_below_ref, last_above_ref):
    first = own_ref[0] + from_above_ref[1] + last_below_ref[...]
    second = own_ref[1] + from_below_ref[1] + last_above_ref[...]
    return first, second


def next_ring_kernel(*refs):
    up_ref, down_ref, hold_ref, own_ref, sums = refs[-5:]
    lanes = refs[0].shape[2]
    half = RING // 2
    for i in range(2):
        at = slice(i * lanes, (i + 1) * lanes)
        first, second = ring_sum(*refs[5 * i : 5 * i + 5])
        shape = (half, 2, sums.shape[2], lanes)
        sums[0:half, :, :, at] = first.reshape(shape)
        sums[half:, :, :, at] = second.reshape(shape)

    def part(target, which):
        return sums[target, which]

    ring_parts(places()[1], part, up_ref, down_ref, hold_ref, own_ref)


def last_ring_kernel(*refs):
    inner_ref, shared_ref, step_ref, side = refs[6:]
    half = inner_ref.shape[0] // 2
    inner = inner_ref.shape[1]
    shared_cols = shared_ref.shape[0]
    side[2 * half :, :] = jnp.zeros((side.shape[0] - 2 * half, LANES), F32)
    for i, part in enumerate(ring_sum(*refs[0:5])):
        rows = slice(i * half, (i + 1) * half)
        inner_ref[rows, :] = part[:, 0:inner]
        side[rows, :] = part[:, inner:]
    flat = jnp.transpose(side[...])
    shared_ref[...] = flat[0:shared_cols, 0 : 2 * half]
    step_ref[...] = flat[shared_cols : shared_cols + step_ref.shape[0], 0 : 2 * half]


def whole(shape):
    return pl.BlockSpec(shape, lambda *_: (0,) * len(shape))


def after():
    return pl.BlockSpec(memory_space=pl.ANY)


def far():
    return pl.BlockSpec(memory_space=pltpu.HBM)


def body(
    tokens,
    inner_weight,
    shared_weight,
    step_weight,
    conv_inner,
    conv_shared,
    step_bias,
    decay_rate,
    skip_gain,
    cotangent,
):
    length, width = tokens.shape
    inner = inner_weight.shape[1]
    shared = shared_weight.shape[1]
    heads = step_weight.shape[1]
    tiles = inner // LANES
    ctx = lax.axis_size("ctx")
    tp = lax.axis_size("tp")
    chips = ctx // CORES
    same_core = [[CORES * chip + i for chip in range(chips)] for i in range(CORES)]
    sds = jax.ShapeDtypeStruct
    step_weight_t = step_weight.T

    rim = shifted(tokens[length - 8 :].astype(F32), "ctx", 1)

    total = inner + shared
    pay_rows = 8 * tiles + 8
    z, sp, dt, cum, cum_t, keep, send, params = pl.pallas_call(
        functools.partial(project_kernel, tiles, heads),
        in_specs=[
            far(),
            whole((8, width)),
            far(),
            far(),
            whole((heads, width)),
            whole((K, inner)),
            whole((K, shared)),
            whole((1, heads)),
            whole((1, heads)),
            whole((1, heads)),
            far(),
        ],
        out_specs=[
            whole((length, total)),
            whole((length, LANES)),
            whole((length, LANES)),
            whole((length, LANES)),
            whole((SLOT, length)),
            whole((chips, pay_rows, LANES)),
            whole((chips, pay_rows, LANES)),
            whole((8, LANES)),
        ],
        out_shape=[
            sds((length, total), F32),
            sds((length, LANES), F32),
            sds((length, LANES), F32),
            sds((length, LANES), F32),
            sds((SLOT, length), F32),
            sds((chips, pay_rows, LANES), F32),
            sds((chips, pay_rows, LANES), F32),
            sds((8, LANES), F32),
        ],
        scratch_shapes=[
            pltpu.VMEM((width // BLOCK, length + 16, BLOCK), BF16),
            pltpu.VMEM((width // BLOCK, BLOCK, total + LANES), BF16),
            pltpu.VMEM((length + 16, total + LANES), F32),
            pltpu.VMEM((length, inner), BF16),
            DMA((width // BLOCK,)),
            DMA((width // BLOCK,)),
            DMA((width // BLOCK,)),
            DMA,
        ],
        compiler_params=LARGE,
        name="project",
    )(
        tokens, rim, inner_weight, shared_weight, step_weight_t,
        conv_inner, conv_shared, step_bias[None], decay_rate[None], skip_gain[None], cotangent,
    )

    got = ctx_shift(send, 0, 0, 1)
    chip_state = pl.pallas_call(
        functools.partial(chip_kernel, tiles),
        out_shape=sds((chips, pay_rows, LANES), F32),
        compiler_params=PARAMS,
        name="chip_state",
    )(keep, got)
    by_rows = lax.all_to_all(
        chip_state, "ctx", 0, 0, axis_index_groups=same_core, tiled=True
    )

    y, u, db, dc = pl.pallas_call(
        functools.partial(local_kernel, tiles),
        out_shape=[
            sds((length, inner), F32),
            sds((length, inner), F32),
            sds((length, LANES), F32),
            sds((length, LANES), F32),
        ],
        scratch_shapes=[
            pltpu.VMEM((2, length // 2, length // 2), F32),
            pltpu.VMEM((2, length // 2, length // 2), F32),
        ],
        compiler_params=LARGE,
        cost_estimate=pl.CostEstimate(
            flops=10 * length * length * inner, bytes_accessed=8_000_000, transcendentals=0
        ),
        name="local",
    )(z, dt, cum, cum_t, cotangent)

    scanned = pl.pallas_call(
        functools.partial(ctx_scan_kernel, tiles),
        in_specs=[whole((chips, pay_rows, LANES)), after()],
        out_specs=whole((chips, 8 * tiles, LANES)),
        out_shape=sds((chips, 8 * tiles, LANES), F32),
        compiler_params=PARAMS,
        name="ctx_scan",
    )(by_rows, dc)
    arrived = lax.all_to_all(scanned, "ctx", 0, 0, axis_index_groups=same_core, tiled=True)
    right_rows = inner + 2 * shared + 2 * SLOT
    tok_t, left, mark = pl.pallas_call(
        functools.partial(prepare_kernel, heads),
        in_specs=[
            whole((length, width)),
            whole((width, inner)),
            whole((width, shared)),
            whole((heads, width)),
            after(),
        ],
        out_specs=[whole((width, length)), whole((width, right_rows)), whole((8, LANES))],
        out_shape=[
            sds((width, length), BF16),
            sds((width, right_rows), BF16),
            sds((8, LANES), F32),
        ],
        compiler_params=LARGE,
        name="prepare",
    )(tokens, inner_weight, shared_weight, step_weight_t, scanned)
    onward = pl.pallas_call(
        functools.partial(onward_kernel, tiles),
        in_specs=[
            whole((chips, pay_rows, LANES)), whole((chips, 8 * tiles, LANES)), after(),
        ],
        out_specs=whole((chips, 8 * tiles, LANES)),
        out_shape=sds((chips, 8 * tiles, LANES), F32),
        compiler_params=PARAMS,
        name="onward",
    )(keep, arrived, mark)
    other = ctx_shift(onward, 0, 0, 1)

    column = whole((length, LANES))
    mixed, dinner, dshared, gstep, rim_out = pl.pallas_call(
        functools.partial(join_kernel, tiles),
        in_specs=[
            far(),
            column,
            column,
            column,
            whole((8, LANES)),
            far(),
            far(),
            far(),
            column,
            column,
            far(),
            far(),
            far(),
            far(),
        ],
        out_specs=[
            whole((length, inner)), whole((length, inner)), whole((length, shared)), column,
            whole((8, total)),
        ],
        out_shape=[
            sds((length, inner), BF16),
            sds((length, inner), F32),
            sds((length, shared), F32),
            sds((length, LANES), F32),
            sds((8, total), F32),
        ],
        scratch_shapes=[
            pltpu.VMEM((length, total), F32),
            pltpu.VMEM((length, inner), BF16),
            pltpu.VMEM((length, inner), F32),
            pltpu.VMEM((length, inner), F32),
            pltpu.VMEM((4, chips, 8 * tiles, LANES), F32),
            DMA((tiles + 1,)),
            DMA((tiles,)),
            DMA((tiles,)),
            DMA((tiles,)),
            DMA((4,)),
        ],
        compiler_params=LARGE,
        name="join",
    )(
        z, sp, dt, cum, params, cotangent, y, u, db, dc,
        keep, send, arrived, other,
    )

    rim_back = shifted(rim_out, "ctx", -1)
    grad_inner, grad_shared_t, right = pl.pallas_call(
        conv_back_kernel,
        in_specs=[
            whole((length, inner)),
            whole((length, shared)),
            whole((8, total)),
            whole((K, inner)),
            whole((K, shared)),
            column,
        ],
        out_specs=[far(), far(), far()],
        out_shape=[
            sds((length, inner), BF16),
            sds((shared, length), F32),
            sds((right_rows, length), BF16),
        ],
        scratch_shapes=[
            pltpu.VMEM((length + 8, inner), F32),
            pltpu.VMEM((length + 8, shared), F32),
            pltpu.VMEM((length, inner), BF16),
            pltpu.VMEM((shared, length), F32),
            pltpu.VMEM((right_rows, length), BF16),
            DMA,
            DMA,
            DMA,
        ],
        compiler_params=LARGE,
        name="conv_back",
    )(dinner, dshared, rim_back, conv_inner, conv_shared, gstep)

    shared_cols = shared // tp
    shared_parts = lax.all_to_all(
        grad_shared_t.reshape(tp, shared_cols, length), "tp", 0, 0, tiled=True
    )

    cols = width // tp
    t_half = cols // 2
    t_quarter = cols // 4
    message = sds((2, t_half, length), F32)
    side_block = sds((RING, t_half, length), F32)
    t_up, t_down, t_hold, t_own, t_mine, t_other, token_mark = pl.pallas_call(
        token_grad_kernel,
        in_specs=[far(), far()],
        out_specs=[far()] * 6 + [whole((8, LANES))],
        out_shape=[message] * 4 + [side_block] * 2 + [sds((8, LANES), F32)],
        scratch_shapes=[
            pltpu.VMEM((RING, 2 * cols, right_rows), BF16),
            pltpu.VMEM((right_rows, length), BF16),
        ]
        + [pltpu.VMEM(message.shape, F32)] * 4
        + [pltpu.VMEM(side_block.shape, F32)] * 2
        + [DMA((RING,)), DMA, DMA((RING,)), DMA((RING,)), DMA((RING,))],
        compiler_params=LARGE,
        cost_estimate=CHEAP,
        name="token_grad",
    )(left, right)

    def exchange_tp(up, down):
        return tp_shift(up, 1, 0), tp_shift(down, -1, 0)

    t_first = exchange_tp(t_up, t_down)
    t_got = tp_shift(t_other, 0, 1)

    rows = width // ctx
    y_half = RING * rows // 2
    z_half = rows // 2
    lanes = (inner + LANES) // 2

    def row_block(wide):
        return whole((RING, 2, y_half, wide))

    def row_shape(wide):
        return sds((RING, 2, y_half, wide), F32)

    mine, core_other = pl.pallas_call(
        weight_grad_kernel,
        in_specs=[whole((width, length)), whole((length, inner)), after(), after()],
        out_specs=[row_block(inner)] * 2,
        out_shape=[row_shape(inner)] * 2,
        compiler_params=PARAMS,
        cost_estimate=CHEAP,
        name="weight_grad",
    )(tok_t, grad_inner, token_mark, shared_parts)
    core_got = ctx_shift(core_other, 0, 0, 1)

    def core_sum(blocks, spans, ready):
        return pl.pallas_call(
            functools.partial(core_sum_kernel, spans),
            in_specs=[whole(block.shape) for block in blocks] + [after()],
            out_specs=[whole((2, y_half, lanes))] * 4,
            out_shape=[sds((2, y_half, lanes), F32)] * 4,
            compiler_params=PARAMS,
            cost_estimate=CHEAP,
            name="core_sum",
        )(*blocks, ready)

    def exchange(up, down, dy, dz):
        return ctx_shift(up, dy, dz, 0), ctx_shift(down, -dy, -dz, 0)

    def pass_on(hold, below, above, ready):
        half, wide = hold.shape[1:]
        return pl.pallas_call(
            pass_on_kernel,
            in_specs=[whole(hold.shape)] * 3 + [after()],
            out_specs=[whole((half, wide))] * 2,
            out_shape=[sds((half, wide), F32)] * 2,
            compiler_params=PARAMS,
            cost_estimate=CHEAP,
            name="pass_on",
        )(hold, below, above, ready)

    def next_ring(parts_a, parts_b, ready):
        wide = 2 * lanes
        return pl.pallas_call(
            next_ring_kernel,
            in_specs=([whole((2, y_half, lanes))] * 3 + [whole((y_half, lanes))] * 2) * 2
            + [after()],
            out_specs=[whole((2, z_half, wide))] * 4,
            out_shape=[sds((2, z_half, wide), F32)] * 4,
            scratch_shapes=[pltpu.VMEM((RING, 2, z_half, wide), F32)],
            compiler_params=PARAMS,
            cost_estimate=CHEAP,
            name="next_ring",
        )(*parts_a, *parts_b, ready)

    side_mine, side_other = pl.pallas_call(
        side_grad_kernel,
        in_specs=[
            whole((tp, shared_cols, length)),
            column,
            whole((width, length)),
        ],
        out_specs=[row_block(LANES)] * 2,
        out_shape=[row_shape(LANES)] * 2,
        compiler_params=PARAMS,
        cost_estimate=CHEAP,
        name="side_grad",
    )(shared_parts, gstep, tok_t)
    side_got = ctx_shift(side_other, 0, 0, 1)
    up_a, down_a, hold_a, own_a = core_sum((mine, core_got), [slice(0, lanes)], side_mine)
    first_a = exchange(up_a, down_a, 1, 0)
    side_got = ctx_shift(side_other, 0, 0, 1)
    up_b, down_b, hold_b, own_b = core_sum(
        (mine, core_got, side_mine, side_got), [slice(lanes, inner), slice(0, LANES)], hold_a
    )
    first_b = exchange(up_b, down_b, 1, 0)
    t_up, t_down = pass_on(t_hold, *t_first, hold_b)
    t_second = exchange_tp(t_up, t_down)
    up_a, down_a = pass_on(hold_a, *first_a, t_up)
    second_a = exchange(up_a, down_a, 1, 0)
    t_keep, t_send = pl.pallas_call(
        token_split_kernel,
        in_specs=[whole(message.shape)] * 3 + [whole(message.shape[1:])] * 2 + [after()],
        out_specs=[whole(message.shape[1:])] * 2,
        out_shape=[sds(message.shape[1:], F32)] * 2,
        compiler_params=PARAMS,
        cost_estimate=CHEAP,
        name="token_split",
    )(t_own, *t_first, *t_second, up_a)
    t_last = tp_shift(t_send, 0, 1)
    quarter = sds((2, t_quarter, length), F32)
    q_up, q_down, q_hold, q_own = pl.pallas_call(
        token_ring_kernel,
        in_specs=[whole(side_block.shape)] * 2 + [after()],
        out_specs=[whole(quarter.shape)] * 4,
        out_shape=[quarter] * 4,
        compiler_params=PARAMS,
        cost_estimate=CHEAP,
        name="token_ring",
    )(t_mine, t_got, t_keep)
    q_first = exchange_tp(q_up, q_down)
    up_b, down_b = pass_on(hold_b, *first_b, q_hold)
    second_b = exchange(up_b, down_b, 1, 0)
    up, down, hold, own = next_ring(
        (own_a, *first_a, *second_a), (own_b, *first_b, *second_b), up_b
    )
    first = exchange(up, down, 0, 1)
    q_up, q_down = pass_on(q_hold, *q_first, hold)
    q_second = exchange_tp(q_up, q_down)
    up, down = pass_on(hold, *first, q_up)
    second = exchange(up, down, 0, 1)
    grad_tokens, last_mark = pl.pallas_call(
        token_sum_kernel,
        in_specs=[whole(t_keep.shape)] * 2
        + [whole(quarter.shape)] * 3
        + [whole(quarter.shape[1:])] * 2
        + [after()],
        out_specs=[whole((cols, length)), whole((8, LANES))],
        out_shape=[sds((cols, length), BF16), sds((8, LANES), F32)],
        compiler_params=PARAMS,
        cost_estimate=CHEAP,
        name="token_sum",
    )(t_keep, t_last, q_own, *q_first, *q_second, up)
    grad_inner_weight, grad_shared_weight, grad_step_weight = pl.pallas_call(
        last_ring_kernel,
        out_shape=[
            sds((rows, inner), F32),
            sds((shared_cols, rows), F32),
            sds((heads, rows), F32),
        ],
        scratch_shapes=[pltpu.VMEM((LANES, LANES), F32)],
        compiler_params=PARAMS,
        cost_estimate=CHEAP,
        name="last_ring",
    )(own, *first, *second, last_mark)

    return (
        mixed,
        grad_tokens.T,
        grad_inner_weight,
        grad_shared_weight.T,
        grad_step_weight.T,
    )


def solution(mesh):
    in_specs = (
        P("ctx", None),
        P(None, "tp"),
        P(),
        P(None, "tp"),
        P(None, "tp"),
        P(),
        P("tp"),
        P("tp"),
        P("tp"),
        P("ctx", "tp"),
    )
    out_specs = (P("ctx", "tp"), P("ctx", "tp"), P("ctx", "tp"), P("ctx", "tp"), P("ctx", "tp"))
    return jax.shard_map(body, mesh=mesh, in_specs=in_specs, out_specs=out_specs, check_vma=False)
```

```python
import functools

import jax
import jax.numpy as jnp
from jax import lax
from jax.experimental import pallas as pl
from jax.experimental.pallas import tpu as pltpu
from jax.sharding import PartitionSpec as P

P_SIZE = 64
N = 128
K = 4
LANES = 128
SLOT = 16
CORES = 2
RING = 4
F32 = jnp.float32
BF16 = jnp.bfloat16
NN = (((1,), (0,)), ((), ()))
NT = (((1,), (1,)), ((), ()))
TN = (((0,), (0,)), ((), ()))
BLOCK = 512
MIB = 1024 * 1024
PARAMS = pltpu.CompilerParams(vmem_limit_bytes=20 * MIB)
LARGE = pltpu.CompilerParams(vmem_limit_bytes=63 * MIB)
CHEAP = pl.CostEstimate(flops=1, bytes_accessed=1, transcendentals=0)
DMA = pltpu.SemaphoreType.DMA


def shifted(block, axis, distance):
    size = lax.axis_size(axis)
    return lax.ppermute(block, axis, [(i, (i + distance) % size) for i in range(size)])


def ctx_shift(block, dy, dz, dcore):
    def at(y, z, core):
        return (y % RING) * RING * CORES + (z % RING) * CORES + core % CORES

    route = [
        (at(y, z, core), at(y + dy, z + dz, core + dcore))
        for y in range(RING)
        for z in range(RING)
        for core in range(CORES)
    ]
    return lax.ppermute(block, "ctx", route)


def tp_shift(block, dx, dz):
    def at(x, z):
        return x % RING * 2 + z % 2

    route = [(at(x, z), at(x + dx, z + dz)) for x in range(RING) for z in range(2)]
    return lax.ppermute(block, "tp", route)


def places():
    place = lax.axis_index("ctx")
    return place // (RING * CORES), place // CORES % RING, place % CORES


def dot1(a, b, dims):
    return lax.dot_general(a, b, dims, preferred_element_type=F32)


def split(a):
    high = a.astype(BF16)
    return high, (a - high.astype(F32)).astype(BF16)


def dot3(a, b, dims):
    ah, al = a
    bh, bl = b
    return dot1(ah, bh, dims) + (dot1(ah, bl, dims) + dot1(al, bh, dims))


def dot2(a, b, dims):
    return dot1(a[0], b, dims) + dot1(a[1], b, dims)


def halves(a, axis):
    return jnp.concatenate(split(a), axis)


def square(a):
    both = halves(a, 1)
    return jnp.concatenate([both, both], 0)


def full_dot(left, right):
    both = dot1(left, right, NN)
    return both[:, 0:LANES] + both[:, LANES:]


def tall_dot(left, right):
    both = dot1(left, right, NN)
    return (both[0:LANES, 0:LANES] + both[LANES:, LANES:]) + (
        both[0:LANES, LANES:] + both[LANES:, 0:LANES]
    )


def sigmoid(z):
    return 1.0 / (1.0 + jnp.exp(-z))


def of_tile(cols, k):
    lane = lax.broadcasted_iota(jnp.int32, (cols.shape[0], LANES), 1)
    left = jnp.broadcast_to(cols[:, 2 * k : 2 * k + 1], lane.shape)
    right = jnp.broadcast_to(cols[:, 2 * k + 1 : 2 * k + 2], lane.shape)
    return jnp.where(lane < P_SIZE, left, right)


def triangle_sum(a, dims):
    length = a.shape[0]
    row = lax.broadcasted_iota(jnp.int32, (length, length), 0)
    col = lax.broadcasted_iota(jnp.int32, (length, length), 1)
    reach = row >= col if dims == NN else row <= col
    ones = jnp.where(reach, 1.0, 0.0).astype(BF16)
    first = a.astype(BF16).astype(F32)
    second = (a - first).astype(BF16).astype(F32)
    third = (a - first - second).astype(BF16).astype(F32)
    packed = first + pltpu.roll(second, SLOT, 1) + pltpu.roll(third, 2 * SLOT, 1)
    sums = dot1(ones, packed.astype(BF16), NN)
    total = sums + pltpu.roll(sums, LANES - SLOT, 1) + pltpu.roll(sums, LANES - 2 * SLOT, 1)
    lane = lax.broadcasted_iota(jnp.int32, total.shape, 1)
    return jnp.where(lane < SLOT, total, 0.0)


def project_kernel(
    tiles, heads,
    tok_ref, rim_ref, wi_ref, ws_ref, wt_ref, ci_ref, cs_ref, bias_ref, rate_ref, skip_ref, cot_ref,
    z_ref, sp_ref, dt_ref, cum_ref, cumt_ref, keep_ref, send_ref, par_ref,
    lhs, rhs, acc, cot, tok_sem, wi_sem, ws_sem, cot_sem,
):
    length = tok_ref.shape[0]
    head_rows = lhs.shape[1] - length
    inner = wi_ref.shape[1]
    total = inner + ws_ref.shape[1]
    par_ref[...] = jnp.zeros_like(par_ref)
    for i, ref in enumerate((bias_ref, rate_ref, skip_ref)):
        par_ref[i : i + 1, 0:heads] = ref[...]
    steps = tok_ref.shape[1] // BLOCK
    copies = []
    for step in range(steps):
        at = slice(step * BLOCK, (step + 1) * BLOCK)
        copies.append([
            pltpu.make_async_copy(
                tok_ref.at[:, at], lhs.at[step, head_rows:], tok_sem.at[step]
            ),
            pltpu.make_async_copy(wi_ref.at[at], rhs.at[step, :, 0:inner], wi_sem.at[step]),
            pltpu.make_async_copy(ws_ref.at[at], rhs.at[step, :, inner:total], ws_sem.at[step]),
        ])
    last_copy = pltpu.make_async_copy(cot_ref, cot, cot_sem)
    for copy in copies[0] + copies[1]:
        copy.start()
    keep = jnp.where(lax.axis_index("ctx") == 0, 0.0, 1.0)
    blank = jnp.zeros((LANES - heads, BLOCK), F32)
    for step in range(steps):
        at = slice(step * BLOCK, (step + 1) * BLOCK)
        rim = rim_ref[:, at] * keep
        lhs[step, 0:head_rows, :] = jnp.concatenate([jnp.zeros_like(rim), rim], 0).astype(BF16)
        weights = jnp.concatenate([wt_ref[:, at].astype(F32), blank], 0)
        rhs[step, :, total:] = jnp.transpose(weights).astype(BF16)
        for copy in copies[step]:
            copy.wait()
        for copy in copies[step + 2] if step + 2 < steps else [last_copy] * (step + 2 == steps):
            copy.start()
        product = dot1(lhs[step], rhs[step], NN)
        if step == 0:
            acc[...] = product
        else:
            acc[...] += product
    last_copy.wait()
    start = head_rows - (K - 1)
    sp = acc[head_rows:, total:] + par_ref[0:1, :]
    sp_ref[...] = sp
    dt = jnp.maximum(sp, 0.0) + jnp.log1p(jnp.exp(-jnp.abs(sp)))
    dt_ref[...] = dt
    cum = triangle_sum(-par_ref[1:2, :] * dt, NN)
    cum_ref[...] = cum
    cumt_ref[...] = jnp.transpose(cum)[0:SLOT, :]
    last = cum[length - 1 :, :]
    write_weight = dt * jnp.exp(last - cum)
    read_weight = jnp.exp(cum)

    def conv(at, taps, k):
        lo = k * LANES
        out = taps[0:1, lo : lo + LANES] * acc[start : start + length, at : at + LANES]
        for j in range(1, K):
            out += taps[j : j + 1, lo : lo + LANES] * acc[
                start + j : start + j + length, at : at + LANES
            ]
        return out

    zb = conv(inner, cs_ref, 0)
    z_ref[:, inner : inner + LANES] = zb
    zc = conv(inner + LANES, cs_ref, 1)
    z_ref[:, inner + LANES :] = zc
    b_rows = halves(jnp.transpose(zb * sigmoid(zb)), 0)
    c_rows = halves(jnp.transpose(zc * sigmoid(zc)), 0)
    groups = N // 8
    forward = places()[2] == 0
    blank = jnp.zeros((groups, 8, LANES), F32)
    keep_ref[:, 8 * tiles :, :] = blank
    send_ref[:, 8 * tiles :, :] = blank
    for k in range(tiles):
        lo = k * LANES
        rows = slice(8 * k, 8 * k + 8)
        z = conv(lo, ci_ref, k)
        z_ref[:, lo : lo + LANES] = z
        x = z * sigmoid(z) * of_tile(write_weight, k)
        state = tall_dot(b_rows, halves(x, 1))
        g = cot[:, lo : lo + LANES].astype(F32) * of_tile(read_weight, k)
        grad = tall_dot(c_rows, halves(g, 1))
        keep_ref[:, rows, :] = jnp.where(forward, state, grad).reshape(groups, 8, LANES)
        send_ref[:, rows, :] = jnp.where(forward, grad, state).reshape(groups, 8, LANES)
        row = jnp.broadcast_to(of_tile(last, k)[None], (groups, 1, LANES))
        keep_ref[:, 8 * tiles + k : 8 * tiles + k + 1, :] = row
        send_ref[:, 8 * tiles + k : 8 * tiles + k + 1, :] = row


def decay_rows(tiles, block):
    decay = jnp.exp(block[..., 8 * tiles :, :])
    shape = block.shape[:-2] + (8, LANES)
    return jnp.concatenate(
        [jnp.broadcast_to(decay[..., k : k + 1, :], shape) for k in range(tiles)], -2
    )


def chip_kernel(tiles, keep_ref, got_ref, out_ref):
    rows = 8 * tiles
    for i in range(keep_ref.shape[0]):
        keep = keep_ref[i]
        got = got_ref[i]
        out_ref[i, 0:rows, :] = got[0:rows, :] + decay_rows(tiles, got) * keep[0:rows, :]
        out_ref[i, rows:, :] = got[rows:, :] + keep[rows:, :]


def onward_kernel(tiles, keep_ref, arrived_ref, after_ref, out_ref):
    rows = 8 * tiles
    for i in range(keep_ref.shape[0]):
        keep = keep_ref[i]
        out_ref[i] = keep[0:rows, :] + decay_rows(tiles, keep) * arrived_ref[i]


def ctx_scan_kernel(tiles, in_ref, after_ref, out_ref):
    count = in_ref.shape[0]
    rows = 8 * tiles
    backward = places()[2] == 1

    def turn(i, held):
        at = jnp.where(backward, count - 1 - i, i)
        out_ref[at] = held
        got = in_ref[at]
        return got[0:rows, :] + decay_rows(tiles, got) * held

    lax.fori_loop(0, count, turn, jnp.zeros((rows, LANES), F32), unroll=4)


def local_kernel(
    tiles,
    z_ref, dt_ref, cum_ref, cumt_ref, cot_ref,
    y_ref, u_ref, db_ref, dc_ref,
    scores, grad_scores,
):
    length = z_ref.shape[0]
    half = length // 2
    inner = tiles * LANES
    chunks = (slice(0, half), slice(half, length))
    early, late = chunks
    zb = z_ref[:, inner : inner + LANES]
    zc = z_ref[:, inner + LANES :]
    b = zb * sigmoid(zb)
    c = zc * sigmoid(zc)
    b_wide = halves(b, 1)
    c_wide = halves(c, 1)
    b_rows = halves(jnp.transpose(b[early]), 0)
    c_rows = halves(jnp.transpose(c[late]), 0)
    row = lax.broadcasted_iota(jnp.int32, (half, half), 0)
    col = lax.broadcasted_iota(jnp.int32, (half, half), 1)
    lane = lax.broadcasted_iota(jnp.int32, (length, LANES), 1)

    def pieces(wide, at):
        return wide[at, 0:LANES], wide[at, LANES:]

    for chunk, at in enumerate(chunks):
        full = dot3(pieces(c_wide, at), pieces(b_wide, at), NT)
        scores[chunk] = jnp.where(row >= col, full, 0.0)
    grad_scores[...] = jnp.zeros_like(grad_scores)
    db_ref[...] = jnp.zeros_like(db_ref)
    dc_ref[...] = jnp.zeros_like(dc_ref)

    def one_tile(tile, carry):
        here = pl.ds(pl.multiple_of(tile * LANES, LANES), LANES)
        turn = (LANES - 2 * tile) % LANES
        dt_cols = pltpu.roll(dt_ref[...], turn, 1)
        cum_cols = pltpu.roll(cum_ref[...], turn, 1)
        dt = jnp.where(lane < P_SIZE, dt_cols[:, 0:1], dt_cols[:, 1:2])
        cum = jnp.where(lane < P_SIZE, cum_cols[:, 0:1], cum_cols[:, 1:2])
        z = z_ref[:, here]
        x = z * sigmoid(z) * dt
        g = cot_ref[:, here]
        xh, xl = split(x)
        gt = jnp.transpose(g.astype(F32)).astype(BF16)
        for chunk, at in enumerate(chunks):
            ys = []
            us = []
            for head in range(2):
                of = slice(head * P_SIZE, (head + 1) * P_SIZE)
                row_logs = cumt_ref[pl.ds(2 * tile + head, 1), at]
                decays = jnp.exp(jnp.minimum(cum_cols[at, head : head + 1] - row_logs, 0.0))
                wh, wl = split(scores[chunk] * decays)
                x_pair = jnp.concatenate([xh[at, of], xl[at, of]], 1)
                y_pair = dot1(wh, x_pair, NN) + dot1(wl, x_pair, NN)
                ys.append(y_pair[:, 0:P_SIZE] + y_pair[:, P_SIZE:])
                us.append(dot1(gt[of, at], wh, NN) + dot1(gt[of, at], wl, NN))
                g_pair = jnp.concatenate([g[at, of], g[at, of]], 1)
                grad_scores[chunk] += dot1(g_pair, x_pair, NT) * decays
            y_ref[at, here] = jnp.concatenate(ys, 1)
            u_ref[at, here] = jnp.transpose(jnp.concatenate(us, 0))
        middle = cum[half - 1 : half, :]
        down = jnp.exp(middle - cum[early])
        up = jnp.exp(cum[late] - middle)
        xd = halves(x[early] * down, 1)
        gd = halves(g[late].astype(F32) * up, 1)
        state = tall_dot(b_rows, xd)
        grad = tall_dot(c_rows, gd)
        y_ref[late, here] += up * full_dot(c_wide[late], square(state))
        u_ref[early, here] += down * full_dot(b_wide[early], square(grad))
        dc_ref[late, :] += full_dot(gd, square(jnp.transpose(state)))
        db_ref[early, :] += full_dot(xd, square(jnp.transpose(grad)))
        return carry

    lax.fori_loop(0, tiles, one_tile, 0)
    for chunk, at in enumerate(chunks):
        gs = split(jnp.where(row >= col, grad_scores[chunk], 0.0))
        dc_ref[at, :] += dot3(gs, pieces(b_wide, at), NN)
        db_ref[at, :] += dot3(gs, pieces(c_wide, at), TN)


def join_kernel(
    tiles,
    z_ref, sp_ref, dt_ref, cum_ref, par_ref, cot_ref, y_ref, u_ref,
    db_ref, dc_ref, keep_ref, send_ref, arrived_ref, other_ref,
    mixed_ref, dinner_ref, dshared_ref, gstep_ref, rim_ref,
    z_in, cot_in, y_in, u_in, state_in, z_sem, cot_sem, y_sem, u_sem, state_sem,
):
    length = z_ref.shape[0]
    inner = tiles * LANES
    states = [
        pltpu.make_async_copy(ref.at[:, 0 : 8 * tiles], state_in.at[i], state_sem.at[i])
        for i, ref in enumerate((arrived_ref, keep_ref, send_ref, other_ref))
    ]
    sides = pltpu.make_async_copy(
        z_ref.at[:, inner:], z_in.at[:, inner:], z_sem.at[tiles]
    )
    loads = []
    for k in range(tiles):
        at = slice(k * LANES, (k + 1) * LANES)
        loads.append([
            pltpu.make_async_copy(ref.at[:, at], held.at[:, at], sem.at[k])
            for ref, held, sem in (
                (z_ref, z_in, z_sem), (cot_ref, cot_in, cot_sem),
                (y_ref, y_in, y_sem), (u_ref, u_in, u_sem),
            )
        ])
    for copy in [sides, *states, *loads[0], *loads[1]]:
        copy.start()
    forward = places()[2] == 0
    dt = dt_ref[...]
    cum = cum_ref[...]
    last = cum[length - 1 :, :]
    read_weight = jnp.exp(cum)
    tail_weight = jnp.exp(last - cum)
    total_decay = jnp.exp(last)
    sides.wait()
    zb = z_in[:, inner : inner + LANES]
    zc = z_in[:, inner + LANES :]
    b_wide = halves(zb * sigmoid(zb), 1)
    c_wide = halves(zc * sigmoid(zc), 1)
    reads = jnp.zeros((length, LANES), F32)
    writes = jnp.zeros((length, LANES), F32)
    ends = jnp.zeros((8, LANES), F32)
    db = db_ref[...]
    dc = dc_ref[...]
    lane = lax.broadcasted_iota(jnp.int32, (LANES, LANES), 1)
    row = lax.broadcasted_iota(jnp.int32, (LANES, LANES), 0)
    for copy in states:
        copy.wait()
    for k in range(tiles):
        for copy in loads[k]:
            copy.wait()
        for copy in loads[k + 2] if k + 2 < tiles else []:
            copy.start()
        at = slice(k * LANES, (k + 1) * LANES)
        rows = slice(8 * k, 8 * k + 8)
        gather = jnp.where(lane == 2 * k + row // P_SIZE, 1.0, 0.0).astype(BF16)
        gather = jnp.concatenate([gather, gather], 0)
        arrived = state_in[0, :, rows, :].reshape(N, LANES)
        other = state_in[3, :, rows, :].reshape(N, LANES)
        keep = state_in[1, :, rows, :].reshape(N, LANES)
        send = state_in[2, :, rows, :].reshape(N, LANES)
        state = jnp.where(forward, arrived, other)
        grad = jnp.where(forward, other, arrived)
        own = jnp.where(forward, keep, send)
        z = z_in[:, at]
        s = sigmoid(z)
        v = z * s
        g = cot_in[:, at].astype(F32)
        read_k = of_tile(read_weight, k)
        tail_k = of_tile(tail_weight, k)
        dt_k = of_tile(dt, k)
        skip = of_tile(par_ref[...], k)[2:3, :]
        y = y_in[:, at] + read_k * full_dot(c_wide, square(state))
        u = u_in[:, at] + tail_k * full_dot(b_wide, square(grad))
        mixed_ref[:, at] = (y + skip * v).astype(BF16)
        dv = dt_k * u + skip * g
        dinner_ref[:, at] = dv * (s * (1.0 + z * (1.0 - s)))
        reads += dot1(halves(g * y, 1), gather, NN)
        writes += dot1(halves(v * u, 1), gather, NN)
        dc += full_dot(halves(g * read_k, 1), square(jnp.transpose(state)))
        db += full_dot(halves(v * dt_k * tail_k, 1), square(jnp.transpose(grad)))
        end = jnp.sum(grad * (own + of_tile(total_decay, k) * state), 0, keepdims=True)
        ends += dot1(halves(jnp.broadcast_to(end, (8, LANES)), 1), gather, NN)
    sb = sigmoid(zb)
    sc = sigmoid(zc)
    dshared_ref[:, 0:LANES] = db * (sb * (1.0 + zb * (1.0 - sb)))
    dshared_ref[:, LANES:] = dc * (sc * (1.0 + zc * (1.0 - sc)))
    rim_ref[:, 0:inner] = dinner_ref[0:8, :]
    rim_ref[:, inner:] = dshared_ref[0:8, :]
    grad_logs = triangle_sum(reads - dt * writes, TN) + ends[0:1]
    grad_dt = writes - par_ref[1:2, :] * grad_logs
    gstep_ref[...] = grad_dt * sigmoid(sp_ref[...])


def conv_back_kernel(
    dinner_ref, dshared_ref, rim_ref, ci_ref, cs_ref, gstep_ref,
    gi_ref, gst_ref, right_ref, wide_i, wide_s, gi, gst, right, gi_sem, gst_sem, right_sem,
):
    length, inner = dinner_ref.shape
    shared = dshared_ref.shape[1]
    rim = rim_ref[...] * jnp.where(lax.axis_index("ctx") < lax.axis_size("ctx") - 1, 1.0, 0.0)
    wide_s[0:length, :] = dshared_ref[...]
    wide_s[length:, :] = rim[:, inner:]

    def back(wide, taps, k):
        at = slice(k * LANES, (k + 1) * LANES)
        out = taps[K - 1 : K, at] * wide[0:length, at]
        for j in range(1, K):
            out += taps[K - 1 - j : K - j, at] * wide[j : j + length, at]
        return out

    for k in range(shared // LANES):
        at = slice(k * LANES, (k + 1) * LANES)
        grad = jnp.transpose(back(wide_s, cs_ref, k))
        gst[at, :] = grad
        high, low = split(grad)
        right[inner + k * LANES : inner + (k + 1) * LANES, :] = high
        right[inner + shared + k * LANES : inner + shared + (k + 1) * LANES, :] = low
    gst_copy = pltpu.make_async_copy(gst, gst_ref, gst_sem)
    gst_copy.start()
    high, low = split(jnp.transpose(gstep_ref[...])[0:SLOT, :])
    right[inner + 2 * shared : inner + 2 * shared + SLOT, :] = high
    right[inner + 2 * shared + SLOT :, :] = low
    wide_i[0:length, :] = dinner_ref[...]
    wide_i[length:, :] = rim[:, 0:inner]
    for k in range(inner // LANES):
        at = slice(k * LANES, (k + 1) * LANES)
        grad = back(wide_i, ci_ref, k)
        gi[:, at] = grad.astype(BF16)
        right[at, :] = jnp.transpose(grad).astype(BF16)
    gi_copy = pltpu.make_async_copy(gi, gi_ref, gi_sem)
    gi_copy.start()
    right_copy = pltpu.make_async_copy(right, right_ref, right_sem)
    right_copy.start()
    gst_copy.wait()
    gi_copy.wait()
    right_copy.wait()


def prepare_kernel(
    heads, tok_ref, wi_ref, ws_ref, wt_ref, after_ref, tok_t_ref, left_ref, mark_ref
):
    inner = wi_ref.shape[1]
    shared = ws_ref.shape[1]
    end = inner + 2 * shared
    mark_ref[...] = jnp.zeros_like(mark_ref)

    def turn(step, carry):
        at = pl.ds(pl.multiple_of(step * BLOCK, BLOCK), BLOCK)
        tok_t_ref[at, :] = jnp.transpose(tok_ref[:, at].astype(F32)).astype(BF16)
        return carry

    lax.fori_loop(0, tok_ref.shape[1] // BLOCK, turn, 0)
    left_ref[:, 0:inner] = wi_ref[...]
    left_ref[:, inner : inner + shared] = ws_ref[...]
    left_ref[:, inner + shared : end] = ws_ref[...]
    blank = jnp.zeros((SLOT - heads, left_ref.shape[0]), F32)
    step = jnp.concatenate([wt_ref[...].astype(F32), blank], 0)
    left_ref[:, end:] = jnp.transpose(jnp.concatenate([step, step], 0)).astype(BF16)


def token_grad_kernel(
    left_ref, right_ref,
    up_ref, down_ref, hold_ref, own_ref, mine_ref, other_ref, mark_ref,
    left, right, up, down, hold, own, mine, other,
    left_sem, right_sem, ring_sem, mine_sem, other_sem,
):
    mark_ref[...] = jnp.zeros_like(mark_ref)
    place = lax.axis_index("tp")
    x, z = place // 2, place % 2
    rows = up_ref.shape[1]
    slab = left.shape[1]
    right_copy = pltpu.make_async_copy(right_ref, right, right_sem)
    right_copy.start()
    order = (2, 1, 3, 0)
    loads = [
        pltpu.make_async_copy(
            left_ref.at[pl.ds(pl.multiple_of((x + step) % RING * slab, slab), slab)],
            left.at[step],
            left_sem.at[step],
        )
        for step in range(RING)
    ]
    for step in order[0:2]:
        loads[step].start()
    right_copy.wait()
    rings = [
        pltpu.make_async_copy(held, ref, ring_sem.at[i])
        for i, (held, ref) in enumerate(
            ((up, up_ref), (down, down_ref), (hold, hold_ref), (own, own_ref))
        )
    ]
    stores = []
    for turn, step in enumerate(order):
        loads[step].wait()
        if turn + 2 < RING:
            loads[order[turn + 2]].start()
        product = dot1(left[step], right[...], NN).reshape(2, 2 * rows, right.shape[1])
        first, second = product[0, 0:rows], product[1, 0:rows]
        if step == 2:
            up[0] = first
            down[0] = second
        elif step == 1:
            hold[0] = first
            up[1] = second
            stores.append(rings[0])
        elif step == 3:
            down[1] = first
            hold[1] = second
            stores += rings[1:3]
        else:
            own[0] = first
            own[1] = second
            stores.append(rings[3])
        mine[step] = jnp.where(z == 0, product[0, rows:], product[1, rows:])
        other[step] = jnp.where(z == 0, product[1, rows:], product[0, rows:])
        sides = [
            pltpu.make_async_copy(mine.at[step], mine_ref.at[step], mine_sem.at[step]),
            pltpu.make_async_copy(other.at[step], other_ref.at[step], other_sem.at[step]),
        ]
        stores += sides
        for copy in sides:
            copy.start()
        if step == 1:
            rings[0].start()
        elif step == 3:
            rings[1].start()
            rings[2].start()
        elif step == 0:
            rings[3].start()
    for copy in stores:
        copy.wait()


def token_split_kernel(
    own_ref, from_below_ref, from_above_ref, last_below_ref, last_above_ref, after_ref,
    keep_ref, send_ref,
):
    near = lax.axis_index("tp") % 2 == 0
    first, second = ring_sum(
        own_ref, from_below_ref, from_above_ref, last_below_ref, last_above_ref
    )
    keep_ref[...] = jnp.where(near, first, second)
    send_ref[...] = jnp.where(near, second, first)


def token_ring_kernel(mine_ref, got_ref, after_ref, up_ref, down_ref, hold_ref, own_ref):
    half = up_ref.shape[1]

    def part(target, which):
        at = slice(which * half, (which + 1) * half)
        return mine_ref[target, at, :] + got_ref[target, at, :]

    ring_parts(0, part, up_ref, down_ref, hold_ref, own_ref)


def token_sum_kernel(
    keep_ref, got_ref,
    own_ref, from_below_ref, from_above_ref, last_below_ref, last_above_ref, after_ref,
    out_ref, mark_ref,
):
    mark_ref[...] = jnp.zeros_like(mark_ref)
    rows = keep_ref.shape[0]
    half = rows // 2
    first, second = ring_sum(
        own_ref, from_below_ref, from_above_ref, last_below_ref, last_above_ref
    )
    out_ref[0:rows, :] = (keep_ref[...] + got_ref[...]).astype(out_ref.dtype)
    out_ref[rows : rows + half, :] = first.astype(out_ref.dtype)
    out_ref[rows + half :, :] = second.astype(out_ref.dtype)


def put_rows(y, product, mine_ref, other_ref):
    rows = mine_ref.shape[1] * mine_ref.shape[2] // RING
    parts = product.reshape(RING, CORES, rows, product.shape[1])

    def put(first, second):
        for z in range(RING):
            at = z * rows % mine_ref.shape[2]
            first[y, z * rows // mine_ref.shape[2], at : at + rows, :] = parts[z, 0]
            second[y, z * rows // mine_ref.shape[2], at : at + rows, :] = parts[z, 1]

    @pl.when(places()[2] == 0)
    def _():
        put(mine_ref, other_ref)

    @pl.when(places()[2] == 1)
    def _():
        put(other_ref, mine_ref)


def weight_grad_kernel(tok_ref, gi_ref, after_ref, later_ref, mine_ref, other_ref):
    slab = tok_ref.shape[0] // RING
    right = gi_ref[...]

    def turn(y, carry):
        at = pl.ds(pl.multiple_of(y * slab, slab), slab)
        put_rows(y, dot1(tok_ref[at, :], right, NN), mine_ref, other_ref)
        return carry

    lax.fori_loop(0, RING, turn, 0)


def side_grad_kernel(parts_ref, gstep_ref, tok_ref, mine_ref, other_ref):
    slab = tok_ref.shape[0] // RING
    shared_cols = parts_ref.shape[1]
    total = parts_ref[0]
    for i in range(1, parts_ref.shape[0]):
        total += parts_ref[i]
    blank = jnp.zeros((LANES - shared_cols, total.shape[1]), F32)
    cols = jnp.transpose(jnp.concatenate([total, blank], 0))
    right = halves(cols + pltpu.roll(gstep_ref[...], shared_cols, 1), 1)

    def turn(y, carry):
        at = pl.ds(pl.multiple_of(y * slab, slab), slab)
        both = dot1(tok_ref[at, :], right, NN)
        put_rows(y, both[:, 0:LANES] + both[:, LANES:], mine_ref, other_ref)
        return carry

    lax.fori_loop(0, RING, turn, 0)


def ring_parts(place, part, up_ref, down_ref, hold_ref, own_ref):
    above, facing, below = [(place + i) % RING for i in (1, 2, 3)]
    up_ref[0] = part(facing, 0)
    up_ref[1] = part(above, 1)
    down_ref[0] = part(facing, 1)
    down_ref[1] = part(below, 0)
    hold_ref[0] = part(above, 0)
    hold_ref[1] = part(below, 1)
    own_ref[0] = part(place, 0)
    own_ref[1] = part(place, 1)


def core_sum_kernel(lanes, *refs):
    blocks = refs[:-5]

    def part(target, half):
        sums = [
            blocks[i][target, half, :, at] + blocks[i + 1][target, half, :, at]
            for i, at in zip(range(0, len(blocks), 2), lanes)
        ]
        return jnp.concatenate(sums, 1) if len(sums) > 1 else sums[0]

    ring_parts(places()[0], part, *refs[-4:])


def pass_on_kernel(hold_ref, from_below_ref, from_above_ref, after_ref, up_ref, down_ref):
    up_ref[...] = hold_ref[0] + from_below_ref[0]
    down_ref[...] = hold_ref[1] + from_above_ref[0]


def ring_sum(own_ref, from_below_ref, from_above_ref, last_below_ref, last_above_ref):
    first = own_ref[0] + from_above_ref[1] + last_below_ref[...]
    second = own_ref[1] + from_below_ref[1] + last_above_ref[...]
    return first, second


def next_ring_kernel(*refs):
    up_ref, down_ref, hold_ref, own_ref, sums = refs[-5:]
    lanes = refs[0].shape[2]
    half = RING // 2
    for i in range(2):
        at = slice(i * lanes, (i + 1) * lanes)
        first, second = ring_sum(*refs[5 * i : 5 * i + 5])
        shape = (half, 2, sums.shape[2], lanes)
        sums[0:half, :, :, at] = first.reshape(shape)
        sums[half:, :, :, at] = second.reshape(shape)

    def part(target, which):
        return sums[target, which]

    ring_parts(places()[1], part, up_ref, down_ref, hold_ref, own_ref)


def last_ring_kernel(*refs):
    inner_ref, shared_ref, step_ref, side = refs[6:]
    half = inner_ref.shape[0] // 2
    inner = inner_ref.shape[1]
    shared_cols = shared_ref.shape[0]
    side[2 * half :, :] = jnp.zeros((side.shape[0] - 2 * half, LANES), F32)
    for i, part in enumerate(ring_sum(*refs[0:5])):
        rows = slice(i * half, (i + 1) * half)
        inner_ref[rows, :] = part[:, 0:inner]
        side[rows, :] = part[:, inner:]
    flat = jnp.transpose(side[...])
    shared_ref[...] = flat[0:shared_cols, 0 : 2 * half]
    step_ref[...] = flat[shared_cols : shared_cols + step_ref.shape[0], 0 : 2 * half]


def whole(shape):
    return pl.BlockSpec(shape, lambda *_: (0,) * len(shape))


def after():
    return pl.BlockSpec(memory_space=pl.ANY)


def far():
    return pl.BlockSpec(memory_space=pltpu.HBM)


def body(
    tokens,
    inner_weight,
    shared_weight,
    step_weight,
    conv_inner,
    conv_shared,
    step_bias,
    decay_rate,
    skip_gain,
    cotangent,
):
    length, width = tokens.shape
    inner = inner_weight.shape[1]
    shared = shared_weight.shape[1]
    heads = step_weight.shape[1]
    tiles = inner // LANES
    ctx = lax.axis_size("ctx")
    tp = lax.axis_size("tp")
    chips = ctx // CORES
    same_core = [[CORES * chip + i for chip in range(chips)] for i in range(CORES)]
    sds = jax.ShapeDtypeStruct
    step_weight_t = step_weight.T

    rim = shifted(tokens[length - 8 :].astype(F32), "ctx", 1)

    total = inner + shared
    pay_rows = 8 * tiles + 8
    z, sp, dt, cum, cum_t, keep, send, params = pl.pallas_call(
        functools.partial(project_kernel, tiles, heads),
        in_specs=[
            far(),
            whole((8, width)),
            far(),
            far(),
            whole((heads, width)),
            whole((K, inner)),
            whole((K, shared)),
            whole((1, heads)),
            whole((1, heads)),
            whole((1, heads)),
            far(),
        ],
        out_specs=[
            whole((length, total)),
            whole((length, LANES)),
            whole((length, LANES)),
            whole((length, LANES)),
            whole((SLOT, length)),
            whole((chips, pay_rows, LANES)),
            whole((chips, pay_rows, LANES)),
            whole((8, LANES)),
        ],
        out_shape=[
            sds((length, total), F32),
            sds((length, LANES), F32),
            sds((length, LANES), F32),
            sds((length, LANES), F32),
            sds((SLOT, length), F32),
            sds((chips, pay_rows, LANES), F32),
            sds((chips, pay_rows, LANES), F32),
            sds((8, LANES), F32),
        ],
        scratch_shapes=[
            pltpu.VMEM((width // BLOCK, length + 16, BLOCK), BF16),
            pltpu.VMEM((width // BLOCK, BLOCK, total + LANES), BF16),
            pltpu.VMEM((length + 16, total + LANES), F32),
            pltpu.VMEM((length, inner), BF16),
            DMA((width // BLOCK,)),
            DMA((width // BLOCK,)),
            DMA((width // BLOCK,)),
            DMA,
        ],
        compiler_params=LARGE,
        name="project",
    )(
        tokens, rim, inner_weight, shared_weight, step_weight_t,
        conv_inner, conv_shared, step_bias[None], decay_rate[None], skip_gain[None], cotangent,
    )

    got = ctx_shift(send, 0, 0, 1)
    chip_state = pl.pallas_call(
        functools.partial(chip_kernel, tiles),
        out_shape=sds((chips, pay_rows, LANES), F32),
        compiler_params=PARAMS,
        name="chip_state",
    )(keep, got)
    by_rows = lax.all_to_all(
        chip_state, "ctx", 0, 0, axis_index_groups=same_core, tiled=True
    )

    y, u, db, dc = pl.pallas_call(
        functools.partial(local_kernel, tiles),
        out_shape=[
            sds((length, inner), F32),
            sds((length, inner), F32),
            sds((length, LANES), F32),
            sds((length, LANES), F32),
        ],
        scratch_shapes=[
            pltpu.VMEM((2, length // 2, length // 2), F32),
            pltpu.VMEM((2, length // 2, length // 2), F32),
        ],
        compiler_params=LARGE,
        cost_estimate=pl.CostEstimate(
            flops=10 * length * length * inner, bytes_accessed=8_000_000, transcendentals=0
        ),
        name="local",
    )(z, dt, cum, cum_t, cotangent)

    scanned = pl.pallas_call(
        functools.partial(ctx_scan_kernel, tiles),
        in_specs=[whole((chips, pay_rows, LANES)), after()],
        out_specs=whole((chips, 8 * tiles, LANES)),
        out_shape=sds((chips, 8 * tiles, LANES), F32),
        compiler_params=PARAMS,
        name="ctx_scan",
    )(by_rows, dc)
    arrived = lax.all_to_all(scanned, "ctx", 0, 0, axis_index_groups=same_core, tiled=True)
    right_rows = inner + 2 * shared + 2 * SLOT
    tok_t, left, mark = pl.pallas_call(
        functools.partial(prepare_kernel, heads),
        in_specs=[
            whole((length, width)),
            whole((width, inner)),
            whole((width, shared)),
            whole((heads, width)),
            after(),
        ],
        out_specs=[whole((width, length)), whole((width, right_rows)), whole((8, LANES))],
        out_shape=[
            sds((width, length), BF16),
            sds((width, right_rows), BF16),
            sds((8, LANES), F32),
        ],
        compiler_params=LARGE,
        name="prepare",
    )(tokens, inner_weight, shared_weight, step_weight_t, scanned)
    onward = pl.pallas_call(
        functools.partial(onward_kernel, tiles),
        in_specs=[
            whole((chips, pay_rows, LANES)), whole((chips, 8 * tiles, LANES)), after(),
        ],
        out_specs=whole((chips, 8 * tiles, LANES)),
        out_shape=sds((chips, 8 * tiles, LANES), F32),
        compiler_params=PARAMS,
        name="onward",
    )(keep, arrived, mark)
    other = ctx_shift(onward, 0, 0, 1)

    column = whole((length, LANES))
    mixed, dinner, dshared, gstep, rim_out = pl.pallas_call(
        functools.partial(join_kernel, tiles),
        in_specs=[
            far(),
            column,
            column,
            column,
            whole((8, LANES)),
            far(),
            far(),
            far(),
            column,
            column,
            far(),
            far(),
            far(),
            far(),
        ],
        out_specs=[
            whole((length, inner)), whole((length, inner)), whole((length, shared)), column,
            whole((8, total)),
        ],
        out_shape=[
            sds((length, inner), BF16),
            sds((length, inner), F32),
            sds((length, shared), F32),
            sds((length, LANES), F32),
            sds((8, total), F32),
        ],
        scratch_shapes=[
            pltpu.VMEM((length, total), F32),
            pltpu.VMEM((length, inner), BF16),
            pltpu.VMEM((length, inner), F32),
            pltpu.VMEM((length, inner), F32),
            pltpu.VMEM((4, chips, 8 * tiles, LANES), F32),
            DMA((tiles + 1,)),
            DMA((tiles,)),
            DMA((tiles,)),
            DMA((tiles,)),
            DMA((4,)),
        ],
        compiler_params=LARGE,
        name="join",
    )(
        z, sp, dt, cum, params, cotangent, y, u, db, dc,
        keep, send, arrived, other,
    )

    rim_back = shifted(rim_out, "ctx", -1)
    grad_inner, grad_shared_t, right = pl.pallas_call(
        conv_back_kernel,
        in_specs=[
            whole((length, inner)),
            whole((length, shared)),
            whole((8, total)),
            whole((K, inner)),
            whole((K, shared)),
            column,
        ],
        out_specs=[far(), far(), far()],
        out_shape=[
            sds((length, inner), BF16),
            sds((shared, length), F32),
            sds((right_rows, length), BF16),
        ],
        scratch_shapes=[
            pltpu.VMEM((length + 8, inner), F32),
            pltpu.VMEM((length + 8, shared), F32),
            pltpu.VMEM((length, inner), BF16),
            pltpu.VMEM((shared, length), F32),
            pltpu.VMEM((right_rows, length), BF16),
            DMA,
            DMA,
            DMA,
        ],
        compiler_params=LARGE,
        name="conv_back",
    )(dinner, dshared, rim_back, conv_inner, conv_shared, gstep)

    shared_cols = shared // tp
    shared_parts = lax.all_to_all(
        grad_shared_t.reshape(tp, shared_cols, length), "tp", 0, 0, tiled=True
    )

    cols = width // tp
    t_half = cols // 2
    t_quarter = cols // 4
    message = sds((2, t_half, length), F32)
    side_block = sds((RING, t_half, length), F32)
    t_up, t_down, t_hold, t_own, t_mine, t_other, token_mark = pl.pallas_call(
        token_grad_kernel,
        in_specs=[far(), far()],
        out_specs=[far()] * 6 + [whole((8, LANES))],
        out_shape=[message] * 4 + [side_block] * 2 + [sds((8, LANES), F32)],
        scratch_shapes=[
            pltpu.VMEM((RING, 2 * cols, right_rows), BF16),
            pltpu.VMEM((right_rows, length), BF16),
        ]
        + [pltpu.VMEM(message.shape, F32)] * 4
        + [pltpu.VMEM(side_block.shape, F32)] * 2
        + [DMA((RING,)), DMA, DMA((RING,)), DMA((RING,)), DMA((RING,))],
        compiler_params=LARGE,
        cost_estimate=CHEAP,
        name="token_grad",
    )(left, right)

    def exchange_tp(up, down):
        return tp_shift(up, 1, 0), tp_shift(down, -1, 0)

    t_first = exchange_tp(t_up, t_down)
    t_got = tp_shift(t_other, 0, 1)

    rows = width // ctx
    y_half = RING * rows // 2
    z_half = rows // 2
    lanes = (inner + LANES) // 2

    def row_block(wide):
        return whole((RING, 2, y_half, wide))

    def row_shape(wide):
        return sds((RING, 2, y_half, wide), F32)

    mine, core_other = pl.pallas_call(
        weight_grad_kernel,
        in_specs=[whole((width, length)), whole((length, inner)), after(), after()],
        out_specs=[row_block(inner)] * 2,
        out_shape=[row_shape(inner)] * 2,
        compiler_params=PARAMS,
        cost_estimate=CHEAP,
        name="weight_grad",
    )(tok_t, grad_inner, token_mark, shared_parts)
    core_got = ctx_shift(core_other, 0, 0, 1)

    def core_sum(blocks, spans, ready):
        return pl.pallas_call(
            functools.partial(core_sum_kernel, spans),
            in_specs=[whole(block.shape) for block in blocks] + [after()],
            out_specs=[whole((2, y_half, lanes))] * 4,
            out_shape=[sds((2, y_half, lanes), F32)] * 4,
            compiler_params=PARAMS,
            cost_estimate=CHEAP,
            name="core_sum",
        )(*blocks, ready)

    def exchange(up, down, dy, dz):
        return ctx_shift(up, dy, dz, 0), ctx_shift(down, -dy, -dz, 0)

    def pass_on(hold, below, above, ready):
        half, wide = hold.shape[1:]
        return pl.pallas_call(
            pass_on_kernel,
            in_specs=[whole(hold.shape)] * 3 + [after()],
            out_specs=[whole((half, wide))] * 2,
            out_shape=[sds((half, wide), F32)] * 2,
            compiler_params=PARAMS,
            cost_estimate=CHEAP,
            name="pass_on",
        )(hold, below, above, ready)

    def next_ring(parts_a, parts_b, ready):
        wide = 2 * lanes
        return pl.pallas_call(
            next_ring_kernel,
            in_specs=([whole((2, y_half, lanes))] * 3 + [whole((y_half, lanes))] * 2) * 2
            + [after()],
            out_specs=[whole((2, z_half, wide))] * 4,
            out_shape=[sds((2, z_half, wide), F32)] * 4,
            scratch_shapes=[pltpu.VMEM((RING, 2, z_half, wide), F32)],
            compiler_params=PARAMS,
            cost_estimate=CHEAP,
            name="next_ring",
        )(*parts_a, *parts_b, ready)

    side_mine, side_other = pl.pallas_call(
        side_grad_kernel,
        in_specs=[
            whole((tp, shared_cols, length)),
            column,
            whole((width, length)),
        ],
        out_specs=[row_block(LANES)] * 2,
        out_shape=[row_shape(LANES)] * 2,
        compiler_params=PARAMS,
        cost_estimate=CHEAP,
        name="side_grad",
    )(shared_parts, gstep, tok_t)
    side_got = ctx_shift(side_other, 0, 0, 1)
    up_a, down_a, hold_a, own_a = core_sum((mine, core_got), [slice(0, lanes)], side_mine)
    first_a = exchange(up_a, down_a, 1, 0)
    side_got = ctx_shift(side_other, 0, 0, 1)
    up_b, down_b, hold_b, own_b = core_sum(
        (mine, core_got, side_mine, side_got), [slice(lanes, inner), slice(0, LANES)], hold_a
    )
    first_b = exchange(up_b, down_b, 1, 0)
    up_a, down_a = pass_on(hold_a, *first_a, hold_b)
    second_a = exchange(up_a, down_a, 1, 0)
    t_up, t_down = pass_on(t_hold, *t_first, up_a)
    t_second = exchange_tp(t_up, t_down)
    t_keep, t_send = pl.pallas_call(
        token_split_kernel,
        in_specs=[whole(message.shape)] * 3 + [whole(message.shape[1:])] * 2 + [after()],
        out_specs=[whole(message.shape[1:])] * 2,
        out_shape=[sds(message.shape[1:], F32)] * 2,
        compiler_params=PARAMS,
        cost_estimate=CHEAP,
        name="token_split",
    )(t_own, *t_first, *t_second, t_up)
    t_last = tp_shift(t_send, 0, 1)
    up_b, down_b = pass_on(hold_b, *first_b, t_keep)
    second_b = exchange(up_b, down_b, 1, 0)
    quarter = sds((2, t_quarter, length), F32)
    q_up, q_down, q_hold, q_own = pl.pallas_call(
        token_ring_kernel,
        in_specs=[whole(side_block.shape)] * 2 + [after()],
        out_specs=[whole(quarter.shape)] * 4,
        out_shape=[quarter] * 4,
        compiler_params=PARAMS,
        cost_estimate=CHEAP,
        name="token_ring",
    )(t_mine, t_got, up_b)
    q_first = exchange_tp(q_up, q_down)
    up, down, hold, own = next_ring(
        (own_a, *first_a, *second_a), (own_b, *first_b, *second_b), q_hold
    )
    first = exchange(up, down, 0, 1)
    q_up, q_down = pass_on(q_hold, *q_first, hold)
    q_second = exchange_tp(q_up, q_down)
    up, down = pass_on(hold, *first, q_up)
    second = exchange(up, down, 0, 1)
    grad_tokens, last_mark = pl.pallas_call(
        token_sum_kernel,
        in_specs=[whole(t_keep.shape)] * 2
        + [whole(quarter.shape)] * 3
        + [whole(quarter.shape[1:])] * 2
        + [after()],
        out_specs=[whole((cols, length)), whole((8, LANES))],
        out_shape=[sds((cols, length), BF16), sds((8, LANES), F32)],
        compiler_params=PARAMS,
        cost_estimate=CHEAP,
        name="token_sum",
    )(t_keep, t_last, q_own, *q_first, *q_second, up)
    grad_inner_weight, grad_shared_weight, grad_step_weight = pl.pallas_call(
        last_ring_kernel,
        out_shape=[
            sds((rows, inner), F32),
            sds((shared_cols, rows), F32),
            sds((heads, rows), F32),
        ],
        scratch_shapes=[pltpu.VMEM((LANES, LANES), F32)],
        compiler_params=PARAMS,
        cost_estimate=CHEAP,
        name="last_ring",
    )(own, *first, *second, last_mark)

    return (
        mixed,
        grad_tokens.T,
        grad_inner_weight,
        grad_shared_weight.T,
        grad_step_weight.T,
    )


def solution(mesh):
    in_specs = (
        P("ctx", None),
        P(None, "tp"),
        P(),
        P(None, "tp"),
        P(None, "tp"),
        P(),
        P("tp"),
        P("tp"),
        P("tp"),
        P("ctx", "tp"),
    )
    out_specs = (P("ctx", "tp"), P("ctx", "tp"), P("ctx", "tp"), P("ctx", "tp"), P("ctx", "tp"))
    return jax.shard_map(body, mesh=mesh, in_specs=in_specs, out_specs=out_specs, check_vma=False)
```
